32 devices in a mesh: dp: 2 (over core), seq: 4 (over y, x), fsdp: 4 (over z).
Axes of the slice: x: 2, y: 2, z: 4, core: 2. Of those that a mesh axis runs over, the one named last changes fastest.
Arguments:
- image_tokens: bfloat16 [4, 16, 196, 768], P('dp', 'fsdp', 'seq'), may hold values from -6 to 6
- slot_window: int32 [16], P('fsdp'), may hold values from 0 to 15, as said below
- first_gain: float32 [768], replicated, may hold values from 0.5 to 1.5
- first_bias: float32 [768], replicated, may hold values from -1.2 to 1.2
- qkv_weight: bfloat16 [768, 2304], P('fsdp'), may hold values from -0.21875 to 0.21875
- qkv_bias: float32 [2304], replicated, may hold values from -1.2 to 1.2
- rel_height: bfloat16 [27, 64], replicated, may hold values from -0.75 to 0.75
- rel_width: bfloat16 [27, 64], replicated, may hold values from -0.75 to 0.75
- proj_weight: bfloat16 [768, 768], P('fsdp'), may hold values from -0.875 to 0.875
- proj_bias: float32 [768], replicated, may hold values from -1.2 to 1.2
- second_gain: float32 [768], replicated, may hold values from 0.5 to 1.5
- second_bias: float32 [768], replicated, may hold values from -1.2 to 1.2
- hidden_weight: bfloat16 [768, 3072], P('fsdp'), may hold values from -0.21875 to 0.21875
- hidden_bias: float32 [3072], replicated, may hold values from -1.2 to 1.2
- output_weight: bfloat16 [3072, 768], P('fsdp'), may hold values from -0.109375 to 0.109375
- output_bias: float32 [768], replicated, may hold values from -1.2 to 1.2
- cotangent: bfloat16 [4, 16, 196, 768], P('dp', 'fsdp', 'seq'), may hold values from -6 to 6
Outputs:
- block_out: bfloat16 [4, 16, 196, 768], P('dp', 'fsdp', 'seq')
- input_grad: bfloat16 [4, 16, 196, 768], P('dp', 'fsdp', 'seq')
- first_gain_grad: float32 [768], replicated
- first_bias_grad: float32 [768], replicated
- qkv_weight_grad: float32 [768, 2304], P(('dp', 'seq', 'fsdp'))
- qkv_bias_grad: float32 [2304], replicated
- rel_height_grad: float32 [27, 64], replicated
- rel_width_grad: float32 [27, 64], replicated
- proj_weight_grad: float32 [768, 768], P(('dp', 'seq', 'fsdp'))
- proj_bias_grad: float32 [768], replicated
- second_gain_grad: float32 [768], replicated
- second_bias_grad: float32 [768], replicated
- hidden_weight_grad: float32 [768, 3072], P(('dp', 'seq', 'fsdp'))
- hidden_bias_grad: float32 [3072], replicated
- output_weight_grad: float32 [3072, 768], P(None, ('dp', 'seq', 'fsdp'))
- output_bias_grad: float32 [768], replicated
The draws below stay inside these ranges and needn't reach their ends.
Inputs may be any that keep to these rules, and one draw needn't show every extreme that they name: `slot_window`: each window number 0 to 15 stands in exactly one slot; any other slots hold -1.
All inputs are finite; a program needn't handle non-finite values.
Results may differ from the reference program's by a relative error of at most 0.012.
Values may be sent and summed in bfloat16 or wider, within the bound.
No kernel may reach another device: no remote copies, remote signals or barrier semaphores. Data moves between devices by JAX's collectives and lax.ppermute only.
A program may use at most 256 MiB of HBM per device.

```python
import jax
import jax.numpy as jnp
from jax import lax

D = 768
HEADS = 12
HD = 64
FF = 3072
WIN = 14
GRID = 48
NWS = 4
WT = 196
RELN = 27
CAP = 4
SLOTS = 16
IMAGES = 4
N_FSDP = 4


def draw_slot_window(key, part):
    key = jax.random.fold_in(key, 7)
    order = jax.random.permutation(key, CAP * N_FSDP).astype(jnp.int32)
    return jnp.where(order < NWS * NWS, order, -1).astype(jnp.int32)


def raised(drawn, rng, source, target, shards_of, factor):
    owner, partner = [(jnp.arange(drawn.shape[axis_at]) // (drawn.shape[axis_at] // shards_of)).reshape([-1 if axis == axis_at else 1 for axis in range(drawn.ndim)]) for axis_at in (source, target)]
    chosen = jax.random.permutation(rng, shards_of)[partner]
    strong = (owner == chosen) | (owner == (partner + shards_of // 2) % shards_of)
    return jnp.where(strong, factor * drawn, drawn)


def block_levels(own_key, dims, pieces, least, high):
    level = 1.0
    for axis_at, blocks in pieces:
        heights = jax.random.uniform(jax.random.fold_in(jax.random.fold_in(own_key, 6), axis_at), (blocks,), jnp.float32, least / len(pieces), high / len(pieces))
        level = level * jnp.repeat(jnp.exp(heights), dims[axis_at] // blocks).reshape((-1,) + (1,) * (len(dims) - 1 - axis_at))
    return level


def scatter_about(own_key, dims, scale, most, shards=(), kind=jnp.bfloat16):
    values = scale * jax.random.normal(own_key, dims, jnp.float32)
    if shards:
        values = values * block_levels(own_key, dims, shards, -0.22, 0.18)
    return jnp.clip(values, -most, most).astype(kind)


def bell_draw_with(rng, extent, width, reach, pieces, heavy, dtype=jnp.bfloat16):
    values = width * jax.random.normal(rng, extent, jnp.float32)
    if pieces:
        values = values * block_levels(rng, extent, pieces, -0.22, 0.18)
    return jnp.clip(raised(values, jax.random.fold_in(rng, 3), *heavy), -reach, reach).astype(dtype)


def setup_inputs(seed: int = 0) -> dict:
    key_list = jax.random.split(jax.random.key(seed), 18)
    image_tokens = scatter_about(key_list[0], (IMAGES, SLOTS, WT, D), 1.0, 6.0, ((0, 2), (1, 4), (2, 4)))
    slot_window = draw_slot_window(jax.random.fold_in(key_list[17], 71), 0)
    first_gain = jnp.clip(1.0 + 0.1 * jax.random.normal(key_list[2], (D,), jnp.float32), 0.5, 1.5)
    first_bias = scatter_about(key_list[3], (D,), 0.3, 1.2, (), jnp.float32)
    qkv_weight = scatter_about(key_list[4], (D, 3 * D), D ** -0.5, 0.21875, ((0, 4),))
    qkv_bias = scatter_about(key_list[5], (3 * D,), 0.3, 1.2, (), jnp.float32)
    rel_height = scatter_about(key_list[6], (RELN, HD), HD ** -0.5, 0.75)
    rel_width = scatter_about(key_list[7], (RELN, HD), HD ** -0.5, 0.75)
    proj_weight = scatter_about(key_list[8], (D, D), (D // WIN) ** -0.5, 0.875, ((0, 4),))
    proj_bias = scatter_about(key_list[9], (D,), 0.3, 1.2, (), jnp.float32)
    second_gain = jnp.clip(1.0 + 0.1 * jax.random.normal(key_list[10], (D,), jnp.float32), 0.5, 1.5)
    second_bias = scatter_about(key_list[11], (D,), 0.3, 1.2, (), jnp.float32)
    hidden_weight = scatter_about(key_list[12], (D, FF), D ** -0.5, 0.21875, ((0, 4),))
    hidden_bias = scatter_about(key_list[13], (FF,), 0.3, 1.2, (), jnp.float32)
    output_weight = scatter_about(key_list[14], (FF, D), FF ** -0.5, 0.109375, ((0, 4),))
    output_bias = scatter_about(key_list[15], (D,), 0.3, 1.2, (), jnp.float32)
    cotangent = bell_draw_with(key_list[16], (IMAGES, SLOTS, WT, D), 1.0, 6.0, ((0, 2), (1, 4), (2, 4)), (0, 3, 2, 2.0))
    return {"image_tokens": image_tokens, "slot_window": slot_window, "first_gain": first_gain, "first_bias": first_bias, "qkv_weight": qkv_weight, "qkv_bias": qkv_bias, "rel_height": rel_height, "rel_width": rel_width, "proj_weight": proj_weight, "proj_bias": proj_bias, "second_gain": second_gain, "second_bias": second_bias, "hidden_weight": hidden_weight, "hidden_bias": hidden_bias, "output_weight": output_weight, "output_bias": output_bias, "cotangent": cotangent}


@jax.custom_vjp
def low(v):
    return lax.optimization_barrier(v.astype(jnp.bfloat16)).astype(jnp.float32)

@jax.custom_vjp
def low_back(v):
    return v

def low_keep(v):
    return (low(v), None)

def low_pass(kept, grad):
    return (grad,)

def back_keep(v):
    return (v, None)

def back_low(kept, grad):
    return (low(grad),)
low.defvjp(low_keep, low_pass)
low_back.defvjp(back_keep, back_low)

def exact_dot(left, right):
    return jnp.dot(left, right, preferred_element_type=jnp.float32, precision=lax.Precision.HIGHEST)

def exact_einsum(form, left, right):
    return jnp.einsum(form, left, right, preferred_element_type=jnp.float32, precision=lax.Precision.HIGHEST)

def layer_norm(values, gain, shift):
    centre = values - lax.optimization_barrier(jnp.mean(values, axis=-1, keepdims=True))
    spread = lax.optimization_barrier(jnp.mean(centre * centre, axis=-1, keepdims=True))
    return centre * lax.rsqrt(spread + 1e-06) * gain + shift

def offset_table():
    offsets = jnp.arange(WIN)[:, None] - jnp.arange(WIN)[None, :] + WIN - 1
    return (offsets[:, :, None] == jnp.arange(2 * WIN - 1)[None, None, :]).astype(jnp.float32)

def valid_of(slot_window):
    positions = jnp.arange(WIN * WIN)
    window_ids = slot_window[:, None]
    row_ok = window_ids // NWS * WIN + positions[None, :] // WIN < GRID
    col_ok = window_ids % NWS * WIN + positions[None, :] % WIN < GRID
    return ((window_ids >= 0) & row_ok & col_ok).astype(jnp.float32)

def image_forward(params, tokens, valid_mask):
    gain_one, bias_one, w_qkv, b_qkv, height_rel, width_rel, w_proj, b_proj, gain_two, bias_two, w_hidden, b_hidden, w_output, b_output = params
    slot_count = tokens.shape[0]
    token_rows = tokens.reshape(slot_count * WT, D)
    keep_rows = valid_mask.reshape(slot_count * WT, 1)
    normed = low(layer_norm(token_rows, gain_one, bias_one) * keep_rows)
    packed = low(low_back(exact_dot(normed, w_qkv) + b_qkv)).reshape(slot_count, WT, 3, HEADS, HD)
    queries = packed[:, :, 0]
    key_part = packed[:, :, 1]
    value_part = packed[:, :, 2]
    table = offset_table()
    height_table = exact_einsum('abk,kd->abd', table, height_rel)
    width_table = exact_einsum('abk,kd->abd', table, width_rel)
    grid_query = queries.reshape(slot_count, WIN, WIN, HEADS, HD)
    height_terms = exact_einsum('nrchd,rkd->nhrck', grid_query, height_table)
    width_terms = exact_einsum('nrchd,ckd->nhrck', grid_query, width_table)
    rel_terms = (height_terms[..., :, None] + width_terms[..., None, :]).reshape(slot_count, HEADS, WT, WT)
    scores = HD ** (-0.5) * exact_einsum('nqhd,nkhd->nhqk', queries, key_part) + rel_terms
    scores = low_back(scores)
    soft_weights = low(jax.nn.softmax(scores, axis=-1))
    attended = low(low_back(exact_einsum('nhqk,nkhd->nqhd', soft_weights, value_part)))
    attended = attended.reshape(slot_count * WT, D)
    branch = low_back(exact_dot(attended, w_proj) + b_proj)
    middle = token_rows + branch
    second = low(layer_norm(middle, gain_two, bias_two))
    pre_act = low_back(exact_dot(second, w_hidden) + b_hidden)
    active = low(jax.nn.gelu(pre_act, approximate=False))
    feed_out = low_back(exact_dot(active, w_output) + b_output)
    return ((middle + feed_out) * keep_rows).reshape(tokens.shape)

def reference(image_tokens, slot_window, first_gain, first_bias, qkv_weight, qkv_bias, rel_height, rel_width, proj_weight, proj_bias, second_gain, second_bias, hidden_weight, hidden_bias, output_weight, output_bias, cotangent):
    valid_mask = valid_of(slot_window)
    params = tuple((arg.astype(jnp.float32) for arg in (first_gain, first_bias, qkv_weight, qkv_bias, rel_height, rel_width, proj_weight, proj_bias, second_gain, second_bias, hidden_weight, hidden_bias, output_weight, output_bias)))

    def one_image(totals, item):
        tokens, grad_in = item
        result, back_fn = jax.vjp(lambda weights, values: image_forward(weights, values, valid_mask), params, tokens.astype(jnp.float32))
        param_grads, token_grads = back_fn(grad_in.astype(jnp.float32))
        totals = jax.tree.map(lambda left, right: left + right, totals, param_grads)
        return (totals, (result.astype(jnp.bfloat16), token_grads.astype(jnp.bfloat16)))
    start = jax.tree.map(jnp.zeros_like, params)
    totals, (block_out, input_grad) = lax.scan(one_image, start, (image_tokens, cotangent))
    return (block_out, input_grad, totals[0], totals[1], totals[2], totals[3], totals[4], totals[5], totals[6], totals[7], totals[8], totals[9], totals[10], totals[11], totals[12], totals[13])
```

```python
import functools

import jax
import jax.numpy as jnp
from jax import lax
from jax.experimental import pallas as pl
from jax.experimental.pallas import tpu as pltpu
from jax.sharding import PartitionSpec as P

D = 768
HEADS = 12
HD = 64
FF = 3072
WIN = 14
GRID = 48
NWS = 4
TOK = 49
PAD = 56
ROWS = 4 * PAD
HALF = D // 2
PAIRS = 3
LANES = 128
TAB = 512
NEG = -1e30
BF = jnp.bfloat16
F32 = jnp.float32


def mm(left, right, dims=((1,), (0,))):
    return lax.dot_general(left, right, (dims, ((), ())), preferred_element_type=F32)


def attn_fwd_kernel(packed, table, spot, fold, keys, bias, out, probs):
    lane = lax.broadcasted_iota(jnp.int32, (ROWS, LANES), 1)
    for pair in range(PAIRS):
        q = packed[0, :, pair * LANES : (pair + 1) * LANES]
        k = packed[0, :, HALF + pair * LANES : HALF + (pair + 1) * LANES]
        v = packed[0, :, 2 * HALF + pair * LANES : 2 * HALF + (pair + 1) * LANES]
        right = jnp.concatenate([k, keys[...]], axis=1)
        parts = []
        for e in range(2):
            mine = (lane < HD) if e == 0 else (lane >= HD)
            spread = (mm(q, table[e]) * spot[...]).astype(BF)
            rel = mm(spread, fold[...]).astype(BF)
            scaled = jnp.where(mine, q.astype(F32) * (HD**-0.5), 0.0).astype(BF)
            left = jnp.concatenate([scaled, rel], axis=1)
            s = mm(left, right, ((1,), (1,))) + bias[...]
            p = jnp.exp(s - jnp.max(s, axis=1, keepdims=True))
            p = (p / jnp.sum(p, axis=1, keepdims=True)).astype(BF)
            probs[0, 2 * pair + e] = p
            parts.append(mm(p, v))
        out[0, :, pair * LANES : (pair + 1) * LANES] = jnp.where(
            lane < HD, parts[0], parts[1]
        ).astype(BF)


def attn_bwd_kernel(packed, grads, probs, table, spot, fold, keys, out, tab_grad):
    lane = lax.broadcasted_iota(jnp.int32, (ROWS, LANES), 1)
    lane_t = lax.broadcasted_iota(jnp.int32, (TAB, LANES), 1)

    @pl.when(pl.program_id(0) == 0)
    def _():
        tab_grad[...] = jnp.zeros_like(tab_grad)

    for pair in range(PAIRS):
        q = packed[0, :, pair * LANES : (pair + 1) * LANES]
        k = packed[0, :, HALF + pair * LANES : HALF + (pair + 1) * LANES]
        v = packed[0, :, 2 * HALF + pair * LANES : 2 * HALF + (pair + 1) * LANES]
        go = grads[0, :, pair * LANES : (pair + 1) * LANES]
        right = jnp.concatenate([k, keys[...]], axis=1)
        dq, dk, dv, dt = [], [], [], []
        for e in range(2):
            mine = (lane < HD) if e == 0 else (lane >= HD)
            go_e = jnp.where(mine, go.astype(F32), 0.0).astype(BF)
            p_low = probs[0, 2 * pair + e]
            p = p_low.astype(F32)
            dp = mm(go_e, v, ((1,), (1,)))
            ds = (p * (dp - jnp.sum(dp * p, axis=1, keepdims=True))).astype(BF)
            both = mm(ds, right)
            rel = both[:, LANES:].astype(BF)
            spread = (mm(rel, fold[...], ((1,), (1,))) * spot[...]).astype(BF)
            dq.append((HD**-0.5) * both[:, :LANES] + mm(spread, table[e], ((1,), (1,))))
            dk.append((HD**-0.5) * mm(ds, q, ((0,), (0,))))
            dv.append(mm(p_low, go, ((0,), (0,))))
            dt.append(mm(spread, q, ((0,), (0,))))
        tab_grad[...] += jnp.where(lane_t < HD, dt[0], dt[1])
        for at, two in ((0, dq), (HALF, dk), (2 * HALF, dv)):
            out[0, :, at + pair * LANES : at + (pair + 1) * LANES] = jnp.where(
                lane < HD, two[0], two[1]
            ).astype(BF)


def whole(shape):
    return pl.BlockSpec(shape, lambda w: (0,) * len(shape))


def per_window(shape):
    return pl.BlockSpec((1,) + shape, lambda w: (w,) + (0,) * len(shape))


PARAMS = pltpu.CompilerParams(vmem_limit_bytes=48 * 1024 * 1024)


def attn_fwd(packed, table, spot, fold, keys, bias):
    count = packed.shape[0]
    return pl.pallas_call(
        attn_fwd_kernel,
        grid=(count,),
        in_specs=[
            per_window((ROWS, 3 * HALF)),
            whole((2, LANES, TAB)),
            whole((ROWS, TAB)),
            whole((TAB, LANES)),
            whole((ROWS, LANES)),
            whole((1, ROWS)),
        ],
        out_specs=[per_window((ROWS, HALF)), per_window((2 * PAIRS, ROWS, ROWS))],
        out_shape=[
            jax.ShapeDtypeStruct((count, ROWS, HALF), BF),
            jax.ShapeDtypeStruct((count, 2 * PAIRS, ROWS, ROWS), BF),
        ],
        compiler_params=PARAMS,
        name="attn_fwd",
    )(packed, table, spot, fold, keys, bias)


def attn_bwd(packed, grads, probs, table, spot, fold, keys):
    count = packed.shape[0]
    return pl.pallas_call(
        attn_bwd_kernel,
        grid=(count,),
        in_specs=[
            per_window((ROWS, 3 * HALF)),
            per_window((ROWS, HALF)),
            per_window((2 * PAIRS, ROWS, ROWS)),
            whole((2, LANES, TAB)),
            whole((ROWS, TAB)),
            whole((TAB, LANES)),
            whole((ROWS, LANES)),
        ],
        out_specs=[per_window((ROWS, 3 * HALF)), whole((TAB, LANES))],
        out_shape=[
            jax.ShapeDtypeStruct((count, ROWS, 3 * HALF), BF),
            jax.ShapeDtypeStruct((TAB, LANES), F32),
        ],
        compiler_params=PARAMS,
        name="attn_bwd",
    )(packed, grads, probs, table, spot, fold, keys)


def place_kernel(where, shard, first, second, third, out, sems):
    z, s, a, b, d = where[0], where[1], where[2], where[3], where[4]
    copies = [pltpu.make_async_copy(shard, out.at[z], sems.at[0])]
    for i in range(3):
        zz = lax.rem(z + 3 - i, 4)
        for n, (src, q) in enumerate(
            (
                (first.at[i], s),
                (second.at[i], a),
                (third.at[i], b),
                (third.at[3 + i], d),
            )
        ):
            copies.append(pltpu.make_async_copy(src, out.at[zz, q], sems.at[1 + 4 * i + n]))
    for copy in copies:
        copy.start()
    for copy in copies:
        copy.wait()


def place(where, shard, first, second, third):
    rows, columns = first.shape[1:]
    anyspace = pl.BlockSpec(memory_space=pl.ANY)
    return pl.pallas_call(
        place_kernel,
        in_specs=[pl.BlockSpec(memory_space=pltpu.SMEM)] + [anyspace] * 4,
        out_specs=pl.BlockSpec(memory_space=pltpu.VMEM),
        out_shape=jax.ShapeDtypeStruct((4, 4, rows, columns), BF),
        scratch_shapes=[pltpu.SemaphoreType.DMA((13,))],
        name="place",
    )(where, shard.reshape(4, rows, columns), first, second, third).reshape(16 * rows, columns)


def per_device(
    n_dp,
    image_tokens,
    slot_window,
    first_gain,
    first_bias,
    qkv_weight,
    qkv_bias,
    rel_height,
    rel_width,
    proj_weight,
    proj_bias,
    second_gain,
    second_bias,
    hidden_weight,
    hidden_bias,
    output_weight,
    output_bias,
    cotangent,
):
    images = image_tokens.shape[0]
    own_rows = images * ROWS
    c = lax.axis_index("dp") % 2
    s = lax.axis_index("seq")
    z = lax.axis_index("fsdp")
    a = jnp.where(c == 0, s ^ 1, s ^ 2)
    b = jnp.where(c == 0, s ^ 2, s ^ 1)
    d = s ^ 3

    def plane_perm(step):
        out = []
        for i in range(n_dp):
            hop = (1, 2)[(i + step) % 2]
            out += [(i * 4 + j, i * 4 + (j ^ hop)) for j in range(4)]
        return out

    plane_one, plane_two = plane_perm(0), plane_perm(1)

    def to_core(v):
        return lax.ppermute(v, "dp", [(i, i ^ 1) for i in range(n_dp)])

    def to_seq(v, k):
        return lax.ppermute(v, "seq", [(i, i ^ k) for i in range(4)])

    def to_z(v, k):
        return lax.ppermute(v, "fsdp", [(i, (i + k) % 4) for i in range(4)])

    def to_plane(v, perm):
        return lax.ppermute(v, ("dp", "seq"), perm)

    def pick(v, index, axis=0):
        return lax.dynamic_index_in_dim(v, index, axis, keepdims=False)

    def gather(shard):
        rows = shard.shape[0] // 4
        own = pick(shard.reshape(4, rows, -1), s)
        first = jnp.stack([to_z(own, k) for k in (1, 2, 3)])
        second = to_plane(first, plane_one)
        third = to_plane(jnp.concatenate([first, second]), plane_two)
        where = jnp.stack([z, s, a, b, d]).astype(jnp.int32)
        return place(where, shard, first, second, third)

    def spread_tokens(v):
        own = []
        for k in range(4):
            piece = jnp.pad(pick(v, s ^ k, 1), ((0, 0), (0, PAD - TOK), (0, 0)))
            own.append(to_seq(piece, k) if k else piece)
        other = [to_core(piece) for piece in own]
        return jnp.concatenate(
            [jnp.stack(own, axis=1), jnp.stack(other, axis=1)], axis=0
        ).reshape(2 * own_rows, D)

    def home_tokens(v):
        v = v.reshape(images, 4, PAD, D)
        got = [to_seq(v[:, k], k) if k else v[:, 0] for k in range(4)]
        for bit in (1, 2):
            flip = (s & bit) != 0
            got = [jnp.where(flip, got[k ^ bit], got[k]) for k in range(4)]
        return jnp.stack([piece[:, :TOK] for piece in got], axis=1)

    qp_shard = jnp.concatenate(
        [
            pick(qkv_weight.reshape(-1, 3, 2, HALF), c, 2).reshape(-1, 3 * HALF),
            pick(proj_weight.reshape(-1, 2, HALF), c, 1),
        ],
        axis=1,
    )
    hidden_shard = pick(hidden_weight.reshape(-1, 4, 2, HALF), c, 2).reshape(-1, FF // 2)
    output_shard = pick(output_weight.reshape(2, HALF, D), c)
    x_low = spread_tokens(image_tokens)
    w_qp = gather(qp_shard)
    w_hidden = gather(hidden_shard)
    w_output = gather(output_shard)
    cot = spread_tokens(cotangent)
    w_qkv = w_qp[:, : 3 * HALF]
    proj_cols = w_qp[:, 3 * HALF :].reshape(2, HALF, HALF)
    proj_mine = pick(proj_cols, c)
    proj_other = to_core(pick(proj_cols, 1 - c))
    w_proj = jnp.where(
        c == 0,
        jnp.concatenate([proj_mine, proj_other], axis=1),
        jnp.concatenate([proj_other, proj_mine], axis=1),
    )
    b_qkv = pick(qkv_bias.reshape(3, 2, HALF), c, 1).reshape(-1)
    b_hidden = pick(hidden_bias.reshape(4, 2, HALF), c, 1).reshape(-1)

    row = jnp.arange(ROWS)
    token = (s ^ (row // PAD)) * TOK + row % PAD
    real = row % PAD < TOK
    t_r, t_c = token // WIN, token % WIN
    window = pick(slot_window, s)
    ok = (
        real
        & (window >= 0)
        & (window // NWS * WIN + t_r < GRID)
        & (window % NWS * WIN + t_c < GRID)
    ).astype(F32)
    keep_own = jnp.tile(ok, images)[:, None]
    keep = jnp.tile(ok, 2 * images)[:, None]
    near = jnp.arange(WIN)[:, None] - jnp.arange(WIN)[None, :] + WIN - 1
    height = rel_height[near].reshape(WIN * WIN, HD).T
    width = rel_width[near].reshape(WIN * WIN, HD).T
    gap = jnp.zeros((HD, TAB // 2 - WIN * WIN), BF)
    flat = jnp.concatenate([height, gap, width, gap], axis=1)
    blank = jnp.zeros_like(flat)
    table = jnp.stack([jnp.concatenate([flat, blank]), jnp.concatenate([blank, flat])])
    col = jnp.arange(TAB)
    in_half = col % (TAB // 2)
    col_from = jnp.where(in_half < WIN * WIN, in_half // WIN, -1)
    spot = (
        jnp.where(col[None, :] < TAB // 2, t_r[:, None], t_c[:, None]) == col_from[None, :]
    ).astype(F32)
    col_to = jnp.where(in_half < WIN * WIN, in_half % WIN + WIN * (col // (TAB // 2)), -1)
    fold = (col_to[:, None] == jnp.arange(LANES)[None, :]).astype(BF)
    lanes = jnp.arange(LANES)[None, :]
    keys = (
        real[:, None] & ((lanes == t_r[:, None]) | (lanes == WIN + t_c[:, None]))
    ).astype(BF)
    key_bias = jnp.where(real, 0.0, NEG).astype(F32)[None, :]

    def centre_of(v):
        v = v - jnp.mean(v, axis=-1, keepdims=True)
        rstd = lax.rsqrt(jnp.mean(v * v, axis=-1, keepdims=True) + 1e-06)
        return v * rstd, rstd

    def norm_back(grad, unit, rstd):
        return rstd * (
            grad
            - jnp.mean(grad, axis=-1, keepdims=True)
            - unit * jnp.mean(grad * unit, axis=-1, keepdims=True)
        )

    x = x_low.astype(F32)
    unit_one, rstd_one = centre_of(x)
    normed = ((unit_one * first_gain + first_bias) * keep).astype(BF)
    packed = (mm(normed, w_qkv) + b_qkv).astype(BF).reshape(2 * images, ROWS, 3 * HALF)
    attended, probs = attn_fwd(packed, table, spot, fold, keys, key_bias)
    attended = attended.reshape(2 * own_rows, HALF)
    branch = mm(attended, w_proj)
    branch_there = to_core(jnp.concatenate([branch[own_rows:], branch[:own_rows]]).astype(BF))
    middle = x + (branch + branch_there.astype(F32)) + proj_bias
    unit_two, rstd_two = centre_of(middle)
    second = (unit_two * second_gain + second_bias).astype(BF)
    pre_act = mm(second, w_hidden) + b_hidden
    phi = 0.5 * (1.0 + lax.erf(pre_act * (0.5**0.5)))
    active = (pre_act * phi).astype(BF)
    slope = (phi + pre_act * jnp.exp(-0.5 * pre_act * pre_act) * 0.3989422804014327).astype(BF)

    def blocks(grad):
        keep_two = jnp.stack([pick(grad, s, 1), pick(grad, b, 1)])
        send_two = jnp.stack([pick(grad, a, 1), pick(grad, d, 1)])
        return keep_two, send_two

    def reduce_plane(grad):
        keep_two, send_two = blocks(grad.astype(BF))
        one = keep_two.astype(F32) + to_plane(send_two, plane_one).astype(F32)
        two = one[0] + to_plane(one[1].astype(BF), plane_two).astype(F32)
        heads, rows, width_here = two.shape
        two = two.reshape(heads, 4, rows // 4, width_here)
        total = pick(two, z, 1)
        for k in (1, 2, 3):
            total = total + to_z(pick(two, (z + k) % 4, 1).astype(BF), k).astype(F32)
        return total

    def swap_halves(total):
        mine = pick(total, c)
        there = to_core(pick(total, 1 - c))
        return jnp.where(c == 0, mine, there), jnp.where(c == 0, there, mine)

    def interleave(grad, parts):
        if n_dp == 2:
            low, high = swap_halves(reduce_plane(grad.reshape(2, 4, -1, parts * HALF)))
            rows = low.shape[0]
            return jnp.stack(
                [low.reshape(rows, parts, HALF), high.reshape(rows, parts, HALF)], axis=2
            ).reshape(rows, 2 * parts * HALF)
        grad = grad.reshape(D, parts, HALF)
        zero = jnp.zeros_like(grad)
        full = jnp.where(
            c == 0, jnp.stack([grad, zero], axis=2), jnp.stack([zero, grad], axis=2)
        ).reshape(D, 2 * parts * HALF)
        return lax.psum_scatter(full, ("dp", "seq", "fsdp"), scatter_dimension=0, tiled=True)

    def stacked(grad):
        if n_dp == 2:
            return reduce_plane(grad.reshape(1, 4, -1, D))[0]
        zero = jnp.zeros_like(grad)
        full = jnp.where(c == 0, jnp.concatenate([grad, zero]), jnp.concatenate([zero, grad]))
        return lax.psum_scatter(full, ("dp", "seq", "fsdp"), scatter_dimension=0, tiled=True)

    grad_out = cot.astype(F32) * keep
    grad_feed = grad_out.astype(BF)
    g_output = interleave(mm(grad_feed, active, ((0,), (0,))), 4).T
    grad_pre = (mm(grad_feed, w_output, ((1,), (1,))) * slope.astype(F32)).astype(BF)
    g_hidden = interleave(mm(second, grad_pre, ((0,), (0,))), 4)
    part = mm(grad_pre, w_hidden, ((1,), (1,)))
    part_there = to_core(jnp.concatenate([part[own_rows:], part[:own_rows]]).astype(BF))
    grad_second = part + part_there.astype(F32)
    grad_middle = grad_out + norm_back(grad_second * second_gain, unit_two, rstd_two)
    grad_branch = grad_middle.astype(BF)
    g_proj = stacked(mm(attended, grad_branch, ((0,), (0,))))
    grad_att = mm(grad_branch, w_proj, ((1,), (1,))).astype(BF)

    feed = mm(active, w_output)
    feed_there = to_core(feed[own_rows:].astype(BF))
    block = (
        (middle[:own_rows] + feed[:own_rows] + feed_there.astype(F32) + output_bias) * keep_own
    ).astype(BF)
    block_out = home_tokens(block)

    grad_packed, tab_grad = attn_bwd(
        packed, grad_att.reshape(2 * images, ROWS, HALF), probs, table, spot, fold, keys
    )
    grad_packed = grad_packed.reshape(2 * own_rows, 3 * HALF)
    g_qkv = interleave(mm(normed, grad_packed, ((0,), (0,))), 3)
    back = mm(grad_packed, w_qkv, ((1,), (1,)))
    back_there = to_core(back[own_rows:].astype(BF))
    grad_normed = (back[:own_rows] + back_there.astype(F32)) * keep_own
    unit_own = unit_one[:own_rows]
    tok_grad = norm_back(grad_normed * first_gain, unit_own, rstd_one[:own_rows])
    input_grad = home_tokens((grad_middle[:own_rows] + tok_grad).astype(BF))

    def at_core(v, parts):
        v = v.reshape(parts, HALF)
        zero = jnp.zeros_like(v)
        return jnp.where(
            c == 0, jnp.stack([v, zero], axis=1), jnp.stack([zero, v], axis=1)
        ).reshape(-1)

    tab_sum = (tab_grad[:, :HD] + tab_grad[:, HD:]).reshape(2, TAB // 2, HD)[:, : WIN * WIN]
    to_offset = (near.reshape(-1)[None, :] == jnp.arange(2 * WIN - 1)[:, None]).astype(F32)
    rel_sums = jnp.einsum(
        "jp,apd->ajd", to_offset, tab_sum, precision=lax.Precision.HIGHEST
    )
    terms = [
        jnp.sum(grad_normed * unit_own, axis=0),
        jnp.sum(grad_normed, axis=0),
        at_core(jnp.sum(grad_packed.astype(F32), axis=0), 3),
        rel_sums[0].reshape(-1),
        rel_sums[1].reshape(-1),
        jnp.sum(grad_branch[:own_rows].astype(F32), axis=0),
        jnp.sum(grad_second[:own_rows] * unit_two[:own_rows], axis=0),
        jnp.sum(grad_second[:own_rows], axis=0),
        at_core(jnp.sum(grad_pre.astype(F32), axis=0), 4),
        jnp.sum(grad_feed[:own_rows].astype(F32), axis=0),
    ]
    sizes = [term.shape[0] for term in terms]
    total = jnp.concatenate(terms)
    total = total + to_core(total)
    total = total + to_seq(total, 1)
    total = total + to_seq(total, 2)
    for hop in (1, 2):
        total = total + lax.ppermute(total, "fsdp", [(i, i ^ hop) for i in range(4)])
    if n_dp > 2:
        groups = [list(range(core, n_dp, 2)) for core in range(2)]
        total = lax.psum(total, "dp", axis_index_groups=groups)
    small = []
    at = 0
    for size in sizes:
        small.append(total[at : at + size])
        at += size
    return (
        block_out,
        input_grad,
        small[0],
        small[1],
        g_qkv,
        small[2],
        small[3].reshape(2 * WIN - 1, HD),
        small[4].reshape(2 * WIN - 1, HD),
        g_proj,
        small[5],
        small[6],
        small[7],
        g_hidden,
        small[8],
        g_output,
        small[9],
    )


def solution(mesh):
    tokens = P("dp", "fsdp", "seq", None)
    rows = P("fsdp", None)
    every = P(("dp", "seq", "fsdp"), None)
    return jax.shard_map(
        functools.partial(per_device, mesh.shape["dp"]),
        mesh=mesh,
        in_specs=(
            tokens,
            P("fsdp"),
            P(),
            P(),
            rows,
            P(),
            P(),
            P(),
            rows,
            P(),
            P(),
            P(),
            rows,
            P(),
            rows,
            P(),
            tokens,
        ),
        out_specs=(
            tokens,
            tokens,
            P(),
            P(),
            every,
            P(),
            P(),
            P(),
            every,
            P(),
            P(),
            P(),
            every,
            P(),
            P(None, ("dp", "seq", "fsdp")),
            P(),
        ),
        check_vma=False,
    )
```

```python
import functools

import jax
import jax.numpy as jnp
from jax import lax
from jax.experimental import pallas as pl
from jax.experimental.pallas import tpu as pltpu
from jax.sharding import PartitionSpec as P

D = 768
HD = 64
FF = 3072
WIN = 14
GRID = 48
NWS = 4
TOK = 49
PAD = 56
ROWS = 4 * PAD
SPLIT = 4 * TOK
HALF = D // 2
QKV = 3 * HALF
WIDE = 4 * HALF
PIECE = 48
PAIRS = 3
LANES = 128
TAB = 512
NEG = -1e30
EPS = 1e-06
SCALE = HD**-0.5
BF = jnp.bfloat16
F32 = jnp.float32
ANY = pl.BlockSpec(memory_space=pl.ANY)
HBM = pl.BlockSpec(memory_space=pltpu.HBM)
SMEM = pl.BlockSpec(memory_space=pltpu.SMEM)


def mm(left, right, dims=((1,), (0,))):
    return lax.dot_general(left, right, (dims, ((), ())), preferred_element_type=F32)


def array(shape, dtype=BF):
    return jax.ShapeDtypeStruct(shape, dtype)


def whole(shape):
    return pl.BlockSpec(shape, lambda *at: (0,) * len(shape))


def window(shape, index=None):
    index = index or (lambda w: w)
    return pl.BlockSpec((1,) + shape, lambda w: (index(w),) + (0,) * len(shape))


TIMES = dict(cut=0.3, join=0.3, pair_up=0.3, weld=0.3, norm_one=0.3, place_qp=0.3)


def call(kernel, name, ins, outs, grid=(), scratch=(), after=(), vmem=8, alias=()):
    count = len(ins)
    extra = len(after)

    def held(v):
        mode = pl.Buffered(1) if grid else None
        return pl.BlockSpec(v.shape, lambda *at: (0,) * len(v.shape), pipeline_mode=mode)

    def body(*refs):
        return kernel(*refs[:count], *refs[count + extra :])

    return pl.pallas_call(
        body,
        grid=grid,
        in_specs=[spec or held(v) for v, spec in ins] + [ANY] * extra,
        out_specs=[spec or whole(v.shape) for v, spec in outs],
        out_shape=[v for v, _ in outs],
        scratch_shapes=list(scratch),
        compiler_params=pltpu.CompilerParams(vmem_limit_bytes=vmem * 1024 * 1024),
        input_output_aliases=dict(alias),
        cost_estimate=pl.CostEstimate(
            flops=int(1.15e9 * TIMES.get(name, 87.0)),
            bytes_accessed=int(1.15e6 * TIMES.get(name, 87.0)),
            transcendentals=0,
        ),
        name=name,
    )(*[v for v, _ in ins], *after)


def pieces_kernel(where, qkv, proj, hidden, output, out, qp_out, sems):
    s, c = where[1], where[5]
    rows = pl.ds(pl.multiple_of(s * PIECE, PIECE), PIECE)
    start = pl.multiple_of(c * HALF + s * 2 * PIECE, 2 * PIECE)
    copies = [(output.at[pl.ds(start, 2 * PIECE)], out.at[: 2 * PIECE])]
    for i in range(4):
        cols = pl.ds(pl.multiple_of(i * D + c * HALF, LANES), HALF)
        at = (2 + i // 2) * PIECE
        half = slice(i % 2 * HALF, (i % 2 + 1) * HALF)
        copies.append((hidden.at[rows, cols], out.at[at : at + PIECE, half]))
    for i in range(3):
        cols = pl.ds(pl.multiple_of(i * D + c * HALF, LANES), HALF)
        copies.append((qkv.at[rows, cols], qp_out.at[:, i * HALF : (i + 1) * HALF]))
    cols = pl.ds(pl.multiple_of(c * HALF, LANES), HALF)
    copies.append((proj.at[rows, cols], qp_out.at[:, QKV:]))
    run_copies(copies, sems)


def run_copies(pairs, sems):
    copies = [
        pltpu.make_async_copy(src, dst, sems.at[n]) for n, (src, dst) in enumerate(pairs)
    ]
    for copy in copies:
        copy.start()
    for copy in copies:
        copy.wait()


def pieces(where, qkv, proj, hidden, output):
    return call(
        pieces_kernel,
        "pieces",
        [(where, SMEM), (qkv, HBM), (proj, HBM), (hidden, HBM), (output, HBM)],
        [(array((4 * PIECE, D)), None), (array((PIECE, WIDE)), None)],
        scratch=[pltpu.SemaphoreType.DMA((9,))],
        vmem=60,
    )


def output_part(w, first=0, count=16):
    return w[first : first + count, : 2 * PIECE, :].reshape(count * 2 * PIECE, D)


def hidden_part(w, half):
    at = (2 + half) * PIECE
    return w[:, at : at + PIECE, :].reshape(D, D)


def join_kernel(one, two, three, out):
    out[0] = one[...]
    out[1] = two[...]
    out[2] = three[...]


def join(parts, after=()):
    return call(
        join_kernel,
        "join",
        [(part, None) for part in parts],
        [(array((3,) + parts[0].shape), None)],
        after=after,
    )[0]


def place_qp_kernel(where, qkv, proj, first, second, third, fourth, out, send, sems):
    z, c = where[0], where[5]
    copies = []

    def add(src, dst):
        copies.append(pltpu.make_async_copy(src, dst, sems.at[len(copies)]))

    for i in range(3):
        for q in range(4):
            cols = pl.ds(pl.multiple_of(i * D + c * HALF, LANES), HALF)
            add(
                qkv.at[q * PIECE : (q + 1) * PIECE, cols],
                out.at[z, q, :, i * HALF : (i + 1) * HALF],
            )
    for q in range(4):
        cols = pl.ds(pl.multiple_of(c * HALF, LANES), HALF)
        add(proj.at[q * PIECE : (q + 1) * PIECE, cols], out.at[z, q, :, QKV:])
    for i in range(3):
        zz = lax.rem(z + 3 - i, 4)
        for n, src in enumerate((first, second, third, fourth)):
            add(src.at[i], out.at[zz, where[1 + n]])
    for copy in copies:
        copy.start()
    for copy in copies:
        copy.wait()
    send[...] = out[pl.ds(2 * (1 - c), 2), :, :, QKV:]


def place_ho_kernel(where, hidden, output, first, second, third, fourth, out, sems):
    z, c = where[0], where[5]
    copies = []
    for q in range(4):
        start = pl.multiple_of(c * HALF + q * 2 * PIECE, 2 * PIECE)
        copies.append((output.at[pl.ds(start, 2 * PIECE)], out.at[z, q, : 2 * PIECE]))
        for i in range(4):
            cols = pl.ds(pl.multiple_of(i * D + c * HALF, LANES), HALF)
            at = (2 + i // 2) * PIECE
            half = slice(i % 2 * HALF, (i % 2 + 1) * HALF)
            copies.append(
                (
                    hidden.at[q * PIECE : (q + 1) * PIECE, cols],
                    out.at[z, q, at : at + PIECE, half],
                )
            )
    for i in range(3):
        zz = lax.rem(z + 3 - i, 4)
        for n, src in enumerate((first, second, third, fourth)):
            copies.append((src.at[i], out.at[zz, where[1 + n]]))
    run_copies(copies, sems)


def hand_out(c, rows, i, outs):
    near, both, far = outs

    def piece(k):
        return rows[pl.ds(pl.multiple_of(k * PAD, 8), PAD), :].astype(BF)

    near[i] = piece(0)
    both[0, i] = piece(1 + c)
    both[1, i] = piece(3)
    far[i] = piece(2 - c)


def handed(images):
    shape = (images, PAD, D)
    return [(array(shape), None), (array((2,) + shape), None), (array(shape), None)]


ROWS_F32 = pltpu.VMEM((ROWS, D), F32)


def gathered_rows(c, near, one, two, i):
    first, second = one[0, i].astype(F32), two[0, i].astype(F32)
    parts = [near[i].astype(F32)]
    parts += [jnp.where(c == 0, first, second), jnp.where(c == 0, second, first)]
    return jnp.concatenate(parts + [two[1, i].astype(F32)])


def pair_kernel(far, one, out):
    out[0] = far[...]
    out[1] = one[1]


def pair_up(far, one, after=()):
    return call(
        pair_kernel,
        "pair_up",
        [(far, None), (one, None)],
        [(array((2,) + far.shape), None)],
        after=after,
    )[0]


def cut_kernel(where, tokens, cotangent, *rest):
    s, c = where[1], where[5]
    images = tokens.shape[0]
    outs, rows = rest[:3], rest[3]
    row = lax.broadcasted_iota(jnp.int32, (ROWS, SPLIT), 0)
    col = lax.broadcasted_iota(jnp.int32, (ROWS, SPLIT), 1)
    token = row % PAD
    take = ((token < TOK) & (col == token * 4 + (s ^ (row // PAD)))).astype(F32).astype(BF)
    for i in range(2 * images):
        rows[...] = mm(take, tokens[i] if i < images else cotangent[i - images])
        hand_out(c, rows, i, outs)


def cut(where, tokens, cotangent, after=()):
    images = tokens.shape[0]
    flat = [jnp.transpose(v, (0, 2, 1, 3)).reshape(images, SPLIT, D) for v in (tokens, cotangent)]
    return call(
        cut_kernel,
        "cut",
        [(where, SMEM)] + [(v, None) for v in flat],
        handed(2 * images),
        scratch=[ROWS_F32],
        after=after,
        vmem=12,
    )


def weld_kernel(where, ok, near, one, two, out):
    count = out.shape[0]
    for i in range(count):
        rows = gathered_rows(where[5], near, one, two, i)
        out[i] = (rows if i < count // 2 else rows * ok[...]).astype(BF)


def weld(where, ok, near, one, two, after=()):
    return call(
        weld_kernel,
        "weld",
        [(where, SMEM), (ok, None)] + [(part, None) for part in (near, one, two)],
        [(array((near.shape[0], ROWS, D)), None)],
        after=after,
    )[0]


def home_kernel(where, near, one, two, *outs):
    s = where[1]
    row = lax.broadcasted_iota(jnp.int32, (SPLIT, ROWS), 0)
    col = lax.broadcasted_iota(jnp.int32, (SPLIT, ROWS), 1)
    token = col % PAD
    take = ((token < TOK) & (row == token * 4 + (s ^ (col // PAD)))).astype(F32).astype(BF)
    images = outs[0].shape[0]
    for i in range(2 * images):
        rows = gathered_rows(where[5], near, one, two, i).astype(BF)
        outs[i // images][i % images] = mm(take, rows).astype(BF)


def home(where, near, one, two, after=()):
    images = near.shape[0] // 2
    flat = call(
        home_kernel,
        "home",
        [(where, SMEM)] + [(part, None) for part in (near, one, two)],
        [(array((images, SPLIT, D)), None)] * 2,
        after=after,
        vmem=12,
    )
    return [jnp.transpose(v.reshape(images, TOK, 4, D), (0, 2, 1, 3)) for v in flat]


def unit_of(v):
    v = v - jnp.mean(v, axis=-1, keepdims=True)
    rstd = lax.rsqrt(jnp.mean(v * v, axis=-1, keepdims=True) + EPS)
    return v * rstd, rstd


def norm_back(grad, unit, rstd):
    return rstd * (
        grad
        - jnp.mean(grad, axis=-1, keepdims=True)
        - unit * jnp.mean(grad * unit, axis=-1, keepdims=True)
    )


def norm_one_kernel(ok, own, other, gain, shift, out):
    images = own.shape[0] // 2
    for w in range(2 * images):
        x = own[w] if w < images else other[w - images]
        unit, _ = unit_of(x.astype(F32))
        out[w] = ((unit * gain[...] + shift[...]) * ok[...]).astype(BF)


def norm_one(ok, own, other, gain, shift, after=()):
    return call(
        norm_one_kernel,
        "norm_one",
        [(v, None) for v in (ok, own, other, gain, shift)],
        [(array(own.shape), None)],
        after=after,
        vmem=12,
    )[0]


def norm_two_kernel(
    own, other, branch, branch_other, there, bias, gain, shift, middle, second
):
    images = own.shape[0] // 2
    for w in range(2 * images):
        x, mine = (own, branch) if w < images else (other, branch_other)
        at = w % images
        value = x[at].astype(F32) + (mine[at] + there[w].astype(F32)) + bias[...]
        middle[w] = value
        unit, _ = unit_of(value)
        second[w] = (unit * gain[...] + shift[...]).astype(BF)


def norm_two(own, other, branch, branch_other, there, bias, gain, shift, after=()):
    shape = own.shape
    ins = (own, other, branch, branch_other, there, bias, gain, shift)
    return call(
        norm_two_kernel,
        "norm_two",
        [(v, None) for v in ins],
        [(array(shape, F32), None), (array(shape), None)],
        after=after,
        vmem=14,
    )


def norm_two_back_kernel(
    images, part, there, middle, gain, feed, feed_other, grad_middle, grad_branch, sums
):
    sums[...] = jnp.zeros_like(sums)
    for w in range(2 * images):
        grad = part[w] + there[w].astype(F32)
        unit, rstd = unit_of(middle[w])
        feed_w = (feed[images + w] if w < images else feed_other[w]).astype(F32)
        total = feed_w + norm_back(grad * gain[...], unit, rstd)
        low = total.astype(BF)
        grad_branch[w] = low
        if w < images:
            grad_middle[w] = total
            sums[0:1] += jnp.sum(grad * unit, axis=0, keepdims=True)
            sums[1:2] += jnp.sum(grad, axis=0, keepdims=True)
            sums[2:3] += jnp.sum(low.astype(F32), axis=0, keepdims=True)
            sums[3:4] += jnp.sum(feed_w, axis=0, keepdims=True)


def norm_two_back(part, there, middle, gain, feed, feed_other, after=()):
    count = part.shape[0]
    return call(
        functools.partial(norm_two_back_kernel, count // 2),
        "norm_two_back",
        [(v, None) for v in (part, there, middle, gain, feed, feed_other)],
        [
            (array((count // 2, ROWS, D), F32), None),
            (array((count, ROWS, D)), None),
            (array((8, D), F32), None),
        ],
        after=after,
        vmem=16,
    )


def last_kernel(
    where, ok, back, back_there, own, gain, grad_middle, middle, feed, feed_there, bias, *rest
):
    outs, sums, rows = rest[:3], rest[3], rest[4]
    images = back.shape[0]
    sums[...] = jnp.zeros_like(sums)
    for w in range(images):
        grad = (back[w] + back_there[w].astype(F32)) * ok[...]
        unit, rstd = unit_of(own[w].astype(F32))
        sums[0:1] += jnp.sum(grad * unit, axis=0, keepdims=True)
        sums[1:2] += jnp.sum(grad, axis=0, keepdims=True)
        rows[...] = grad_middle[w] + norm_back(grad * gain[...], unit, rstd)
        hand_out(where[5], rows, w, outs)
        rows[...] = (middle[w] + feed[w] + feed_there[w].astype(F32) + bias[...]) * ok[...]
        hand_out(where[5], rows, images + w, outs)


def last(where, ok, back, back_there, own, gain, grad_middle, middle, feed, feed_there, bias, after=()):
    ins = (ok, back, back_there, own, gain, grad_middle, middle, feed, feed_there, bias)
    return call(
        last_kernel,
        "last",
        [(where, SMEM)] + [(v, None) for v in ins],
        handed(own.shape[0]) + [(array((8, D), F32), None)],
        scratch=[ROWS_F32],
        after=after,
        vmem=20,
    )


def attn_fwd_kernel(
    where, normed, w_qp, other, b_qkv, table, spot, fold, keys, bias, *rest
):
    packed, out, probs, low, branch = rest[-5:]
    c = where[5]
    lane = lax.broadcasted_iota(jnp.int32, (ROWS, LANES), 1)
    packed[0] = (mm(normed[0], w_qp[:, :QKV]) + b_qkv[...]).astype(BF)
    for pair in range(PAIRS):
        q = packed[0, :, pair * LANES : (pair + 1) * LANES]
        k = packed[0, :, HALF + pair * LANES : HALF + (pair + 1) * LANES]
        v = packed[0, :, 2 * HALF + pair * LANES : 2 * HALF + (pair + 1) * LANES]
        right = jnp.concatenate([k, keys[...]], axis=1)
        parts = []
        for e in range(2):
            mine = (lane < HD) if e == 0 else (lane >= HD)
            spread = (mm(q, table[e]) * spot[...]).astype(BF)
            rel = mm(spread, fold[...]).astype(BF)
            scaled = jnp.where(mine, q.astype(F32) * SCALE, 0.0).astype(BF)
            left = jnp.concatenate([scaled, rel], axis=1)
            s = mm(left, right, ((1,), (1,))) + bias[...]
            p = jnp.exp(s - jnp.max(s, axis=1, keepdims=True))
            p = (p * (1.0 / jnp.sum(p, axis=1, keepdims=True))).astype(BF)
            probs[0, 2 * pair + e] = p
            parts.append(mm(p, v))
        out[0, :, pair * LANES : (pair + 1) * LANES] = jnp.where(
            lane < HD, parts[0], parts[1]
        ).astype(BF)
    att = out[0]
    own_cols = pl.ds(pl.multiple_of(c * HALF, LANES), HALF)
    other_cols = pl.ds(pl.multiple_of((1 - c) * HALF, LANES), HALF)
    own_rows = pl.ds(pl.multiple_of(c * HALF, HALF), HALF)
    mine = mm(att, w_qp[own_rows, QKV:])
    theirs = mm(att, other[...])
    branch[0, :, own_cols] = mine
    branch[0, :, other_cols] = theirs
    low[0, :, own_cols] = mine.astype(BF)
    low[0, :, other_cols] = theirs.astype(BF)


def attn_fwd(where, group, normed, w_qp, other, b_qkv, tables, before=(), after=()):
    table, spot, fold, keys, bias = tables
    count = normed.shape[0]
    half = count // 2
    start = group * half
    ins = [(where, SMEM), (normed, window((ROWS, D), lambda w: w + start))]
    ins += [(v, None) for v in (w_qp, other, b_qkv, table, spot, fold, keys, bias)]
    kept = ((ROWS, QKV), (ROWS, HALF), (2 * PAIRS, ROWS, ROWS))
    outs = [(array((count,) + shape), window(shape, lambda w: w + start)) for shape in kept]
    outs += [
        (array((count, ROWS, D)), window((ROWS, D), lambda w: (w + start + half) % count)),
        (array((half, ROWS, D), F32), window((ROWS, D))),
    ]
    return call(
        attn_fwd_kernel,
        "attn_fwd",
        ins + [(v, ANY) for v in before],
        outs,
        grid=(half,),
        after=after,
        alias=[(len(ins) + n, n) for n in range(len(before))],
        vmem=18,
    )


def attn_bwd_kernel(
    where, packed, grad_branch, probs, w_qp, other, table, spot, fold, keys, *rest
):
    out, tab_grad, sums, att = rest[-4:]
    c = where[5]
    lane = lax.broadcasted_iota(jnp.int32, (ROWS, LANES), 1)
    lane_t = lax.broadcasted_iota(jnp.int32, (TAB, LANES), 1)

    @pl.when(pl.program_id(0) == 0)
    def _():
        tab_grad[...] = jnp.zeros_like(tab_grad)
        sums[...] = jnp.zeros_like(sums)

    own_cols = pl.ds(pl.multiple_of(c * HALF, LANES), HALF)
    other_cols = pl.ds(pl.multiple_of((1 - c) * HALF, LANES), HALF)
    own_rows = pl.ds(pl.multiple_of(c * HALF, HALF), HALF)
    att[...] = (
        mm(grad_branch[0, :, own_cols], w_qp[own_rows, QKV:], ((1,), (1,)))
        + mm(grad_branch[0, :, other_cols], other[...], ((1,), (1,)))
    ).astype(BF)
    for pair in range(PAIRS):
        q = packed[0, :, pair * LANES : (pair + 1) * LANES]
        k = packed[0, :, HALF + pair * LANES : HALF + (pair + 1) * LANES]
        v = packed[0, :, 2 * HALF + pair * LANES : 2 * HALF + (pair + 1) * LANES]
        go = att[:, pair * LANES : (pair + 1) * LANES]
        right = jnp.concatenate([k, keys[...]], axis=1)
        dq, dk, dv, dt = [], [], [], []
        for e in range(2):
            mine = (lane < HD) if e == 0 else (lane >= HD)
            go_e = jnp.where(mine, go.astype(F32), 0.0).astype(BF)
            p_low = probs[0, 2 * pair + e]
            p = p_low.astype(F32)
            dp = mm(go_e, v, ((1,), (1,)))
            ds = (p * (dp - jnp.sum(dp * p, axis=1, keepdims=True))).astype(BF)
            both = mm(ds, right)
            rel = both[:, LANES:].astype(BF)
            spread = (mm(rel, fold[...], ((1,), (1,))) * spot[...]).astype(BF)
            dq.append(SCALE * both[:, :LANES] + mm(spread, table[e], ((1,), (1,))))
            dk.append(SCALE * mm(ds, q, ((0,), (0,))))
            dv.append(mm(p_low, go, ((0,), (0,))))
            dt.append(mm(spread, q, ((0,), (0,))))
        tab_grad[...] += jnp.where(lane_t < HD, dt[0], dt[1])
        for at, two in ((0, dq), (HALF, dk), (2 * HALF, dv)):
            low = jnp.where(lane < HD, two[0], two[1]).astype(BF)
            cols = slice(at + pair * LANES, at + (pair + 1) * LANES)
            out[0, :, cols] = low
            sums[0:1, cols] += jnp.sum(low.astype(F32), axis=0, keepdims=True)


def attn_bwd(where, group, packed, grad_branch, probs, w_qp, other, tables, before=(), after=()):
    table, spot, fold, keys, _ = tables
    count = packed.shape[0]
    half = count // 2
    start = group * half
    ins = [
        (where, SMEM),
        (packed, window((ROWS, QKV), lambda w: w + start)),
        (grad_branch, window((ROWS, D), lambda w: w + start)),
        (probs, window((2 * PAIRS, ROWS, ROWS), lambda w: w + start)),
    ]
    ins += [(v, None) for v in (w_qp, other, table, spot, fold, keys)]
    return call(
        attn_bwd_kernel,
        "attn_bwd",
        ins + [(v, ANY) for v in before],
        [
            (array((count, ROWS, QKV)), window((ROWS, QKV), lambda w: w + start)),
            (array((TAB, LANES), F32), None),
            (array((8, QKV), F32), None),
        ],
        grid=(half,),
        scratch=[pltpu.VMEM((ROWS, HALF), BF)],
        after=after,
        alias=[(len(ins) + n, n) for n in range(len(before))],
        vmem=18,
    )


def hidden_kernel(second, w, bias, active, slope):
    for half in range(2):
        cols = slice(half * D, (half + 1) * D)
        v = mm(second[0], hidden_part(w, half)) + bias[:, cols]
        phi = 0.5 * (1.0 + lax.erf(v * (0.5**0.5)))
        active[0, :, cols] = (v * phi).astype(BF)
        slope[0, :, cols] = (phi + v * (jnp.exp(-0.5 * v * v) * 0.3989422804014327)).astype(BF)


def hidden_layer(second, w_hidden, bias, after=()):
    count = second.shape[0]
    return call(
        hidden_kernel,
        "hidden",
        [(second, window((ROWS, D))), (w_hidden, None), (bias, None)],
        [(array((count, ROWS, WIDE)), window((ROWS, WIDE)))] * 2,
        grid=(count,),
        after=after,
        vmem=14,
    )


def product_kernel(of, count, left, right, own, low):
    w = pl.program_id(0)
    value = of(left[0], right)

    @pl.when(w < count // 2)
    def _():
        low[w] = value.astype(BF)

    @pl.when(w >= count // 2)
    def _():
        own[w - count // 2] = value


def product(name, left, right, right_spec, of, after=()):
    count = left.shape[0]
    shape = (count // 2, ROWS, D)
    return call(
        functools.partial(product_kernel, of, count),
        name,
        [(left, window(left.shape[1:], lambda w: (w + count // 2) % count)), (right, right_spec)],
        [(array(shape, F32), None), (array(shape), None)],
        grid=(count,),
        after=after,
        vmem=14,
    )


def grad_pre_kernel(count, own, other, slope, w, out, part, low, sums):
    feed = jnp.where(pl.program_id(0) < count // 2, own[0].astype(F32), other[0].astype(F32))
    feed = feed.astype(BF)

    @pl.when(pl.program_id(0) == 0)
    def _():
        sums[...] = jnp.zeros_like(sums)

    for half in range(2):
        cols = slice(half * D, (half + 1) * D)
        value = mm(feed, output_part(w, 8 * half, 8), ((1,), (1,))) * slope[0, :, cols].astype(F32)
        value = value.astype(BF)
        out[0, :, cols] = value
        sums[0:1, cols] += jnp.sum(value.astype(F32), axis=0, keepdims=True)
    value = mm(out[0, :, :D], hidden_part(w, 0), ((1,), (1,)))
    value = value + mm(out[0, :, D:], hidden_part(w, 1), ((1,), (1,)))
    part[0] = value
    low[0] = value.astype(BF)


def grad_pre_of(own, other, slope, w, after=()):
    count = slope.shape[0]
    half = count // 2
    return call(
        functools.partial(grad_pre_kernel, count),
        "grad_pre",
        [
            (own, window((ROWS, D), lambda w: half + jnp.minimum(w, half - 1))),
            (other, window((ROWS, D), lambda w: half + jnp.maximum(w - half, 0))),
            (slope, window((ROWS, WIDE))),
            (w, None),
        ],
        [
            (array((count, ROWS, WIDE)), window((ROWS, WIDE))),
            (array((count, ROWS, D), F32), window((ROWS, D))),
            (array((count, ROWS, D)), window((ROWS, D), lambda w: (w + count // 2) % count)),
            (array((8, WIDE), F32), None),
        ],
        grid=(count,),
        after=after,
        vmem=18,
    )


def deal(where, total, keep, send, cols):
    for n, out in enumerate((keep, keep, send, send)):
        q = where[(1, 3, 2, 4)[n]]
        for h in range(2):
            rows = pl.ds(pl.multiple_of(h * HALF + q * 96, 8), 96)
            out[n % 2, h, :, cols] = total[rows, :].astype(BF)


def weight_grad_kernel(count, where, *refs):
    lefts, (right, keep, send, flip, total) = refs[:count], refs[count:]
    rows = right.shape[0] // count
    for n, left in enumerate(lefts):
        flip[:, n * rows : (n + 1) * rows] = left[left.shape[0] - rows :, :].T
    for at in range(0, WIDE, TAB):
        cols = slice(at, at + TAB)
        total[...] = mm(flip[...], right[:, cols])
        deal(where, total, keep, send, cols)


def weight_grad(where, lefts, right, after=()):
    rows = right.shape[0] * right.shape[1]
    shape = (2, 2, 96, WIDE)
    return call(
        functools.partial(weight_grad_kernel, len(lefts)),
        "weight_grad",
        [(where, SMEM)]
        + [(left.reshape(-1, D), None) for left in lefts]
        + [(right.reshape(rows, WIDE), None)],
        [(array(shape), None), (array(shape), None)],
        scratch=[pltpu.VMEM((D, rows), BF), pltpu.VMEM((D, TAB), F32)],
        after=after,
        vmem=16,
    )


def weight_grad_qp_kernel(
    where, normed, packed, att, branch, keep, send, flip, total, flip_att, total_att
):
    flip[...] = normed[...].T
    for at in range(0, QKV, HALF):
        cols = slice(at, at + HALF)
        total[...] = mm(flip[...], packed[:, cols])
        deal(where, total, keep, send, cols)
    flip_att[...] = att[...].T
    total_att[...] = mm(flip_att[...], branch[...])
    for n, out in enumerate((keep, keep, send, send)):
        q = where[(1, 3, 2, 4)[n]]
        rows = pl.ds(pl.multiple_of(q * 96, 8), 96)
        for h in range(2):
            out[n % 2, h, :, QKV:] = total_att[rows, h * HALF : (h + 1) * HALF].astype(BF)


def weight_grad_qp(where, normed, packed, att, branch, after=()):
    rows = normed.shape[0] * normed.shape[1]
    shape = (2, 2, 96, WIDE)
    return call(
        weight_grad_qp_kernel,
        "weight_grad_qp",
        [(where, SMEM)]
        + [(v.reshape(rows, v.shape[-1]), None) for v in (normed, packed, att, branch)],
        [(array(shape), None), (array(shape), None)],
        scratch=[
            pltpu.VMEM((D, rows), BF),
            pltpu.VMEM((D, HALF), F32),
            pltpu.VMEM((HALF, rows), BF),
            pltpu.VMEM((HALF, D), F32),
        ],
        after=after,
        vmem=16,
    )


def add_one_kernel(keep, got, stay, send):
    for h in range(2):
        for q in range(4):
            rows = slice(q * 24, (q + 1) * 24)
            stay[h, q] = keep[0, h, rows].astype(F32) + got[0, h, rows].astype(F32)
            send[h, q] = (keep[1, h, rows].astype(F32) + got[1, h, rows].astype(F32)).astype(BF)


def add_one(keep, got, after=()):
    shape = (2, 4, 24, WIDE)
    return call(
        add_one_kernel,
        "add_one",
        [(keep, None), (got, None)],
        [(array(shape, F32), None), (array(shape), None)],
        after=after,
    )


def add_two_kernel(where, *refs):
    z = where[0]
    keep, send = refs[-2:]
    for i in range(len(refs) // 2 - 1):
        stay, got = refs[2 * i], refs[2 * i + 1]
        for n in range(2):
            mine, theirs = z ^ (2 * n), z ^ (2 * n + 1)
            for h in range(2):
                keep[n, i, h] = stay[h, mine] + got[h, mine].astype(F32)
                send[n, i, h] = (stay[h, theirs] + got[h, theirs].astype(F32)).astype(BF)


def add_two(where, parts, after=()):
    shape = (2, len(parts), 2, 24, WIDE)
    return call(
        add_two_kernel,
        "add_two",
        [(where, SMEM)] + [(v, None) for part in parts for v in part],
        [(array(shape, F32), None), (array(shape), None)],
        after=after,
        vmem=12,
    )


def add_three_kernel(keep, got, stay, send):
    for i in range(stay.shape[0]):
        for h in range(2):
            stay[i, h] = keep[0, i, h] + got[0, i, h].astype(F32)
            send[i, h] = (keep[1, i, h] + got[1, i, h].astype(F32)).astype(BF)


def add_three(keep, got, after=()):
    shape = keep.shape[1:]
    return call(
        add_three_kernel,
        "add_three",
        [(keep, None), (got, None)],
        [(array(shape, F32), None), (array(shape), None)],
        after=after,
    )


def add_four_kernel(where, stay, got, total, send):
    for i in range(stay.shape[0]):
        for h in range(2):
            total[i, h] = stay[i, h] + got[i, h].astype(F32)
        send[i] = total[i, 1 - where[5]]


def add_four(where, stay, got, after=()):
    shape = (stay.shape[0],) + stay.shape[2:]
    return call(
        add_four_kernel,
        "add_four",
        [(where, SMEM), (stay, None), (got, None)],
        [(array(stay.shape, F32), None), (array(shape, F32), None)],
        after=after,
    )


def finish_kernel(where, two, two_there, total, there, output, hidden, qkv, proj):
    c = where[5]

    def lay(out, blocks, mine, theirs):
        for i in range(blocks):
            cols = slice(i * HALF, (i + 1) * HALF)
            out[:, pl.ds(pl.multiple_of(i * D + c * HALF, LANES), HALF)] = mine[:, cols]
            out[:, pl.ds(pl.multiple_of(i * D + (1 - c) * HALF, LANES), HALF)] = theirs[:, cols]

    lay(output, 4, two.at[0, c], two_there.at[0])
    lay(hidden, 4, two.at[1, c], two_there.at[1])
    lay(qkv, 3, total.at[0, c], there.at[0])
    for h in range(2):
        proj[:, h * HALF : (h + 1) * HALF] = total[0, h, :, QKV:]


def finish(where, two, two_there, total, there, after=()):
    return call(
        finish_kernel,
        "finish",
        [(where, SMEM)] + [(v, None) for v in (two, two_there, total, there)],
        [(array((24, blocks * D), F32), None) for blocks in (4, 4, 3, 1)],
        after=after,
    )


def small_kernel(where, two, one, hidden, qkv, qkv_b, tab, tab_b, to_offset, out):
    c = where[5]
    out[...] = jnp.zeros_like(out)
    cols = pl.ds(pl.multiple_of(c * HALF, LANES), HALF)
    for i in range(3):
        part = slice(i * HALF, (i + 1) * HALF)
        out[i : i + 1, cols] = qkv[0:1, part] + qkv_b[0:1, part]
    for i in range(4):
        out[3 + i : 4 + i, cols] = hidden[0:1, i * HALF : (i + 1) * HALF]
    for i in range(4):
        out[7 + i : 8 + i, :] = two[i : i + 1, :]
    for i in range(2):
        out[11 + i : 12 + i, :] = one[i : i + 1, :]
        half = slice(i * (TAB // 2), (i + 1) * (TAB // 2))
        rel = lax.dot_general(
            to_offset[...],
            tab[half, :] + tab_b[half, :],
            (((1,), (0,)), ((), ())),
            preferred_element_type=F32,
            precision=lax.Precision.HIGHEST,
        )
        for k in range(4):
            out[16 + 8 * i : 24 + 8 * i, k * LANES : (k + 1) * LANES] = rel[8 * k : 8 * k + 8]


def tally_kernel(one, two, out):
    out[...] = one[...] + two[...]


def tally(one, two, after=()):
    return call(
        tally_kernel,
        "tally",
        [(one, None), (two, None)],
        [(array(one.shape, F32), None)],
        after=after,
    )[0]


def unpack_kernel(total, *outs):
    qkv, height, width, proj, gain_two, bias_two, hidden, output, gain_one, bias_one = outs
    for i in range(3):
        qkv[i * D : (i + 1) * D] = total[i, :]
    for i in range(4):
        hidden[i * D : (i + 1) * D] = total[3 + i, :]
    rows = (gain_two, bias_two, proj, output, gain_one, bias_one)
    for i, out in enumerate(rows):
        out[...] = total[7 + i, :]
    for i, out in enumerate((height, width)):
        at = slice(16 + 8 * i, 24 + 8 * i)
        rel = jnp.concatenate([total[at, k * LANES : (k + 1) * LANES] for k in range(4)])
        out[...] = (rel + pltpu.roll(rel, HD, 1))[: 2 * WIN - 1, :HD]


def unpack(total):
    rel = (2 * WIN - 1, HD)
    shapes = [(2 * QKV,), rel, rel] + [(D,)] * 3 + [(FF,)] + [(D,)] * 3
    return call(
        unpack_kernel, "unpack", [(total, None)], [(array(shape, F32), None) for shape in shapes]
    )


def per_device(
    n_dp,
    image_tokens,
    slot_window,
    first_gain,
    first_bias,
    qkv_weight,
    qkv_bias,
    rel_height,
    rel_width,
    proj_weight,
    proj_bias,
    second_gain,
    second_bias,
    hidden_weight,
    hidden_bias,
    output_weight,
    output_bias,
    cotangent,
):
    images = image_tokens.shape[0]
    count = 2 * images
    c = lax.axis_index("dp") % 2
    s = lax.axis_index("seq")
    z = lax.axis_index("fsdp")
    a = jnp.where(c == 0, s ^ 1, s ^ 2)
    b = jnp.where(c == 0, s ^ 2, s ^ 1)
    where = jnp.stack([z, s, a, b, s ^ 3, c]).astype(jnp.int32)

    def plane_perm(step):
        out = []
        for i in range(n_dp):
            hop = (1, 2)[(i + step) % 2]
            out += [(i * 4 + j, i * 4 + (j ^ hop)) for j in range(4)]
        return out

    plane_one, plane_two = plane_perm(0), plane_perm(1)

    def to_core(v):
        return lax.ppermute(v, "dp", [(i, i ^ 1) for i in range(n_dp)])

    def to_seq(v, k):
        return lax.ppermute(v, "seq", [(i, i ^ k) for i in range(4)])

    def to_z(v, k):
        return lax.ppermute(v, "fsdp", [(i, (i + k) % 4) for i in range(4)])

    def swap_z(v, hop):
        return lax.ppermute(v, "fsdp", [(i, i ^ hop) for i in range(4)])

    def to_plane(v, perm):
        return lax.ppermute(v, ("dp", "seq"), perm)

    def pick(v, index, axis=0):
        return lax.dynamic_index_in_dim(v, index, axis, keepdims=False)

    row = jnp.arange(ROWS)
    token = (s ^ (row // PAD)) * TOK + row % PAD
    real = row % PAD < TOK
    t_r, t_c = token // WIN, token % WIN
    slot = pick(slot_window, s)
    ok = (
        real
        & (slot >= 0)
        & (slot // NWS * WIN + t_r < GRID)
        & (slot % NWS * WIN + t_c < GRID)
    ).astype(F32)[:, None]
    ones = jnp.ones((ROWS, 1), F32)
    near_offset = jnp.arange(WIN)[:, None] - jnp.arange(WIN)[None, :] + WIN - 1
    height = rel_height[near_offset].reshape(WIN * WIN, HD).T
    width = rel_width[near_offset].reshape(WIN * WIN, HD).T
    gap = jnp.zeros((HD, TAB // 2 - WIN * WIN), BF)
    flat = jnp.concatenate([height, gap, width, gap], axis=1)
    blank = jnp.zeros_like(flat)
    table = jnp.stack([jnp.concatenate([flat, blank]), jnp.concatenate([blank, flat])])
    col = jnp.arange(TAB)
    in_half = col % (TAB // 2)
    col_from = jnp.where(in_half < WIN * WIN, in_half // WIN, -1)
    spot = (
        jnp.where(col[None, :] < TAB // 2, t_r[:, None], t_c[:, None]) == col_from[None, :]
    ).astype(F32)
    col_to = jnp.where(in_half < WIN * WIN, in_half % WIN + WIN * (col // (TAB // 2)), -1)
    fold = (col_to[:, None] == jnp.arange(LANES)[None, :]).astype(BF)
    lanes = jnp.arange(LANES)[None, :]
    keys = (
        real[:, None] & ((lanes == t_r[:, None]) | (lanes == WIN + t_c[:, None]))
    ).astype(BF)
    key_bias = jnp.where(real, 0.0, NEG).astype(F32)[None, :]
    tables = (table, spot, fold, keys, key_bias)
    gain_one, bias_one = first_gain[None], first_bias[None]
    gain_two, bias_two = second_gain[None], second_bias[None]

    def mine_of(v, parts):
        v = v.reshape(parts, 2, HALF)
        return jnp.where(c == 0, v[:, 0], v[:, 1]).reshape(1, -1)

    b_qkv, b_hidden = mine_of(qkv_bias, 3), mine_of(hidden_bias, 4)

    def along_z(piece):
        return [to_z(piece, k) for k in (1, 2, 3)]

    def in_plane(first):
        second = to_plane(first, plane_one)
        third = to_plane(first, plane_two)
        fourth = to_plane(second, plane_two)
        return first, second, third, fourth

    def exchange(parts, after=()):
        near, both, far = parts
        one = to_plane(both, plane_one)
        send = pair_up(far, one, after)
        return near, one, to_plane(send, plane_two), send

    ho_piece, qp_piece = pieces(where, qkv_weight, proj_weight, hidden_weight, output_weight)
    z_qp = along_z(qp_piece)
    tokens_cut = cut(where, image_tokens, cotangent, after=[qp_piece])
    z_ho = along_z(ho_piece)
    first_qp = join(z_qp, after=[tokens_cut[0]])
    got_qp = in_plane(first_qp)
    near, one, two, _ = exchange(tokens_cut, after=[got_qp[1]])
    own = weld(where, ok, near, one, two, after=got_qp[1:])
    other = to_core(own)
    w_qp, proj_send = call(
        place_qp_kernel,
        "place_qp",
        [(where, SMEM), (qkv_weight, HBM), (proj_weight, HBM)] + [(v, ANY) for v in got_qp],
        [
            (array((4, 4, PIECE, WIDE)), None),
            (array((2, 4, PIECE, HALF)), None),
        ],
        scratch=[pltpu.SemaphoreType.DMA((28,))],
        after=[own],
    )
    w_qp = w_qp.reshape(D, WIDE)
    proj_other = to_core(proj_send.reshape(HALF, HALF))
    normed = norm_one(ok, own, other, gain_one, bias_one, after=[w_qp])
    got_ho = in_plane(join(z_ho, after=[normed]))
    packed, attended, probs, low, branch_other = attn_fwd(
        where, 1, normed, w_qp, proj_other, b_qkv, tables, after=[got_ho[0]]
    )
    packed, attended, probs, low, branch = attn_fwd(
        where, 0, normed, w_qp, proj_other, b_qkv, tables,
        before=(packed, attended, probs, low), after=[got_ho[1]],
    )
    there = to_core(low)
    w_ho = call(
        place_ho_kernel,
        "place_ho",
        [(where, SMEM), (hidden_weight, HBM), (output_weight, HBM)] + [(v, ANY) for v in got_ho],
        [(array((4, 4, 4 * PIECE, D)), None)],
        scratch=[pltpu.SemaphoreType.DMA((32,))],
        after=[packed],
    )[0].reshape(16, 4 * PIECE, D)
    middle, second = norm_two(
        own, other, branch, branch_other, there, proj_bias[None], gain_two, bias_two, after=[w_ho]
    )
    active, slope = hidden_layer(second, w_ho, b_hidden)

    def natural(keep_two, send_two):
        out = jnp.zeros((2, 4, 96, WIDE), BF)
        for q, part in ((s, keep_two[0]), (b, keep_two[1]), (a, send_two[0]), (s ^ 3, send_two[1])):
            out = lax.dynamic_update_index_in_dim(out, part, q, 1)
        return out.astype(F32)

    def sum_rows(full):
        return lax.psum_scatter(full, ("dp", "seq", "fsdp"), scatter_dimension=0, tiled=True)

    def spread_cols(grad, parts):
        grad = grad.reshape(D, parts, HALF)
        zero = jnp.zeros_like(grad)
        return jnp.where(
            c == 0, jnp.stack([grad, zero], axis=2), jnp.stack([zero, grad], axis=2)
        ).reshape(D, 2 * parts * HALF)

    def larger_wide(keep_two, send_two):
        return sum_rows(spread_cols(natural(keep_two, send_two).reshape(D, WIDE), 4))

    def larger_qp(keep_two, send_two):
        grad = natural(keep_two, send_two)
        qkv = sum_rows(spread_cols(grad[..., :QKV].reshape(D, QKV), 3))
        proj = jnp.concatenate(list(grad[..., QKV:].reshape(2, HALF, HALF)), axis=1)
        zero = jnp.zeros_like(proj)
        proj = jnp.where(c == 0, jnp.concatenate([proj, zero]), jnp.concatenate([zero, proj]))
        return qkv, sum_rows(proj)

    def step_one(send):
        return to_plane(send, plane_one)

    def step_two(keep, got, after=()):
        stay, send = add_one(keep, got, after)
        return stay, to_plane(send, plane_two), send

    def step_three(parts, after=()):
        keep, send = add_two(where, parts, after)
        return keep, swap_z(send, 1), send

    def step_four(keep, got, after=()):
        stay, send = add_three(keep, got, after)
        return stay, swap_z(send, 2), send

    def step_five(stay, got, after=()):
        total, send = add_four(where, stay, got, after)
        return total, to_core(send), send

    pair = n_dp == 2

    o_keep, o_send = weight_grad(where, [own, other], active)
    o_got = step_one(o_send) if pair else o_send
    grad_pre, part, part_low, hidden_sums = grad_pre_of(own, other, slope, w_ho, after=[o_send])
    part_there = to_core(part_low)
    h_keep, h_send = weight_grad(where, [second], grad_pre)
    h_got = step_one(h_send) if pair else h_send
    held = [h_send]
    if pair:
        o_stay, o_got, mid = step_two(o_keep, o_got, after=held)
        held = [mid]
    grad_middle, grad_branch, sums_two = norm_two_back(
        part, part_there, middle, gain_two, own, other, after=held
    )
    grad_packed, tab_grad, qkv_sums = attn_bwd(
        where, 0, packed, grad_branch, probs, w_qp, proj_other, tables
    )
    held = [grad_packed]
    if pair:
        h_stay, h_got, mid = step_two(h_keep, h_got, after=held)
        held = [mid, o_got]
    grad_packed, tab_grad_b, qkv_sums_b = attn_bwd(
        where, 1, packed, grad_branch, probs, w_qp, proj_other, tables,
        before=(grad_packed,), after=held,
    )
    q_keep, q_send = weight_grad_qp(where, normed, grad_packed, attended, grad_branch)
    held = [q_send]
    if pair:
        q_got = step_one(q_send)
        oh_keep, oh_got, mid = step_three([(o_stay, o_got), (h_stay, h_got)], after=held)
        held = [mid]
    back, back_low = product(
        "back", grad_packed, w_qp, pl.BlockSpec((D, QKV), lambda w: (0, 0)),
        lambda left, right: mm(left, right[...], ((1,), (1,))), after=held,
    )
    back_there = to_core(back_low)
    feed, feed_low = product(
        "feed", active, w_ho, None, lambda left, right: mm(left, output_part(right)),
        after=[back_low],
    )
    feed_there = to_core(feed_low)
    held = [feed_low]
    if pair:
        q_stay, q_got, mid = step_two(q_keep, q_got, after=held)
        oh_stay, oh_got, mid = step_four(oh_keep, oh_got, after=[mid])
        held = [mid]
    *parts, sums_one = last(
        where, ok, back, back_there, own, gain_one, grad_middle, middle, feed, feed_there,
        output_bias[None], after=held,
    )
    to_offset = jnp.pad(
        (near_offset.reshape(-1)[None, :] == jnp.arange(2 * WIN - 1)[:, None]).astype(F32),
        ((0, 32 - (2 * WIN - 1)), (0, TAB // 2 - WIN * WIN)),
    )
    ins = (sums_two, sums_one, hidden_sums, qkv_sums, qkv_sums_b, tab_grad, tab_grad_b, to_offset)
    small = call(
        small_kernel,
        "small",
        [(where, SMEM)] + [(v, None) for v in ins],
        [(array((32, D), F32), None)],
    )[0]
    small_got = to_core(small)
    held = [small]
    if pair:
        q_keep, q_got, mid = step_three([(q_stay, q_got)], after=held)
        held = [mid]
    *parts, mid = exchange(parts, after=held)
    small = tally(small, small_got, after=[mid])
    small_got = to_seq(small, 1)
    held = [small]
    if pair:
        q_stay, q_got, mid = step_four(q_keep, q_got, after=held)
        oh_total, oh_there, mid = step_five(oh_stay, oh_got, after=[mid])
        held = [mid]
    small = tally(small, small_got, after=held)
    small_got = to_seq(small, 2)
    input_grad, block_out = home(where, *parts, after=[small])
    held = [input_grad]
    if pair:
        q_total, q_there, mid = step_five(q_stay, q_got, after=held)
        held = [mid]
    small = tally(small, small_got, after=held)
    small_got = swap_z(small, 1)
    if pair:
        g_output, g_hidden, g_qkv, g_proj = finish(
            where, oh_total, oh_there, q_total, q_there, after=[small]
        )
        g_output = g_output.T
    else:
        g_output = larger_wide(o_keep, o_send).T
        g_hidden = larger_wide(h_keep, h_send)
        g_qkv, g_proj = larger_qp(q_keep, q_send)
    small = tally(small, small_got, after=[g_qkv])
    small_got = swap_z(small, 2)
    small = tally(small, small_got)
    if n_dp > 2:
        groups = [list(range(core, n_dp, 2)) for core in range(2)]
        small = lax.psum(small, "dp", axis_index_groups=groups)
    (
        d_qkv_bias, d_height, d_width, d_proj_bias, d_gain_two, d_bias_two, d_hidden_bias,
        d_output_bias, d_gain_one, d_bias_one,
    ) = unpack(small)
    return (
        block_out,
        input_grad,
        d_gain_one,
        d_bias_one,
        g_qkv,
        d_qkv_bias,
        d_height,
        d_width,
        g_proj,
        d_proj_bias,
        d_gain_two,
        d_bias_two,
        g_hidden,
        d_hidden_bias,
        g_output,
        d_output_bias,
    )


def solution(mesh):
    tokens = P("dp", "fsdp", "seq", None)
    rows = P("fsdp", None)
    every = P(("dp", "seq", "fsdp"), None)
    args = (tokens, P("fsdp"), P(), P(), rows, P(), P(), P(), rows)
    args += (P(), P(), P(), rows, P(), rows, P(), tokens)
    outs = (tokens, tokens, P(), P(), every, P(), P(), P(), every)
    outs += (P(), P(), P(), every, P(), P(None, ("dp", "seq", "fsdp")), P())
    return jax.shard_map(
        functools.partial(per_device, mesh.shape["dp"]),
        mesh=mesh,
        in_specs=args,
        out_specs=outs,
        check_vma=False,
    )
```

```python
import functools

import jax
import jax.numpy as jnp
from jax import lax
from jax.experimental import pallas as pl
from jax.experimental.pallas import tpu as pltpu
from jax.sharding import PartitionSpec as P

D = 768
HD = 64
FF = 3072
WIN = 14
GRID = 48
NWS = 4
TOK = 49
PAD = 56
ROWS = 4 * PAD
SPLIT = 4 * TOK
HALF = D // 2
QKV = 3 * HALF
WIDE = 4 * HALF
PIECE = 48
PAIRS = 3
LANES = 128
TAB = 512
NEG = -1e30
EPS = 1e-06
SCALE = HD**-0.5
BF = jnp.bfloat16
F32 = jnp.float32
ANY = pl.BlockSpec(memory_space=pl.ANY)
HBM = pl.BlockSpec(memory_space=pltpu.HBM)
SMEM = pl.BlockSpec(memory_space=pltpu.SMEM)


def mm(left, right, dims=((1,), (0,))):
    return lax.dot_general(left, right, (dims, ((), ())), preferred_element_type=F32)


def array(shape, dtype=BF):
    return jax.ShapeDtypeStruct(shape, dtype)


def whole(shape):
    return pl.BlockSpec(shape, lambda *at: (0,) * len(shape))


def window(shape, index=None):
    index = index or (lambda w: w)
    return pl.BlockSpec((1,) + shape, lambda w: (index(w),) + (0,) * len(shape))


TIMES = dict(cut=0.3, join=0.3, both_of=0.3, join_ho=0.3, pair_up=0.3, weld=0.3, norm_one=0.3, place_qp=0.3)


def call(kernel, name, ins, outs, grid=(), scratch=(), after=(), vmem=8, alias=()):
    count = len(ins)
    extra = len(after)

    def held(v):
        mode = pl.Buffered(1) if grid else None
        return pl.BlockSpec(v.shape, lambda *at: (0,) * len(v.shape), pipeline_mode=mode)

    def body(*refs):
        return kernel(*refs[:count], *refs[count + extra :])

    return pl.pallas_call(
        body,
        grid=grid,
        in_specs=[spec or held(v) for v, spec in ins] + [ANY] * extra,
        out_specs=[spec or whole(v.shape) for v, spec in outs],
        out_shape=[v for v, _ in outs],
        scratch_shapes=list(scratch),
        compiler_params=pltpu.CompilerParams(vmem_limit_bytes=vmem * 1024 * 1024),
        input_output_aliases=dict(alias),
        cost_estimate=pl.CostEstimate(
            flops=int(1.15e9 * TIMES.get(name, 87.0)),
            bytes_accessed=int(1.15e6 * TIMES.get(name, 87.0)),
            transcendentals=0,
        ),
        name=name,
    )(*[v for v, _ in ins], *after)


def pieces_kernel(where, qkv, proj, hidden, output, out, qp_out, sems):
    s, c = where[1], where[5]
    rows = pl.ds(pl.multiple_of(s * PIECE, PIECE), PIECE)
    start = pl.multiple_of(c * HALF + s * 2 * PIECE, 2 * PIECE)
    copies = [(output.at[pl.ds(start, 2 * PIECE)], out.at[: 2 * PIECE])]
    for i in range(4):
        cols = pl.ds(pl.multiple_of(i * D + c * HALF, LANES), HALF)
        at = (2 + i // 2) * PIECE
        half = slice(i % 2 * HALF, (i % 2 + 1) * HALF)
        copies.append((hidden.at[rows, cols], out.at[at : at + PIECE, half]))
    for i in range(3):
        cols = pl.ds(pl.multiple_of(i * D + c * HALF, LANES), HALF)
        copies.append((qkv.at[rows, cols], qp_out.at[:, i * HALF : (i + 1) * HALF]))
    cols = pl.ds(pl.multiple_of(c * HALF, LANES), HALF)
    copies.append((proj.at[rows, cols], qp_out.at[:, QKV:]))
    run_copies(copies, sems)


def run_copies(pairs, sems):
    copies = [
        pltpu.make_async_copy(src, dst, sems.at[n]) for n, (src, dst) in enumerate(pairs)
    ]
    for copy in copies:
        copy.start()
    for copy in copies:
        copy.wait()


def pieces(where, qkv, proj, hidden, output):
    return call(
        pieces_kernel,
        "pieces",
        [(where, SMEM), (qkv, HBM), (proj, HBM), (hidden, HBM), (output, HBM)],
        [(array((4 * PIECE, D)), None), (array((PIECE, WIDE)), None)],
        scratch=[pltpu.SemaphoreType.DMA((9,))],
        vmem=60,
    )


def output_part(w, first=0, count=16):
    return w[first : first + count, : 2 * PIECE, :].reshape(count * 2 * PIECE, D)


def hidden_part(w, half):
    at = (2 + half) * PIECE
    return w[:, at : at + PIECE, :].reshape(D, D)


def join_kernel(one, two, three, out):
    out[0] = one[...]
    out[1] = two[...]
    out[2] = three[...]


def join(parts, after=()):
    return call(
        join_kernel,
        "join",
        [(part, None) for part in parts],
        [(array((3,) + parts[0].shape), None)],
        after=after,
    )[0]


def both_kernel(one, two, out):
    out[0] = one[...]
    out[1] = two[...]


def both_of(one, two, after=()):
    return call(
        both_kernel,
        "both_of",
        [(one, None), (two, None)],
        [(array((2,) + one.shape), None)],
        after=after,
    )[0]


def join_ho_kernel(one, two, out):
    out[0] = one[...]
    out[1] = two[0]
    out[2] = two[1]


def join_ho(one, two, after=()):
    return call(
        join_ho_kernel,
        "join_ho",
        [(one, None), (two, None)],
        [(array((3,) + one.shape), None)],
        after=after,
    )[0]


def place_qp_kernel(where, qkv, proj, first, second, third, fourth, out, send, sems):
    z, c = where[0], where[5]
    copies = []

    def add(src, dst):
        copies.append(pltpu.make_async_copy(src, dst, sems.at[len(copies)]))

    for i in range(3):
        for q in range(4):
            cols = pl.ds(pl.multiple_of(i * D + c * HALF, LANES), HALF)
            add(
                qkv.at[q * PIECE : (q + 1) * PIECE, cols],
                out.at[z, q, :, i * HALF : (i + 1) * HALF],
            )
    for q in range(4):
        cols = pl.ds(pl.multiple_of(c * HALF, LANES), HALF)
        add(proj.at[q * PIECE : (q + 1) * PIECE, cols], out.at[z, q, :, QKV:])
    for i in range(3):
        zz = lax.rem(z + 3 - i, 4)
        for n, src in enumerate((first, second, third, fourth)):
            add(src.at[i], out.at[zz, where[1 + n]])
    for copy in copies:
        copy.start()
    for copy in copies:
        copy.wait()
    send[...] = out[pl.ds(2 * (1 - c), 2), :, :, QKV:]


def place_ho_kernel(where, hidden, output, first, second, third, fourth, out, sems):
    z, c = where[0], where[5]
    copies = []
    for q in range(4):
        start = pl.multiple_of(c * HALF + q * 2 * PIECE, 2 * PIECE)
        copies.append((output.at[pl.ds(start, 2 * PIECE)], out.at[z, q, : 2 * PIECE]))
        for i in range(4):
            cols = pl.ds(pl.multiple_of(i * D + c * HALF, LANES), HALF)
            at = (2 + i // 2) * PIECE
            half = slice(i % 2 * HALF, (i % 2 + 1) * HALF)
            copies.append(
                (
                    hidden.at[q * PIECE : (q + 1) * PIECE, cols],
                    out.at[z, q, at : at + PIECE, half],
                )
            )
    for i in range(3):
        zz = z ^ (i + 1)
        for n, src in enumerate((first, second, third, fourth)):
            copies.append((src.at[i], out.at[zz, where[1 + n]]))
    run_copies(copies, sems)


def hand_out(c, rows, i, outs):
    near, both, far = outs

    def piece(k):
        return rows[pl.ds(pl.multiple_of(k * PAD, 8), PAD), :].astype(BF)

    near[i] = piece(0)
    both[0, i] = piece(1 + c)
    both[1, i] = piece(3)
    far[i] = piece(2 - c)


def handed(images):
    shape = (images, PAD, D)
    return [(array(shape), None), (array((2,) + shape), None), (array(shape), None)]


ROWS_F32 = pltpu.VMEM((ROWS, D), F32)


def gathered_rows(c, near, one, two, i):
    first, second = one[0, i].astype(F32), two[0, i].astype(F32)
    parts = [near[i].astype(F32)]
    parts += [jnp.where(c == 0, first, second), jnp.where(c == 0, second, first)]
    return jnp.concatenate(parts + [two[1, i].astype(F32)])


def pair_kernel(far, one, out):
    out[0] = far[...]
    out[1] = one[1]


def pair_up(far, one, after=()):
    return call(
        pair_kernel,
        "pair_up",
        [(far, None), (one, None)],
        [(array((2,) + far.shape), None)],
        after=after,
    )[0]


def cut_kernel(where, tokens, cotangent, *rest):
    s, c = where[1], where[5]
    images = tokens.shape[0]
    outs, rows = rest[:3], rest[3]
    row = lax.broadcasted_iota(jnp.int32, (ROWS, SPLIT), 0)
    col = lax.broadcasted_iota(jnp.int32, (ROWS, SPLIT), 1)
    token = row % PAD
    take = ((token < TOK) & (col == token * 4 + (s ^ (row // PAD)))).astype(F32).astype(BF)
    for i in range(2 * images):
        rows[...] = mm(take, tokens[i] if i < images else cotangent[i - images])
        hand_out(c, rows, i, outs)


def cut(where, tokens, cotangent, after=()):
    images = tokens.shape[0]
    flat = [jnp.transpose(v, (0, 2, 1, 3)).reshape(images, SPLIT, D) for v in (tokens, cotangent)]
    return call(
        cut_kernel,
        "cut",
        [(where, SMEM)] + [(v, None) for v in flat],
        handed(2 * images),
        scratch=[ROWS_F32],
        after=after,
        vmem=12,
    )


def weld_kernel(where, ok, near, one, two, out):
    count = out.shape[0]
    for i in range(count):
        rows = gathered_rows(where[5], near, one, two, i)
        out[i] = (rows if i < count // 2 else rows * ok[...]).astype(BF)


def weld(where, ok, near, one, two, after=()):
    return call(
        weld_kernel,
        "weld",
        [(where, SMEM), (ok, None)] + [(part, None) for part in (near, one, two)],
        [(array((near.shape[0], ROWS, D)), None)],
        after=after,
    )[0]


def home_kernel(where, near, one, two, *outs):
    s = where[1]
    row = lax.broadcasted_iota(jnp.int32, (SPLIT, ROWS), 0)
    col = lax.broadcasted_iota(jnp.int32, (SPLIT, ROWS), 1)
    token = col % PAD
    take = ((token < TOK) & (row == token * 4 + (s ^ (col // PAD)))).astype(F32).astype(BF)
    images = outs[0].shape[0]
    for i in range(2 * images):
        rows = gathered_rows(where[5], near, one, two, i).astype(BF)
        outs[i // images][i % images] = mm(take, rows).astype(BF)


def home(where, near, one, two, after=()):
    images = near.shape[0] // 2
    flat = call(
        home_kernel,
        "home",
        [(where, SMEM)] + [(part, None) for part in (near, one, two)],
        [(array((images, SPLIT, D)), None)] * 2,
        after=after,
        vmem=12,
    )
    return [jnp.transpose(v.reshape(images, TOK, 4, D), (0, 2, 1, 3)) for v in flat]


def unit_of(v):
    v = v - jnp.mean(v, axis=-1, keepdims=True)
    rstd = lax.rsqrt(jnp.mean(v * v, axis=-1, keepdims=True) + EPS)
    return v * rstd, rstd


def norm_back(grad, unit, rstd):
    return rstd * (
        grad
        - jnp.mean(grad, axis=-1, keepdims=True)
        - unit * jnp.mean(grad * unit, axis=-1, keepdims=True)
    )


def norm_one_kernel(ok, own, other, gain, shift, out):
    images = own.shape[0] // 2
    for w in range(2 * images):
        x = own[w] if w < images else other[w - images]
        unit, _ = unit_of(x.astype(F32))
        out[w] = ((unit * gain[...] + shift[...]) * ok[...]).astype(BF)


def norm_one(ok, own, other, gain, shift, after=()):
    return call(
        norm_one_kernel,
        "norm_one",
        [(v, None) for v in (ok, own, other, gain, shift)],
        [(array(own.shape), None)],
        after=after,
        vmem=12,
    )[0]


def norm_two_kernel(
    own, other, branch, branch_other, there, bias, gain, shift, middle, second
):
    images = own.shape[0] // 2
    for w in range(2 * images):
        x, mine = (own, branch) if w < images else (other, branch_other)
        at = w % images
        value = x[at].astype(F32) + (mine[at] + there[w].astype(F32)) + bias[...]
        middle[w] = value
        unit, _ = unit_of(value)
        second[w] = (unit * gain[...] + shift[...]).astype(BF)


def norm_two(own, other, branch, branch_other, there, bias, gain, shift, after=()):
    shape = own.shape
    ins = (own, other, branch, branch_other, there, bias, gain, shift)
    return call(
        norm_two_kernel,
        "norm_two",
        [(v, None) for v in ins],
        [(array(shape, F32), None), (array(shape), None)],
        after=after,
        vmem=14,
    )


def norm_two_back_kernel(
    images, part, there, middle, gain, feed, feed_other, grad_middle, grad_branch, sums
):
    sums[...] = jnp.zeros_like(sums)
    for w in range(2 * images):
        grad = part[w] + there[w].astype(F32)
        unit, rstd = unit_of(middle[w])
        feed_w = (feed[images + w] if w < images else feed_other[w]).astype(F32)
        total = feed_w + norm_back(grad * gain[...], unit, rstd)
        low = total.astype(BF)
        grad_branch[w] = low
        if w < images:
            grad_middle[w] = total
            sums[0:1] += jnp.sum(grad * unit, axis=0, keepdims=True)
            sums[1:2] += jnp.sum(grad, axis=0, keepdims=True)
            sums[2:3] += jnp.sum(low.astype(F32), axis=0, keepdims=True)
            sums[3:4] += jnp.sum(feed_w, axis=0, keepdims=True)


def norm_two_back(part, there, middle, gain, feed, feed_other, after=()):
    count = part.shape[0]
    return call(
        functools.partial(norm_two_back_kernel, count // 2),
        "norm_two_back",
        [(v, None) for v in (part, there, middle, gain, feed, feed_other)],
        [
            (array((count // 2, ROWS, D), F32), None),
            (array((count, ROWS, D)), None),
            (array((8, D), F32), None),
        ],
        after=after,
        vmem=16,
    )


def last_kernel(
    where, ok, back, back_there, own, gain, grad_middle, middle, feed, feed_there, bias, *rest
):
    outs, sums, rows = rest[:3], rest[3], rest[4]
    images = back.shape[0]
    sums[...] = jnp.zeros_like(sums)
    for w in range(images):
        grad = (back[w] + back_there[w].astype(F32)) * ok[...]
        unit, rstd = unit_of(own[w].astype(F32))
        sums[0:1] += jnp.sum(grad * unit, axis=0, keepdims=True)
        sums[1:2] += jnp.sum(grad, axis=0, keepdims=True)
        rows[...] = grad_middle[w] + norm_back(grad * gain[...], unit, rstd)
        hand_out(where[5], rows, w, outs)
        rows[...] = (middle[w] + feed[w] + feed_there[w].astype(F32) + bias[...]) * ok[...]
        hand_out(where[5], rows, images + w, outs)


def last(where, ok, back, back_there, own, gain, grad_middle, middle, feed, feed_there, bias, after=()):
    ins = (ok, back, back_there, own, gain, grad_middle, middle, feed, feed_there, bias)
    return call(
        last_kernel,
        "last",
        [(where, SMEM)] + [(v, None) for v in ins],
        handed(own.shape[0]) + [(array((8, D), F32), None)],
        scratch=[ROWS_F32],
        after=after,
        vmem=20,
    )


def attn_fwd_kernel(
    where, normed, w_qp, other, b_qkv, table, spot, fold, keys, bias, *rest
):
    packed, out, probs, low, branch = rest[-5:]
    c = where[5]
    lane = lax.broadcasted_iota(jnp.int32, (ROWS, LANES), 1)
    shift = [b_qkv[:, pl.ds(pl.multiple_of(i * D + c * HALF, LANES), HALF)] for i in range(3)]
    packed[0] = (mm(normed[0], w_qp[:, :QKV]) + jnp.concatenate(shift, axis=1)).astype(BF)

    def columns(part, pair):
        at = part * HALF + pair * LANES
        return packed[0, :, at : at + LANES]

    queries = jnp.concatenate([columns(0, pair) for pair in range(PAIRS)])
    mask = jnp.concatenate([spot[...]] * PAIRS)
    rels = [mm((mm(queries, table[e]) * mask).astype(BF), fold[...]).astype(BF) for e in range(2)]
    for pair in range(PAIRS):
        q, k, v = columns(0, pair), columns(1, pair), columns(2, pair)
        right = jnp.concatenate([k, keys[...]], axis=1)
        parts = []
        for e in range(2):
            mine = (lane < HD) if e == 0 else (lane >= HD)
            rel = rels[e][pair * ROWS : (pair + 1) * ROWS]
            scaled = jnp.where(mine, q.astype(F32) * SCALE, 0.0).astype(BF)
            left = jnp.concatenate([scaled, rel], axis=1)
            s = mm(left, right, ((1,), (1,))) + bias[...]
            p = jnp.exp(s - jnp.max(s, axis=1, keepdims=True))
            p = (p * (1.0 / jnp.sum(p, axis=1, keepdims=True))).astype(BF)
            probs[0, 2 * pair + e] = p
            parts.append(mm(p, v))
        out[0, :, pair * LANES : (pair + 1) * LANES] = jnp.where(
            lane < HD, parts[0], parts[1]
        ).astype(BF)
    att = out[0]
    own_cols = pl.ds(pl.multiple_of(c * HALF, LANES), HALF)
    other_cols = pl.ds(pl.multiple_of((1 - c) * HALF, LANES), HALF)
    own_rows = pl.ds(pl.multiple_of(c * HALF, HALF), HALF)
    mine = mm(att, w_qp[own_rows, QKV:])
    theirs = mm(att, other[...])
    branch[0, :, own_cols] = mine
    branch[0, :, other_cols] = theirs
    low[0, :, own_cols] = mine.astype(BF)
    low[0, :, other_cols] = theirs.astype(BF)


def attn_fwd(where, group, normed, w_qp, other, b_qkv, tables, before=(), after=()):
    table, spot, fold, keys, bias = tables
    count = normed.shape[0]
    half = count // 2
    start = group * half
    ins = [(where, SMEM), (normed, window((ROWS, D), lambda w: w + start))]
    ins += [(v, None) for v in (w_qp, other, b_qkv, table, spot, fold, keys, bias)]
    kept = ((ROWS, QKV), (ROWS, HALF), (2 * PAIRS, ROWS, ROWS))
    outs = [(array((count,) + shape), window(shape, lambda w: w + start)) for shape in kept]
    outs += [
        (array((count, ROWS, D)), window((ROWS, D), lambda w: (w + start + half) % count)),
        (array((half, ROWS, D), F32), window((ROWS, D))),
    ]
    return call(
        attn_fwd_kernel,
        "attn_fwd",
        ins + [(v, ANY) for v in before],
        outs,
        grid=(half,),
        after=after,
        alias=[(len(ins) + n, n) for n in range(len(before))],
        vmem=18,
    )


def attn_bwd_kernel(
    where, packed, grad_branch, probs, w_qp, other, table, spot, fold, keys, *rest
):
    out, tab_grad, sums, att = rest[-4:]
    c = where[5]
    lane = lax.broadcasted_iota(jnp.int32, (ROWS, LANES), 1)
    lane_t = lax.broadcasted_iota(jnp.int32, (TAB, LANES), 1)

    @pl.when(pl.program_id(0) == 0)
    def _():
        tab_grad[...] = jnp.zeros_like(tab_grad)
        sums[...] = jnp.zeros_like(sums)

    own_cols = pl.ds(pl.multiple_of(c * HALF, LANES), HALF)
    other_cols = pl.ds(pl.multiple_of((1 - c) * HALF, LANES), HALF)
    own_rows = pl.ds(pl.multiple_of(c * HALF, HALF), HALF)
    att[...] = (
        mm(grad_branch[0, :, own_cols], w_qp[own_rows, QKV:], ((1,), (1,)))
        + mm(grad_branch[0, :, other_cols], other[...], ((1,), (1,)))
    ).astype(BF)
    def columns(part, pair):
        at = part * HALF + pair * LANES
        return packed[0, :, at : at + LANES]

    queries = jnp.concatenate([columns(0, pair) for pair in range(PAIRS)])
    mask = jnp.concatenate([spot[...]] * PAIRS)
    both, dk, dv = [[], []], [[], []], [[], []]
    for pair in range(PAIRS):
        q, k, v = columns(0, pair), columns(1, pair), columns(2, pair)
        go = att[:, pair * LANES : (pair + 1) * LANES]
        right = jnp.concatenate([k, keys[...]], axis=1)
        for e in range(2):
            mine = (lane < HD) if e == 0 else (lane >= HD)
            go_e = jnp.where(mine, go.astype(F32), 0.0).astype(BF)
            p_low = probs[0, 2 * pair + e]
            p = p_low.astype(F32)
            dp = mm(go_e, v, ((1,), (1,)))
            ds = (p * (dp - jnp.sum(dp * p, axis=1, keepdims=True))).astype(BF)
            both[e].append(mm(ds, right))
            dk[e].append(SCALE * mm(ds, q, ((0,), (0,))))
            dv[e].append(mm(p_low, go, ((0,), (0,))))
    dq, dt = [], []
    for e in range(2):
        rel = jnp.concatenate([part[:, LANES:] for part in both[e]]).astype(BF)
        spread = (mm(rel, fold[...], ((1,), (1,))) * mask).astype(BF)
        flat = jnp.concatenate([part[:, :LANES] for part in both[e]])
        dq.append(SCALE * flat + mm(spread, table[e], ((1,), (1,))))
        dt.append(mm(spread, queries, ((0,), (0,))))
    tab_grad[...] += jnp.where(lane_t < HD, dt[0], dt[1])
    for pair in range(PAIRS):
        rows = slice(pair * ROWS, (pair + 1) * ROWS)
        pairs = ((dq[0][rows], dq[1][rows]), (dk[0][pair], dk[1][pair]), (dv[0][pair], dv[1][pair]))
        for part, two in enumerate(pairs):
            low = jnp.where(lane < HD, two[0], two[1]).astype(BF)
            cols = slice(part * HALF + pair * LANES, part * HALF + (pair + 1) * LANES)
            out[0, :, cols] = low
            sums[0:1, cols] += jnp.sum(low.astype(F32), axis=0, keepdims=True)


def attn_bwd(where, group, packed, grad_branch, probs, w_qp, other, tables, before=(), after=()):
    table, spot, fold, keys, _ = tables
    count = packed.shape[0]
    half = count // 2
    start = group * half
    ins = [
        (where, SMEM),
        (packed, window((ROWS, QKV), lambda w: w + start)),
        (grad_branch, window((ROWS, D), lambda w: w + start)),
        (probs, window((2 * PAIRS, ROWS, ROWS), lambda w: w + start)),
    ]
    ins += [(v, None) for v in (w_qp, other, table, spot, fold, keys)]
    return call(
        attn_bwd_kernel,
        "attn_bwd",
        ins + [(v, ANY) for v in before],
        [
            (array((count, ROWS, QKV)), window((ROWS, QKV), lambda w: w + start)),
            (array((TAB, LANES), F32), None),
            (array((8, QKV), F32), None),
        ],
        grid=(half,),
        scratch=[pltpu.VMEM((ROWS, HALF), BF)],
        after=after,
        alias=[(len(ins) + n, n) for n in range(len(before))],
        vmem=18,
    )


def hidden_kernel(where, second, w, bias, active, slope):
    c = where[5]
    for half in range(2):
        cols = slice(half * D, (half + 1) * D)
        shift = [
            bias[:, pl.ds(pl.multiple_of(i * D + c * HALF, LANES), HALF)]
            for i in (2 * half, 2 * half + 1)
        ]
        v = mm(second[0], hidden_part(w, half)) + jnp.concatenate(shift, axis=1)
        phi = 0.5 * (1.0 + lax.erf(v * (0.5**0.5)))
        active[0, :, cols] = (v * phi).astype(BF)
        slope[0, :, cols] = (phi + v * (jnp.exp(-0.5 * v * v) * 0.3989422804014327)).astype(BF)


def hidden_layer(where, second, w_hidden, bias, after=()):
    count = second.shape[0]
    return call(
        hidden_kernel,
        "hidden",
        [(where, SMEM), (second, window((ROWS, D))), (w_hidden, None), (bias, None)],
        [(array((count, ROWS, WIDE)), window((ROWS, WIDE)))] * 2,
        grid=(count,),
        after=after,
        vmem=14,
    )


def product_kernel(of, count, left, right, own, low):
    w = pl.program_id(0)
    value = of(left[0], right)

    @pl.when(w < count // 2)
    def _():
        low[w] = value.astype(BF)

    @pl.when(w >= count // 2)
    def _():
        own[w - count // 2] = value


def product(name, left, right, right_spec, of, after=()):
    count = left.shape[0]
    shape = (count // 2, ROWS, D)
    return call(
        functools.partial(product_kernel, of, count),
        name,
        [(left, window(left.shape[1:], lambda w: (w + count // 2) % count)), (right, right_spec)],
        [(array(shape, F32), None), (array(shape), None)],
        grid=(count,),
        after=after,
        vmem=14,
    )


def grad_pre_kernel(count, own, other, slope, w, out, part, low, sums):
    feed = jnp.where(pl.program_id(0) < count // 2, own[0].astype(F32), other[0].astype(F32))
    feed = feed.astype(BF)

    @pl.when(pl.program_id(0) == 0)
    def _():
        sums[...] = jnp.zeros_like(sums)

    for half in range(2):
        cols = slice(half * D, (half + 1) * D)
        value = mm(feed, output_part(w, 8 * half, 8), ((1,), (1,))) * slope[0, :, cols].astype(F32)
        value = value.astype(BF)
        out[0, :, cols] = value
        sums[0:1, cols] += jnp.sum(value.astype(F32), axis=0, keepdims=True)
    value = mm(out[0, :, :D], hidden_part(w, 0), ((1,), (1,)))
    value = value + mm(out[0, :, D:], hidden_part(w, 1), ((1,), (1,)))
    part[0] = value
    low[0] = value.astype(BF)


def grad_pre_of(own, other, slope, w, after=()):
    count = slope.shape[0]
    half = count // 2
    return call(
        functools.partial(grad_pre_kernel, count),
        "grad_pre",
        [
            (own, window((ROWS, D), lambda w: half + jnp.minimum(w, half - 1))),
            (other, window((ROWS, D), lambda w: half + jnp.maximum(w - half, 0))),
            (slope, window((ROWS, WIDE))),
            (w, None),
        ],
        [
            (array((count, ROWS, WIDE)), window((ROWS, WIDE))),
            (array((count, ROWS, D), F32), window((ROWS, D))),
            (array((count, ROWS, D)), window((ROWS, D), lambda w: (w + count // 2) % count)),
            (array((8, WIDE), F32), None),
        ],
        grid=(count,),
        after=after,
        vmem=18,
    )


def deal(where, total, keep, send, cols):
    for n, out in enumerate((keep, keep, send, send)):
        q = where[(1, 3, 2, 4)[n]]
        for h in range(2):
            rows = pl.ds(pl.multiple_of(h * HALF + q * 96, 8), 96)
            out[n % 2, h, :, cols] = total[rows, :].astype(BF)


def weight_grad_kernel(count, where, *refs):
    lefts, (right, keep, send, flip, total) = refs[:count], refs[count:]
    rows = right.shape[0] // count
    for n, left in enumerate(lefts):
        flip[:, n * rows : (n + 1) * rows] = left[left.shape[0] - rows :, :].T
    for at in range(0, WIDE, TAB):
        cols = slice(at, at + TAB)
        total[...] = mm(flip[...], right[:, cols])
        deal(where, total, keep, send, cols)


def weight_grad(where, lefts, right, after=()):
    rows = right.shape[0] * right.shape[1]
    shape = (2, 2, 96, WIDE)
    return call(
        functools.partial(weight_grad_kernel, len(lefts)),
        "weight_grad",
        [(where, SMEM)]
        + [(left.reshape(-1, D), None) for left in lefts]
        + [(right.reshape(rows, WIDE), None)],
        [(array(shape), None), (array(shape), None)],
        scratch=[pltpu.VMEM((D, rows), BF), pltpu.VMEM((D, TAB), F32)],
        after=after,
        vmem=16,
    )


def weight_grad_qp_kernel(
    where, normed, packed, att, branch, keep, send, flip, total, flip_att, total_att
):
    flip[...] = normed[...].T
    for at in range(0, QKV, HALF):
        cols = slice(at, at + HALF)
        total[...] = mm(flip[...], packed[:, cols])
        deal(where, total, keep, send, cols)
    flip_att[...] = att[...].T
    total_att[...] = mm(flip_att[...], branch[...])
    for n, out in enumerate((keep, keep, send, send)):
        q = where[(1, 3, 2, 4)[n]]
        rows = pl.ds(pl.multiple_of(q * 96, 8), 96)
        for h in range(2):
            out[n % 2, h, :, QKV:] = total_att[rows, h * HALF : (h + 1) * HALF].astype(BF)


def weight_grad_qp(where, normed, packed, att, branch, after=()):
    rows = normed.shape[0] * normed.shape[1]
    shape = (2, 2, 96, WIDE)
    return call(
        weight_grad_qp_kernel,
        "weight_grad_qp",
        [(where, SMEM)]
        + [(v.reshape(rows, v.shape[-1]), None) for v in (normed, packed, att, branch)],
        [(array(shape), None), (array(shape), None)],
        scratch=[
            pltpu.VMEM((D, rows), BF),
            pltpu.VMEM((D, HALF), F32),
            pltpu.VMEM((HALF, rows), BF),
            pltpu.VMEM((HALF, D), F32),
        ],
        after=after,
        vmem=16,
    )


def add_one_kernel(*refs):
    stay, send = refs[-2:]
    for i in range(len(refs) // 2 - 1):
        keep, got = refs[2 * i], refs[2 * i + 1]
        for h in range(2):
            for q in range(4):
                rows = slice(q * 24, (q + 1) * 24)
                stay[i, h, q] = keep[0, h, rows].astype(F32) + got[0, h, rows].astype(F32)
                total = keep[1, h, rows].astype(F32) + got[1, h, rows].astype(F32)
                send[i, h, q] = total.astype(BF)


def add_one(parts, after=()):
    shape = (len(parts), 2, 4, 24, WIDE)
    return call(
        add_one_kernel,
        "add_one",
        [(v, None) for part in parts for v in part],
        [(array(shape, F32), None), (array(shape), None)],
        after=after,
        vmem=16,
    )


def add_two_kernel(where, stay, got, keep, send):
    z = where[0]
    for i in range(stay.shape[0]):
        for n in range(2):
            mine, theirs = z ^ (2 * n), z ^ (2 * n + 1)
            for h in range(2):
                keep[n, i, h] = stay[i, h, mine] + got[i, h, mine].astype(F32)
                send[n, i, h] = (stay[i, h, theirs] + got[i, h, theirs].astype(F32)).astype(BF)


def add_two(where, stay, got, after=()):
    shape = (2, stay.shape[0], 2, 24, WIDE)
    return call(
        add_two_kernel,
        "add_two",
        [(where, SMEM), (stay, None), (got, None)],
        [(array(shape, F32), None), (array(shape), None)],
        after=after,
        vmem=14,
    )


def add_three_kernel(keep, got, stay, send):
    for i in range(stay.shape[0]):
        for h in range(2):
            stay[i, h] = keep[0, i, h] + got[0, i, h].astype(F32)
            send[i, h] = (keep[1, i, h] + got[1, i, h].astype(F32)).astype(BF)


def add_three(keep, got, after=()):
    shape = keep.shape[1:]
    return call(
        add_three_kernel,
        "add_three",
        [(keep, None), (got, None)],
        [(array(shape, F32), None), (array(shape), None)],
        after=after,
    )


def add_four_kernel(where, stay, got, total, send):
    for i in range(stay.shape[0]):
        for h in range(2):
            total[i, h] = stay[i, h] + got[i, h].astype(F32)
        send[i] = total[i, 1 - where[5]]


def add_four(where, stay, got, after=()):
    shape = (stay.shape[0],) + stay.shape[2:]
    return call(
        add_four_kernel,
        "add_four",
        [(where, SMEM), (stay, None), (got, None)],
        [(array(stay.shape, F32), None), (array(shape, F32), None)],
        after=after,
    )


def finish_kernel(where, two, two_there, total, there, output, hidden, qkv, proj):
    c = where[5]

    def lay(out, blocks, mine, theirs):
        for i in range(blocks):
            cols = slice(i * HALF, (i + 1) * HALF)
            out[:, pl.ds(pl.multiple_of(i * D + c * HALF, LANES), HALF)] = mine[:, cols]
            out[:, pl.ds(pl.multiple_of(i * D + (1 - c) * HALF, LANES), HALF)] = theirs[:, cols]

    lay(output, 4, two.at[0, c], two_there.at[0])
    lay(hidden, 4, two.at[1, c], two_there.at[1])
    lay(qkv, 3, total.at[0, c], there.at[0])
    for h in range(2):
        proj[:, h * HALF : (h + 1) * HALF] = total[0, h, :, QKV:]


def finish(where, two, two_there, total, there, after=()):
    return call(
        finish_kernel,
        "finish",
        [(where, SMEM)] + [(v, None) for v in (two, two_there, total, there)],
        [(array((24, blocks * D), F32), None) for blocks in (4, 4, 3, 1)],
        after=after,
    )


def small_kernel(where, two, one, hidden, qkv, qkv_b, tab, tab_b, to_offset, out):
    c = where[5]
    out[...] = jnp.zeros_like(out)
    cols = pl.ds(pl.multiple_of(c * HALF, LANES), HALF)
    for i in range(3):
        part = slice(i * HALF, (i + 1) * HALF)
        out[i : i + 1, cols] = qkv[0:1, part] + qkv_b[0:1, part]
    for i in range(4):
        out[3 + i : 4 + i, cols] = hidden[0:1, i * HALF : (i + 1) * HALF]
    for i in range(4):
        out[7 + i : 8 + i, :] = two[i : i + 1, :]
    for i in range(2):
        out[11 + i : 12 + i, :] = one[i : i + 1, :]
        half = slice(i * (TAB // 2), (i + 1) * (TAB // 2))
        rel = lax.dot_general(
            to_offset[...],
            tab[half, :] + tab_b[half, :],
            (((1,), (0,)), ((), ())),
            preferred_element_type=F32,
            precision=lax.Precision.HIGHEST,
        )
        for k in range(4):
            out[16 + 8 * i : 24 + 8 * i, k * LANES : (k + 1) * LANES] = rel[8 * k : 8 * k + 8]


def tally_kernel(*refs):
    if len(refs) == 3:
        refs[2][...] = refs[0][...] + refs[1][...]
    else:
        refs[4][...] = (refs[0][...] + refs[1][...]) + (refs[2][...] + refs[3][...])


def tally(parts, after=()):
    return call(
        tally_kernel,
        "tally",
        [(v, None) for v in parts],
        [(array(parts[0].shape, F32), None)],
        after=after,
    )[0]


def unpack_kernel(total, *outs):
    qkv, height, width, proj, gain_two, bias_two, hidden, output, gain_one, bias_one = outs
    for i in range(3):
        qkv[i * D : (i + 1) * D] = total[i, :]
    for i in range(4):
        hidden[i * D : (i + 1) * D] = total[3 + i, :]
    rows = (gain_two, bias_two, proj, output, gain_one, bias_one)
    for i, out in enumerate(rows):
        out[...] = total[7 + i, :]
    for i, out in enumerate((height, width)):
        at = slice(16 + 8 * i, 24 + 8 * i)
        rel = jnp.concatenate([total[at, k * LANES : (k + 1) * LANES] for k in range(4)])
        out[...] = (rel + pltpu.roll(rel, HD, 1))[: 2 * WIN - 1, :HD]


def unpack(total):
    rel = (2 * WIN - 1, HD)
    shapes = [(2 * QKV,), rel, rel] + [(D,)] * 3 + [(FF,)] + [(D,)] * 3
    return call(
        unpack_kernel, "unpack", [(total, None)], [(array(shape, F32), None) for shape in shapes]
    )


def per_device(
    n_dp,
    image_tokens,
    slot_window,
    first_gain,
    first_bias,
    qkv_weight,
    qkv_bias,
    rel_height,
    rel_width,
    proj_weight,
    proj_bias,
    second_gain,
    second_bias,
    hidden_weight,
    hidden_bias,
    output_weight,
    output_bias,
    cotangent,
):
    images = image_tokens.shape[0]
    count = 2 * images
    c = lax.axis_index("dp") % 2
    s = lax.axis_index("seq")
    z = lax.axis_index("fsdp")
    a = jnp.where(c == 0, s ^ 1, s ^ 2)
    b = jnp.where(c == 0, s ^ 2, s ^ 1)
    where = jnp.stack([z, s, a, b, s ^ 3, c]).astype(jnp.int32)

    def plane_perm(step):
        out = []
        for i in range(n_dp):
            hop = (1, 2)[(i + step) % 2]
            out += [(i * 4 + j, i * 4 + (j ^ hop)) for j in range(4)]
        return out

    plane_one, plane_two = plane_perm(0), plane_perm(1)

    def to_core(v):
        return lax.ppermute(v, "dp", [(i, i ^ 1) for i in range(n_dp)])

    def to_seq(v, k):
        return lax.ppermute(v, "seq", [(i, i ^ k) for i in range(4)])

    def to_z(v, k):
        return lax.ppermute(v, "fsdp", [(i, (i + k) % 4) for i in range(4)])

    def swap_z(v, hop):
        return lax.ppermute(v, "fsdp", [(i, i ^ hop) for i in range(4)])

    def to_plane(v, perm):
        return lax.ppermute(v, ("dp", "seq"), perm)

    def pick(v, index, axis=0):
        return lax.dynamic_index_in_dim(v, index, axis, keepdims=False)

    row = jnp.arange(ROWS)
    token = (s ^ (row // PAD)) * TOK + row % PAD
    real = row % PAD < TOK
    t_r, t_c = token // WIN, token % WIN
    slot = pick(slot_window, s)
    ok = (
        real
        & (slot >= 0)
        & (slot // NWS * WIN + t_r < GRID)
        & (slot % NWS * WIN + t_c < GRID)
    ).astype(F32)[:, None]
    ones = jnp.ones((ROWS, 1), F32)
    near_offset = jnp.arange(WIN)[:, None] - jnp.arange(WIN)[None, :] + WIN - 1
    height = rel_height[near_offset].reshape(WIN * WIN, HD).T
    width = rel_width[near_offset].reshape(WIN * WIN, HD).T
    gap = jnp.zeros((HD, TAB // 2 - WIN * WIN), BF)
    flat = jnp.concatenate([height, gap, width, gap], axis=1)
    blank = jnp.zeros_like(flat)
    table = jnp.stack([jnp.concatenate([flat, blank]), jnp.concatenate([blank, flat])])
    col = jnp.arange(TAB)
    in_half = col % (TAB // 2)
    col_from = jnp.where(in_half < WIN * WIN, in_half // WIN, -1)
    spot = (
        jnp.where(col[None, :] < TAB // 2, t_r[:, None], t_c[:, None]) == col_from[None, :]
    ).astype(F32)
    col_to = jnp.where(in_half < WIN * WIN, in_half % WIN + WIN * (col // (TAB // 2)), -1)
    fold = (col_to[:, None] == jnp.arange(LANES)[None, :]).astype(BF)
    lanes = jnp.arange(LANES)[None, :]
    keys = (
        real[:, None] & ((lanes == t_r[:, None]) | (lanes == WIN + t_c[:, None]))
    ).astype(BF)
    key_bias = jnp.where(real, 0.0, NEG).astype(F32)[None, :]
    tables = (table, spot, fold, keys, key_bias)
    gain_one, bias_one = first_gain[None], first_bias[None]
    gain_two, bias_two = second_gain[None], second_bias[None]

    def along_z(piece):
        return [to_z(piece, k) for k in (1, 2, 3)]

    def in_plane(first):
        second = to_plane(first, plane_one)
        third = to_plane(first, plane_two)
        fourth = to_plane(second, plane_two)
        return first, second, third, fourth

    def exchange(parts, after=()):
        near, both, far = parts
        one = to_plane(both, plane_one)
        send = pair_up(far, one, after)
        return near, one, to_plane(send, plane_two), send

    ho_piece, qp_piece = pieces(where, qkv_weight, proj_weight, hidden_weight, output_weight)
    z_qp = along_z(qp_piece)
    tokens_cut = cut(where, image_tokens, cotangent, after=[qp_piece])
    ho_one = swap_z(ho_piece, 1)
    first_qp = join(z_qp, after=[tokens_cut[0]])
    got_qp = in_plane(first_qp)
    ho_pair = both_of(ho_piece, ho_one, after=[first_qp])
    ho_two = swap_z(ho_pair, 2)
    near, one, two, mid = exchange(tokens_cut, after=[got_qp[1], ho_pair])
    first_ho = join_ho(ho_one, ho_two, after=[mid])
    own = weld(where, ok, near, one, two, after=got_qp[1:] + (first_ho,))
    other = to_core(own)
    got_ho = in_plane(first_ho)
    w_qp, proj_send = call(
        place_qp_kernel,
        "place_qp",
        [(where, SMEM), (qkv_weight, HBM), (proj_weight, HBM)] + [(v, ANY) for v in got_qp],
        [
            (array((4, 4, PIECE, WIDE)), None),
            (array((2, 4, PIECE, HALF)), None),
        ],
        scratch=[pltpu.SemaphoreType.DMA((28,))],
        after=[own],
    )
    w_qp = w_qp.reshape(D, WIDE)
    proj_other = to_core(proj_send.reshape(HALF, HALF))
    normed = norm_one(ok, own, other, gain_one, bias_one, after=[w_qp])
    packed, attended, probs, low, branch_other = attn_fwd(
        where, 1, normed, w_qp, proj_other, qkv_bias[None], tables
    )
    packed, attended, probs, low, branch = attn_fwd(
        where, 0, normed, w_qp, proj_other, qkv_bias[None], tables,
        before=(packed, attended, probs, low), after=[got_ho[1]],
    )
    there = to_core(low)
    w_ho = call(
        place_ho_kernel,
        "place_ho",
        [(where, SMEM), (hidden_weight, HBM), (output_weight, HBM)] + [(v, ANY) for v in got_ho],
        [(array((4, 4, 4 * PIECE, D)), None)],
        scratch=[pltpu.SemaphoreType.DMA((32,))],
        after=[packed],
    )[0].reshape(16, 4 * PIECE, D)
    middle, second = norm_two(
        own, other, branch, branch_other, there, proj_bias[None], gain_two, bias_two, after=[w_ho]
    )
    active, slope = hidden_layer(where, second, w_ho, hidden_bias[None])

    def natural(keep_two, send_two):
        out = jnp.zeros((2, 4, 96, WIDE), BF)
        for q, part in ((s, keep_two[0]), (b, keep_two[1]), (a, send_two[0]), (s ^ 3, send_two[1])):
            out = lax.dynamic_update_index_in_dim(out, part, q, 1)
        return out.astype(F32)

    def sum_rows(full):
        return lax.psum_scatter(full, ("dp", "seq", "fsdp"), scatter_dimension=0, tiled=True)

    def spread_cols(grad, parts):
        grad = grad.reshape(D, parts, HALF)
        zero = jnp.zeros_like(grad)
        return jnp.where(
            c == 0, jnp.stack([grad, zero], axis=2), jnp.stack([zero, grad], axis=2)
        ).reshape(D, 2 * parts * HALF)

    def larger_wide(keep_two, send_two):
        return sum_rows(spread_cols(natural(keep_two, send_two).reshape(D, WIDE), 4))

    def larger_qp(keep_two, send_two):
        grad = natural(keep_two, send_two)
        qkv = sum_rows(spread_cols(grad[..., :QKV].reshape(D, QKV), 3))
        proj = jnp.concatenate(list(grad[..., QKV:].reshape(2, HALF, HALF)), axis=1)
        zero = jnp.zeros_like(proj)
        proj = jnp.where(c == 0, jnp.concatenate([proj, zero]), jnp.concatenate([zero, proj]))
        return qkv, sum_rows(proj)

    def step_one(send):
        return to_plane(send, plane_one)

    def step_two(parts, after=()):
        stay, send = add_one(parts, after)
        return stay, to_plane(send, plane_two), send

    def step_three(stay, got, after=()):
        keep, send = add_two(where, stay, got, after)
        return keep, swap_z(send, 1), send

    def step_four(keep, got, after=()):
        stay, send = add_three(keep, got, after)
        return stay, swap_z(send, 2), send

    def step_five(stay, got, after=()):
        total, send = add_four(where, stay, got, after)
        return total, to_core(send), send

    pair = n_dp == 2

    o_keep, o_send = weight_grad(where, [own, other], active)
    o_got = step_one(o_send) if pair else o_send
    grad_pre, part, part_low, hidden_sums = grad_pre_of(own, other, slope, w_ho, after=[o_send])
    part_there = to_core(part_low)
    h_keep, h_send = weight_grad(where, [second], grad_pre)
    h_got = step_one(h_send) if pair else h_send
    grad_middle, grad_branch, sums_two = norm_two_back(
        part, part_there, middle, gain_two, own, other, after=[h_send]
    )
    grad_packed, tab_grad, qkv_sums = attn_bwd(
        where, 0, packed, grad_branch, probs, w_qp, proj_other, tables
    )
    held = [grad_packed]
    if pair:
        oh_stay, oh_got, mid = step_two([(o_keep, o_got), (h_keep, h_got)], after=held)
        held = [mid]
    grad_packed, tab_grad_b, qkv_sums_b = attn_bwd(
        where, 1, packed, grad_branch, probs, w_qp, proj_other, tables,
        before=(grad_packed,), after=held,
    )
    q_keep, q_send = weight_grad_qp(where, normed, grad_packed, attended, grad_branch)
    held = [q_send]
    if pair:
        q_got = step_one(q_send)
        oh_keep, oh_got, mid = step_three(oh_stay, oh_got, after=held)
        held = [mid]
    back, back_low = product(
        "back", grad_packed, w_qp, pl.BlockSpec((D, QKV), lambda w: (0, 0)),
        lambda left, right: mm(left, right[...], ((1,), (1,))), after=held,
    )
    back_there = to_core(back_low)
    feed, feed_low = product(
        "feed", active, w_ho, None, lambda left, right: mm(left, output_part(right)),
        after=[back_low],
    )
    feed_there = to_core(feed_low)
    held = [feed_low]
    if pair:
        q_stay, q_got, mid = step_two([(q_keep, q_got)], after=held)
        held = [mid]
    *parts, sums_one = last(
        where, ok, back, back_there, own, gain_one, grad_middle, middle, feed, feed_there,
        output_bias[None], after=held,
    )
    to_offset = jnp.pad(
        (near_offset.reshape(-1)[None, :] == jnp.arange(2 * WIN - 1)[:, None]).astype(F32),
        ((0, 32 - (2 * WIN - 1)), (0, TAB // 2 - WIN * WIN)),
    )
    ins = (sums_two, sums_one, hidden_sums, qkv_sums, qkv_sums_b, tab_grad, tab_grad_b, to_offset)
    small = call(
        small_kernel,
        "small",
        [(where, SMEM)] + [(v, None) for v in ins],
        [(array((32, D), F32), None)],
    )[0]
    small_got = to_core(small)
    held = [small]
    if pair:
        oh_stay, oh_got, mid = step_four(oh_keep, oh_got, after=held)
        q_keep, q_got, mid = step_three(q_stay, q_got, after=[mid])
        held = [mid]
    small = tally([small, small_got], after=held)
    small_got = to_seq(small, 1)
    *parts, mid = exchange(parts, after=[small])
    small = tally([small, small_got], after=[mid])
    small_got = to_seq(small, 2)
    held = [small]
    if pair:
        q_stay, q_got, mid = step_four(q_keep, q_got, after=held)
        oh_total, oh_there, mid = step_five(oh_stay, oh_got, after=[mid])
        held = [mid]
    small = tally([small, small_got], after=held)
    small_got = swap_z(small, 1)
    input_grad, block_out = home(where, *parts, after=[small])
    small = tally([small, small_got], after=[input_grad])
    small_got = swap_z(small, 2)
    held = [small]
    if pair:
        q_total, q_there, mid = step_five(q_stay, q_got, after=held)
        held = [mid]
    small = tally([small, small_got], after=held)
    if pair:
        g_output, g_hidden, g_qkv, g_proj = finish(
            where, oh_total, oh_there, q_total, q_there, after=[small]
        )
        g_output = g_output.T
    else:
        g_output = larger_wide(o_keep, o_send).T
        g_hidden = larger_wide(h_keep, h_send)
        g_qkv, g_proj = larger_qp(q_keep, q_send)
    if n_dp > 2:
        groups = [list(range(core, n_dp, 2)) for core in range(2)]
        small = lax.psum(small, "dp", axis_index_groups=groups)
    (
        d_qkv_bias, d_height, d_width, d_proj_bias, d_gain_two, d_bias_two, d_hidden_bias,
        d_output_bias, d_gain_one, d_bias_one,
    ) = unpack(small)
    return (
        block_out,
        input_grad,
        d_gain_one,
        d_bias_one,
        g_qkv,
        d_qkv_bias,
        d_height,
        d_width,
        g_proj,
        d_proj_bias,
        d_gain_two,
        d_bias_two,
        g_hidden,
        d_hidden_bias,
        g_output,
        d_output_bias,
    )


def solution(mesh):
    tokens = P("dp", "fsdp", "seq", None)
    rows = P("fsdp", None)
    every = P(("dp", "seq", "fsdp"), None)
    args = (tokens, P("fsdp"), P(), P(), rows, P(), P(), P(), rows)
    args += (P(), P(), P(), rows, P(), rows, P(), tokens)
    outs = (tokens, tokens, P(), P(), every, P(), P(), P(), every)
    outs += (P(), P(), P(), every, P(), P(None, ("dp", "seq", "fsdp")), P())
    return jax.shard_map(
        functools.partial(per_device, mesh.shape["dp"]),
        mesh=mesh,
        in_specs=args,
        out_specs=outs,
        check_vma=False,
    )
```

```python
import functools

import jax
import jax.numpy as jnp
from jax import lax
from jax.experimental import pallas as pl
from jax.experimental.pallas import tpu as pltpu
from jax.sharding import PartitionSpec as P

D = 768
HD = 64
FF = 3072
WIN = 14
GRID = 48
NWS = 4
TOK = 49
PAD = 56
ROWS = 4 * PAD
SPLIT = 4 * TOK
HALF = D // 2
QKV = 3 * HALF
WIDE = 4 * HALF
PIECE = 48
PAIRS = 3
LANES = 128
TAB = 512
NEG = -1e30
EPS = 1e-06
SCALE = HD**-0.5
BF = jnp.bfloat16
F32 = jnp.float32
ANY = pl.BlockSpec(memory_space=pl.ANY)
HBM = pl.BlockSpec(memory_space=pltpu.HBM)
SMEM = pl.BlockSpec(memory_space=pltpu.SMEM)


def mm(left, right, dims=((1,), (0,))):
    return lax.dot_general(left, right, (dims, ((), ())), preferred_element_type=F32)


def array(shape, dtype=BF):
    return jax.ShapeDtypeStruct(shape, dtype)


def whole(shape):
    return pl.BlockSpec(shape, lambda *at: (0,) * len(shape))


def window(shape, index=None):
    index = index or (lambda w: w)
    return pl.BlockSpec((1,) + shape, lambda w: (index(w),) + (0,) * len(shape))


TIMES = dict(
    add_four0=1, add_four1=0.1, add_one1=8, add_two0=1, add_two1=1, attn_bwd1=1, attn_fwd1=1, back0=8,
    both_of0=1, cut0=3, feed0=1, join0=0.3, join_ho0=20, last0=20, norm_one0=0.3, norm_two0=3,
    norm_two_back0=20, pair_up0=0.3, pair_up1=50, place_qp0=87, small0=0.3, tables0=3, tally0=8, tally3=500,
    tally4=8, unpack0=3, weight_grad1=50, weld0=0.3,
)


COUNT = {}


def call(kernel, name, ins, outs, grid=(), scratch=(), after=(), vmem=8, alias=()):
    count = len(ins)
    extra = len(after)
    at = COUNT.get(name, 0)
    COUNT[name] = at + 1
    cost = TIMES.get(name + str(at), 87.0)

    def held(v):
        mode = pl.Buffered(1) if grid else None
        return pl.BlockSpec(v.shape, lambda *at: (0,) * len(v.shape), pipeline_mode=mode)

    def body(*refs):
        return kernel(*refs[:count], *refs[count + extra :])

    return pl.pallas_call(
        body,
        grid=grid,
        in_specs=[spec or held(v) for v, spec in ins] + [ANY] * extra,
        out_specs=[spec or whole(v.shape) for v, spec in outs],
        out_shape=[v for v, _ in outs],
        scratch_shapes=list(scratch),
        compiler_params=pltpu.CompilerParams(vmem_limit_bytes=vmem * 1024 * 1024),
        input_output_aliases=dict(alias),
        cost_estimate=pl.CostEstimate(
            flops=int(1.15e9 * cost),
            bytes_accessed=int(1.15e6 * cost),
            transcendentals=0,
        ),
        name=name,
    )(*[v for v, _ in ins], *after)


def pieces_kernel(where, qkv, proj, hidden, output, out, qp_out, sems):
    s, c = where[1], where[5]
    rows = pl.ds(pl.multiple_of(s * PIECE, PIECE), PIECE)
    start = pl.multiple_of(c * HALF + s * 2 * PIECE, 2 * PIECE)
    copies = [(output.at[pl.ds(start, 2 * PIECE)], out.at[: 2 * PIECE])]
    for i in range(4):
        cols = pl.ds(pl.multiple_of(i * D + c * HALF, LANES), HALF)
        at = (2 + i // 2) * PIECE
        half = slice(i % 2 * HALF, (i % 2 + 1) * HALF)
        copies.append((hidden.at[rows, cols], out.at[at : at + PIECE, half]))
    for i in range(3):
        cols = pl.ds(pl.multiple_of(i * D + c * HALF, LANES), HALF)
        copies.append((qkv.at[rows, cols], qp_out.at[:, i * HALF : (i + 1) * HALF]))
    cols = pl.ds(pl.multiple_of(c * HALF, LANES), HALF)
    copies.append((proj.at[rows, cols], qp_out.at[:, QKV:]))
    run_copies(copies, sems)


def run_copies(pairs, sems):
    copies = [
        pltpu.make_async_copy(src, dst, sems.at[n]) for n, (src, dst) in enumerate(pairs)
    ]
    for copy in copies:
        copy.start()
    for copy in copies:
        copy.wait()


def pieces(where, qkv, proj, hidden, output):
    return call(
        pieces_kernel,
        "pieces",
        [(where, SMEM), (qkv, HBM), (proj, HBM), (hidden, HBM), (output, HBM)],
        [(array((4 * PIECE, D)), None), (array((PIECE, WIDE)), None)],
        scratch=[pltpu.SemaphoreType.DMA((9,))],
        vmem=60,
    )


def output_part(w, first=0, count=16):
    return w[first : first + count, : 2 * PIECE, :].reshape(count * 2 * PIECE, D)


def hidden_part(w, half):
    at = (2 + half) * PIECE
    return w[:, at : at + PIECE, :].reshape(D, D)


def join_kernel(one, two, three, out):
    out[0] = one[...]
    out[1] = two[...]
    out[2] = three[...]


def join(parts, after=()):
    return call(
        join_kernel,
        "join",
        [(part, None) for part in parts],
        [(array((3,) + parts[0].shape), None)],
        after=after,
    )[0]


def both_kernel(one, two, out):
    out[0] = one[...]
    out[1] = two[...]


def both_of(one, two, after=()):
    return call(
        both_kernel,
        "both_of",
        [(one, None), (two, None)],
        [(array((2,) + one.shape), None)],
        after=after,
    )[0]


def join_ho_kernel(one, two, out):
    out[0] = one[...]
    out[1] = two[0]
    out[2] = two[1]


def join_ho(one, two, after=()):
    return call(
        join_ho_kernel,
        "join_ho",
        [(one, None), (two, None)],
        [(array((3,) + one.shape), None)],
        after=after,
    )[0]


def place_qp_kernel(where, qkv, proj, first, second, third, fourth, out, send, sems):
    z, c = where[0], where[5]
    copies = []

    def add(src, dst):
        copies.append(pltpu.make_async_copy(src, dst, sems.at[len(copies)]))

    for i in range(3):
        for q in range(4):
            cols = pl.ds(pl.multiple_of(i * D + c * HALF, LANES), HALF)
            add(
                qkv.at[q * PIECE : (q + 1) * PIECE, cols],
                out.at[z, q, :, i * HALF : (i + 1) * HALF],
            )
    for q in range(4):
        cols = pl.ds(pl.multiple_of(c * HALF, LANES), HALF)
        add(proj.at[q * PIECE : (q + 1) * PIECE, cols], out.at[z, q, :, QKV:])
    for i in range(3):
        zz = lax.rem(z + 3 - i, 4)
        for n, src in enumerate((first, second, third, fourth)):
            add(src.at[i], out.at[zz, where[1 + n]])
    for copy in copies:
        copy.start()
    for copy in copies:
        copy.wait()
    send[...] = out[pl.ds(2 * (1 - c), 2), :, :, QKV:]


def place_ho_kernel(where, hidden, output, first, second, third, fourth, out, sems):
    z, c = where[0], where[5]
    copies = []
    for q in range(4):
        start = pl.multiple_of(c * HALF + q * 2 * PIECE, 2 * PIECE)
        copies.append((output.at[pl.ds(start, 2 * PIECE)], out.at[z, q, : 2 * PIECE]))
        for i in range(4):
            cols = pl.ds(pl.multiple_of(i * D + c * HALF, LANES), HALF)
            at = (2 + i // 2) * PIECE
            half = slice(i % 2 * HALF, (i % 2 + 1) * HALF)
            copies.append(
                (
                    hidden.at[q * PIECE : (q + 1) * PIECE, cols],
                    out.at[z, q, at : at + PIECE, half],
                )
            )
    for i in range(3):
        zz = z ^ (i + 1)
        for n, src in enumerate((first, second, third, fourth)):
            copies.append((src.at[i], out.at[zz, where[1 + n]]))
    run_copies(copies, sems)


def hand_out(c, rows, i, outs):
    near, both, far = outs

    def piece(k):
        return rows[pl.ds(pl.multiple_of(k * PAD, 8), PAD), :].astype(BF)

    near[i] = piece(0)
    both[0, i] = piece(1 + c)
    both[1, i] = piece(3)
    far[i] = piece(2 - c)


def handed(images):
    shape = (images, PAD, D)
    return [(array(shape), None), (array((2,) + shape), None), (array(shape), None)]


ROWS_F32 = pltpu.VMEM((ROWS, D), F32)


def gathered_rows(c, near, one, two, i):
    first, second = one[0, i].astype(F32), two[0, i].astype(F32)
    parts = [near[i].astype(F32)]
    parts += [jnp.where(c == 0, first, second), jnp.where(c == 0, second, first)]
    return jnp.concatenate(parts + [two[1, i].astype(F32)])


def pair_kernel(far, one, out):
    out[0] = far[...]
    out[1] = one[1]


def pair_up(far, one, after=()):
    return call(
        pair_kernel,
        "pair_up",
        [(far, None), (one, None)],
        [(array((2,) + far.shape), None)],
        after=after,
    )[0]


def cut_kernel(where, tokens, cotangent, *rest):
    s, c = where[1], where[5]
    images = tokens.shape[0]
    outs, rows = rest[:3], rest[3]
    row = lax.broadcasted_iota(jnp.int32, (ROWS, SPLIT), 0)
    col = lax.broadcasted_iota(jnp.int32, (ROWS, SPLIT), 1)
    token = row % PAD
    take = ((token < TOK) & (col == token * 4 + (s ^ (row // PAD)))).astype(F32).astype(BF)
    for i in range(2 * images):
        rows[...] = mm(take, tokens[i] if i < images else cotangent[i - images])
        hand_out(c, rows, i, outs)


def cut(where, tokens, cotangent, after=()):
    images = tokens.shape[0]
    flat = [jnp.transpose(v, (0, 2, 1, 3)).reshape(images, SPLIT, D) for v in (tokens, cotangent)]
    return call(
        cut_kernel,
        "cut",
        [(where, SMEM)] + [(v, None) for v in flat],
        handed(2 * images),
        scratch=[ROWS_F32],
        after=after,
        vmem=12,
    )


def weld_kernel(where, ok, near, one, two, out):
    count = out.shape[0]
    for i in range(count):
        rows = gathered_rows(where[5], near, one, two, i)
        out[i] = (rows if i < count // 2 else rows * ok[...]).astype(BF)


def weld(where, ok, near, one, two, after=()):
    return call(
        weld_kernel,
        "weld",
        [(where, SMEM), (ok, None)] + [(part, None) for part in (near, one, two)],
        [(array((near.shape[0], ROWS, D)), None)],
        after=after,
    )[0]


def home_kernel(where, near, one, two, *outs):
    s = where[1]
    row = lax.broadcasted_iota(jnp.int32, (SPLIT, ROWS), 0)
    col = lax.broadcasted_iota(jnp.int32, (SPLIT, ROWS), 1)
    token = col % PAD
    take = ((token < TOK) & (row == token * 4 + (s ^ (col // PAD)))).astype(F32).astype(BF)
    images = outs[0].shape[0]
    for i in range(2 * images):
        rows = gathered_rows(where[5], near, one, two, i).astype(BF)
        outs[i // images][i % images] = mm(take, rows).astype(BF)


def home(where, near, one, two, after=()):
    images = near.shape[0] // 2
    flat = call(
        home_kernel,
        "home",
        [(where, SMEM)] + [(part, None) for part in (near, one, two)],
        [(array((images, SPLIT, D)), None)] * 2,
        after=after,
        vmem=12,
    )
    return [jnp.transpose(v.reshape(images, TOK, 4, D), (0, 2, 1, 3)) for v in flat]


def unit_of(v):
    v = v - jnp.mean(v, axis=-1, keepdims=True)
    rstd = lax.rsqrt(jnp.mean(v * v, axis=-1, keepdims=True) + EPS)
    return v * rstd, rstd


def norm_back(grad, unit, rstd):
    return rstd * (
        grad
        - jnp.mean(grad, axis=-1, keepdims=True)
        - unit * jnp.mean(grad * unit, axis=-1, keepdims=True)
    )


def norm_one_kernel(ok, own, other, gain, shift, out):
    images = own.shape[0] // 2
    for w in range(2 * images):
        x = own[w] if w < images else other[w - images]
        unit, _ = unit_of(x.astype(F32))
        out[w] = ((unit * gain[...] + shift[...]) * ok[...]).astype(BF)


def norm_one(ok, own, other, gain, shift, after=()):
    return call(
        norm_one_kernel,
        "norm_one",
        [(v, None) for v in (ok, own, other, gain, shift)],
        [(array(own.shape), None)],
        after=after,
        vmem=12,
    )[0]


def norm_two_kernel(
    own, other, branch, branch_other, there, bias, gain, shift, middle, second
):
    images = own.shape[0] // 2
    for w in range(2 * images):
        x, mine = (own, branch) if w < images else (other, branch_other)
        at = w % images
        value = x[at].astype(F32) + (mine[at] + there[w].astype(F32)) + bias[...]
        middle[w] = value
        unit, _ = unit_of(value)
        second[w] = (unit * gain[...] + shift[...]).astype(BF)


def norm_two(own, other, branch, branch_other, there, bias, gain, shift, after=()):
    shape = own.shape
    ins = (own, other, branch, branch_other, there, bias, gain, shift)
    return call(
        norm_two_kernel,
        "norm_two",
        [(v, None) for v in ins],
        [(array(shape, F32), None), (array(shape), None)],
        after=after,
        vmem=14,
    )


def norm_two_back_kernel(
    images, part, there, middle, gain, feed, feed_other, grad_middle, grad_branch, sums
):
    sums[...] = jnp.zeros_like(sums)
    for w in range(2 * images):
        grad = part[w] + there[w].astype(F32)
        unit, rstd = unit_of(middle[w])
        feed_w = (feed[images + w] if w < images else feed_other[w]).astype(F32)
        total = feed_w + norm_back(grad * gain[...], unit, rstd)
        low = total.astype(BF)
        grad_branch[w] = low
        if w < images:
            grad_middle[w] = total
            sums[0:1] += jnp.sum(grad * unit, axis=0, keepdims=True)
            sums[1:2] += jnp.sum(grad, axis=0, keepdims=True)
            sums[2:3] += jnp.sum(low.astype(F32), axis=0, keepdims=True)
            sums[3:4] += jnp.sum(feed_w, axis=0, keepdims=True)


def norm_two_back(part, there, middle, gain, feed, feed_other, after=()):
    count = part.shape[0]
    return call(
        functools.partial(norm_two_back_kernel, count // 2),
        "norm_two_back",
        [(v, None) for v in (part, there, middle, gain, feed, feed_other)],
        [
            (array((count // 2, ROWS, D), F32), None),
            (array((count, ROWS, D)), None),
            (array((8, D), F32), None),
        ],
        after=after,
        vmem=16,
    )


def last_kernel(
    where, ok, back, back_there, own, gain, grad_middle, middle, feed, feed_there, bias, *rest
):
    outs, sums, rows = rest[:3], rest[3], rest[4]
    images = back.shape[0]
    sums[...] = jnp.zeros_like(sums)
    for w in range(images):
        grad = (back[w] + back_there[w].astype(F32)) * ok[...]
        unit, rstd = unit_of(own[w].astype(F32))
        sums[0:1] += jnp.sum(grad * unit, axis=0, keepdims=True)
        sums[1:2] += jnp.sum(grad, axis=0, keepdims=True)
        rows[...] = grad_middle[w] + norm_back(grad * gain[...], unit, rstd)
        hand_out(where[5], rows, w, outs)
        rows[...] = (middle[w] + feed[w] + feed_there[w].astype(F32) + bias[...]) * ok[...]
        hand_out(where[5], rows, images + w, outs)


def last(where, ok, back, back_there, own, gain, grad_middle, middle, feed, feed_there, bias, after=()):
    ins = (ok, back, back_there, own, gain, grad_middle, middle, feed, feed_there, bias)
    return call(
        last_kernel,
        "last",
        [(where, SMEM)] + [(v, None) for v in ins],
        handed(own.shape[0]) + [(array((8, D), F32), None)],
        scratch=[ROWS_F32],
        after=after,
        vmem=20,
    )


def attn_fwd_kernel(
    where, normed, w_qp, other, b_qkv, table, spot, fold, keys, bias, *rest
):
    packed, out, probs, low, branch = rest[-5:]
    c = where[5]
    lane = lax.broadcasted_iota(jnp.int32, (ROWS, LANES), 1)
    shift = [b_qkv[:, pl.ds(pl.multiple_of(i * D + c * HALF, LANES), HALF)] for i in range(3)]
    packed[0] = (mm(normed[0], w_qp[:, :QKV]) + jnp.concatenate(shift, axis=1)).astype(BF)

    def columns(part, pair):
        at = part * HALF + pair * LANES
        return packed[0, :, at : at + LANES]

    queries = jnp.concatenate([columns(0, pair) for pair in range(PAIRS)])
    mask = jnp.concatenate([spot[...]] * PAIRS)
    rels = [mm((mm(queries, table[e]) * mask).astype(BF), fold[...]).astype(BF) for e in range(2)]
    for pair in range(PAIRS):
        q, k, v = columns(0, pair), columns(1, pair), columns(2, pair)
        right = jnp.concatenate([k, keys[...]], axis=1)
        parts = []
        for e in range(2):
            mine = (lane < HD) if e == 0 else (lane >= HD)
            rel = rels[e][pair * ROWS : (pair + 1) * ROWS]
            scaled = jnp.where(mine, q.astype(F32) * SCALE, 0.0).astype(BF)
            left = jnp.concatenate([scaled, rel], axis=1)
            s = mm(left, right, ((1,), (1,))) + bias[...]
            p = jnp.exp(s - jnp.max(s, axis=1, keepdims=True))
            p = (p * (1.0 / jnp.sum(p, axis=1, keepdims=True))).astype(BF)
            probs[0, 2 * pair + e] = p
            parts.append(mm(p, v))
        out[0, :, pair * LANES : (pair + 1) * LANES] = jnp.where(
            lane < HD, parts[0], parts[1]
        ).astype(BF)
    att = out[0]
    own_cols = pl.ds(pl.multiple_of(c * HALF, LANES), HALF)
    other_cols = pl.ds(pl.multiple_of((1 - c) * HALF, LANES), HALF)
    own_rows = pl.ds(pl.multiple_of(c * HALF, HALF), HALF)
    mine = mm(att, w_qp[own_rows, QKV:])
    theirs = mm(att, other[...])
    branch[0, :, own_cols] = mine
    branch[0, :, other_cols] = theirs
    low[0, :, own_cols] = mine.astype(BF)
    low[0, :, other_cols] = theirs.astype(BF)


def attn_fwd(where, group, normed, w_qp, other, b_qkv, tables, before=(), after=()):
    table, spot, fold, keys, bias = tables
    count = normed.shape[0]
    half = count // 2
    start = group * half
    ins = [(where, SMEM), (normed, window((ROWS, D), lambda w: w + start))]
    ins += [(v, None) for v in (w_qp, other, b_qkv, table, spot, fold, keys, bias)]
    kept = ((ROWS, QKV), (ROWS, HALF), (2 * PAIRS, ROWS, ROWS))
    outs = [(array((count,) + shape), window(shape, lambda w: w + start)) for shape in kept]
    outs += [
        (array((count, ROWS, D)), window((ROWS, D), lambda w: (w + start + half) % count)),
        (array((half, ROWS, D), F32), window((ROWS, D))),
    ]
    return call(
        attn_fwd_kernel,
        "attn_fwd",
        ins + [(v, ANY) for v in before],
        outs,
        grid=(half,),
        after=after,
        alias=[(len(ins) + n, n) for n in range(len(before))],
        vmem=18,
    )


def attn_bwd_kernel(
    where, packed, grad_branch, probs, w_qp, other, table, spot, fold, keys, *rest
):
    out, tab_grad, sums, att = rest[-4:]
    c = where[5]
    lane = lax.broadcasted_iota(jnp.int32, (ROWS, LANES), 1)
    lane_t = lax.broadcasted_iota(jnp.int32, (TAB, LANES), 1)

    @pl.when(pl.program_id(0) == 0)
    def _():
        tab_grad[...] = jnp.zeros_like(tab_grad)
        sums[...] = jnp.zeros_like(sums)

    own_cols = pl.ds(pl.multiple_of(c * HALF, LANES), HALF)
    other_cols = pl.ds(pl.multiple_of((1 - c) * HALF, LANES), HALF)
    own_rows = pl.ds(pl.multiple_of(c * HALF, HALF), HALF)
    att[...] = (
        mm(grad_branch[0, :, own_cols], w_qp[own_rows, QKV:], ((1,), (1,)))
        + mm(grad_branch[0, :, other_cols], other[...], ((1,), (1,)))
    ).astype(BF)
    def columns(part, pair):
        at = part * HALF + pair * LANES
        return packed[0, :, at : at + LANES]

    queries = jnp.concatenate([columns(0, pair) for pair in range(PAIRS)])
    mask = jnp.concatenate([spot[...]] * PAIRS)
    both, dk, dv = [[], []], [[], []], [[], []]
    for pair in range(PAIRS):
        q, k, v = columns(0, pair), columns(1, pair), columns(2, pair)
        go = att[:, pair * LANES : (pair + 1) * LANES]
        right = jnp.concatenate([k, keys[...]], axis=1)
        for e in range(2):
            mine = (lane < HD) if e == 0 else (lane >= HD)
            go_e = jnp.where(mine, go.astype(F32), 0.0).astype(BF)
            p_low = probs[0, 2 * pair + e]
            p = p_low.astype(F32)
            dp = mm(go_e, v, ((1,), (1,)))
            ds = (p * (dp - jnp.sum(dp * p, axis=1, keepdims=True))).astype(BF)
            both[e].append(mm(ds, right))
            dk[e].append(SCALE * mm(ds, q, ((0,), (0,))))
            dv[e].append(mm(p_low, go, ((0,), (0,))))
    dq, dt = [], []
    for e in range(2):
        rel = jnp.concatenate([part[:, LANES:] for part in both[e]]).astype(BF)
        spread = (mm(rel, fold[...], ((1,), (1,))) * mask).astype(BF)
        flat = jnp.concatenate([part[:, :LANES] for part in both[e]])
        dq.append(SCALE * flat + mm(spread, table[e], ((1,), (1,))))
        dt.append(mm(spread, queries, ((0,), (0,))))
    tab_grad[...] += jnp.where(lane_t < HD, dt[0], dt[1])
    for pair in range(PAIRS):
        rows = slice(pair * ROWS, (pair + 1) * ROWS)
        pairs = ((dq[0][rows], dq[1][rows]), (dk[0][pair], dk[1][pair]), (dv[0][pair], dv[1][pair]))
        for part, two in enumerate(pairs):
            low = jnp.where(lane < HD, two[0], two[1]).astype(BF)
            cols = slice(part * HALF + pair * LANES, part * HALF + (pair + 1) * LANES)
            out[0, :, cols] = low
            sums[0:1, cols] += jnp.sum(low.astype(F32), axis=0, keepdims=True)


def attn_bwd(where, group, packed, grad_branch, probs, w_qp, other, tables, before=(), after=()):
    table, spot, fold, keys, _ = tables
    count = packed.shape[0]
    half = count // 2
    start = group * half
    ins = [
        (where, SMEM),
        (packed, window((ROWS, QKV), lambda w: w + start)),
        (grad_branch, window((ROWS, D), lambda w: w + start)),
        (probs, window((2 * PAIRS, ROWS, ROWS), lambda w: w + start)),
    ]
    ins += [(v, None) for v in (w_qp, other, table, spot, fold, keys)]
    return call(
        attn_bwd_kernel,
        "attn_bwd",
        ins + [(v, ANY) for v in before],
        [
            (array((count, ROWS, QKV)), window((ROWS, QKV), lambda w: w + start)),
            (array((TAB, LANES), F32), None),
            (array((8, QKV), F32), None),
        ],
        grid=(half,),
        scratch=[pltpu.VMEM((ROWS, HALF), BF)],
        after=after,
        alias=[(len(ins) + n, n) for n in range(len(before))],
        vmem=18,
    )


def hidden_kernel(where, second, w, bias, active, slope):
    c = where[5]
    for half in range(2):
        cols = slice(half * D, (half + 1) * D)
        shift = [
            bias[:, pl.ds(pl.multiple_of(i * D + c * HALF, LANES), HALF)]
            for i in (2 * half, 2 * half + 1)
        ]
        v = mm(second[0], hidden_part(w, half)) + jnp.concatenate(shift, axis=1)
        phi = 0.5 * (1.0 + lax.erf(v * (0.5**0.5)))
        active[0, :, cols] = (v * phi).astype(BF)
        slope[0, :, cols] = (phi + v * (jnp.exp(-0.5 * v * v) * 0.3989422804014327)).astype(BF)


def hidden_layer(where, second, w_hidden, bias, after=()):
    count = second.shape[0]
    return call(
        hidden_kernel,
        "hidden",
        [(where, SMEM), (second, window((ROWS, D))), (w_hidden, None), (bias, None)],
        [(array((count, ROWS, WIDE)), window((ROWS, WIDE)))] * 2,
        grid=(count,),
        after=after,
        vmem=14,
    )


def product_kernel(of, count, left, right, own, low):
    w = pl.program_id(0)
    value = of(left[0], right)

    @pl.when(w < count // 2)
    def _():
        low[w] = value.astype(BF)

    @pl.when(w >= count // 2)
    def _():
        own[w - count // 2] = value


def product(name, left, right, right_spec, of, after=()):
    count = left.shape[0]
    shape = (count // 2, ROWS, D)
    return call(
        functools.partial(product_kernel, of, count),
        name,
        [(left, window(left.shape[1:], lambda w: (w + count // 2) % count)), (right, right_spec)],
        [(array(shape, F32), None), (array(shape), None)],
        grid=(count,),
        after=after,
        vmem=14,
    )


def grad_pre_kernel(count, own, other, slope, w, out, part, low, sums):
    feed = jnp.where(pl.program_id(0) < count // 2, own[0].astype(F32), other[0].astype(F32))
    feed = feed.astype(BF)

    @pl.when(pl.program_id(0) == 0)
    def _():
        sums[...] = jnp.zeros_like(sums)

    for half in range(2):
        cols = slice(half * D, (half + 1) * D)
        value = mm(feed, output_part(w, 8 * half, 8), ((1,), (1,))) * slope[0, :, cols].astype(F32)
        value = value.astype(BF)
        out[0, :, cols] = value
        sums[0:1, cols] += jnp.sum(value.astype(F32), axis=0, keepdims=True)
    value = mm(out[0, :, :D], hidden_part(w, 0), ((1,), (1,)))
    value = value + mm(out[0, :, D:], hidden_part(w, 1), ((1,), (1,)))
    part[0] = value
    low[0] = value.astype(BF)


def grad_pre_of(own, other, slope, w, after=()):
    count = slope.shape[0]
    half = count // 2
    return call(
        functools.partial(grad_pre_kernel, count),
        "grad_pre",
        [
            (own, window((ROWS, D), lambda w: half + jnp.minimum(w, half - 1))),
            (other, window((ROWS, D), lambda w: half + jnp.maximum(w - half, 0))),
            (slope, window((ROWS, WIDE))),
            (w, None),
        ],
        [
            (array((count, ROWS, WIDE)), window((ROWS, WIDE))),
            (array((count, ROWS, D), F32), window((ROWS, D))),
            (array((count, ROWS, D)), window((ROWS, D), lambda w: (w + count // 2) % count)),
            (array((8, WIDE), F32), None),
        ],
        grid=(count,),
        after=after,
        vmem=18,
    )


def deal(where, total, keep, send, cols):
    for n, out in enumerate((keep, keep, send, send)):
        q = where[(1, 3, 2, 4)[n]]
        for h in range(2):
            rows = pl.ds(pl.multiple_of(h * HALF + q * 96, 8), 96)
            out[n % 2, h, :, cols] = total[rows, :].astype(BF)


def weight_grad_kernel(count, where, *refs):
    lefts, (right, keep, send, flip, total) = refs[:count], refs[count:]
    rows = right.shape[0] // count
    for n, left in enumerate(lefts):
        flip[:, n * rows : (n + 1) * rows] = left[left.shape[0] - rows :, :].T
    for at in range(0, WIDE, TAB):
        cols = slice(at, at + TAB)
        total[...] = mm(flip[...], right[:, cols])
        deal(where, total, keep, send, cols)


def weight_grad(where, lefts, right, after=()):
    rows = right.shape[0] * right.shape[1]
    shape = (2, 2, 96, WIDE)
    return call(
        functools.partial(weight_grad_kernel, len(lefts)),
        "weight_grad",
        [(where, SMEM)]
        + [(left.reshape(-1, D), None) for left in lefts]
        + [(right.reshape(rows, WIDE), None)],
        [(array(shape), None), (array(shape), None)],
        scratch=[pltpu.VMEM((D, rows), BF), pltpu.VMEM((D, TAB), F32)],
        after=after,
        vmem=16,
    )


def weight_grad_qp_kernel(
    where, normed, packed, att, branch, keep, send, flip, total, flip_att, total_att
):
    flip[...] = normed[...].T
    for at in range(0, QKV, HALF):
        cols = slice(at, at + HALF)
        total[...] = mm(flip[...], packed[:, cols])
        deal(where, total, keep, send, cols)
    flip_att[...] = att[...].T
    total_att[...] = mm(flip_att[...], branch[...])
    for n, out in enumerate((keep, keep, send, send)):
        q = where[(1, 3, 2, 4)[n]]
        rows = pl.ds(pl.multiple_of(q * 96, 8), 96)
        for h in range(2):
            out[n % 2, h, :, QKV:] = total_att[rows, h * HALF : (h + 1) * HALF].astype(BF)


def weight_grad_qp(where, normed, packed, att, branch, after=()):
    rows = normed.shape[0] * normed.shape[1]
    shape = (2, 2, 96, WIDE)
    return call(
        weight_grad_qp_kernel,
        "weight_grad_qp",
        [(where, SMEM)]
        + [(v.reshape(rows, v.shape[-1]), None) for v in (normed, packed, att, branch)],
        [(array(shape), None), (array(shape), None)],
        scratch=[
            pltpu.VMEM((D, rows), BF),
            pltpu.VMEM((D, HALF), F32),
            pltpu.VMEM((HALF, rows), BF),
            pltpu.VMEM((HALF, D), F32),
        ],
        after=after,
        vmem=16,
    )


def add_one_kernel(*refs):
    stay, send = refs[-2:]
    for i in range(len(refs) // 2 - 1):
        keep, got = refs[2 * i], refs[2 * i + 1]
        for h in range(2):
            for q in range(4):
                rows = slice(q * 24, (q + 1) * 24)
                stay[i, h, q] = keep[0, h, rows].astype(F32) + got[0, h, rows].astype(F32)
                total = keep[1, h, rows].astype(F32) + got[1, h, rows].astype(F32)
                send[i, h, q] = total.astype(BF)


def add_one(parts, after=()):
    shape = (len(parts), 2, 4, 24, WIDE)
    return call(
        add_one_kernel,
        "add_one",
        [(v, None) for part in parts for v in part],
        [(array(shape, F32), None), (array(shape), None)],
        after=after,
        vmem=16,
    )


def add_two_kernel(where, stay, got, keep, send):
    z = where[0]
    for i in range(stay.shape[0]):
        for n in range(2):
            mine, theirs = z ^ (2 * n), z ^ (2 * n + 1)
            for h in range(2):
                keep[n, i, h] = stay[i, h, mine] + got[i, h, mine].astype(F32)
                send[n, i, h] = (stay[i, h, theirs] + got[i, h, theirs].astype(F32)).astype(BF)


def add_two(where, stay, got, after=()):
    shape = (2, stay.shape[0], 2, 24, WIDE)
    return call(
        add_two_kernel,
        "add_two",
        [(where, SMEM), (stay, None), (got, None)],
        [(array(shape, F32), None), (array(shape), None)],
        after=after,
        vmem=14,
    )


def add_three_kernel(keep, got, stay, send):
    for i in range(stay.shape[0]):
        for h in range(2):
            stay[i, h] = keep[0, i, h] + got[0, i, h].astype(F32)
            send[i, h] = (keep[1, i, h] + got[1, i, h].astype(F32)).astype(BF)


def add_three(keep, got, after=()):
    shape = keep.shape[1:]
    return call(
        add_three_kernel,
        "add_three",
        [(keep, None), (got, None)],
        [(array(shape, F32), None), (array(shape), None)],
        after=after,
    )


def add_four_kernel(where, stay, got, total, send):
    for i in range(stay.shape[0]):
        for h in range(2):
            total[i, h] = stay[i, h] + got[i, h].astype(F32)
        send[i] = total[i, 1 - where[5]]


def add_four(where, stay, got, after=()):
    shape = (stay.shape[0],) + stay.shape[2:]
    return call(
        add_four_kernel,
        "add_four",
        [(where, SMEM), (stay, None), (got, None)],
        [(array(stay.shape, F32), None), (array(shape, F32), None)],
        after=after,
    )


def finish_kernel(where, two, two_there, total, there, output, hidden, qkv, proj):
    c = where[5]

    def lay(out, blocks, mine, theirs):
        for i in range(blocks):
            cols = slice(i * HALF, (i + 1) * HALF)
            out[:, pl.ds(pl.multiple_of(i * D + c * HALF, LANES), HALF)] = mine[:, cols]
            out[:, pl.ds(pl.multiple_of(i * D + (1 - c) * HALF, LANES), HALF)] = theirs[:, cols]

    lay(output, 4, two.at[0, c], two_there.at[0])
    lay(hidden, 4, two.at[1, c], two_there.at[1])
    lay(qkv, 3, total.at[0, c], there.at[0])
    for h in range(2):
        proj[:, h * HALF : (h + 1) * HALF] = total[0, h, :, QKV:]


def finish(where, two, two_there, total, there, after=()):
    return call(
        finish_kernel,
        "finish",
        [(where, SMEM)] + [(v, None) for v in (two, two_there, total, there)],
        [(array((24, blocks * D), F32), None) for blocks in (4, 4, 3, 1)],
        after=after,
    )


def small_kernel(where, two, one, hidden, qkv, qkv_b, tab, tab_b, to_offset, out):
    c = where[5]
    out[...] = jnp.zeros_like(out)
    cols = pl.ds(pl.multiple_of(c * HALF, LANES), HALF)
    for i in range(3):
        part = slice(i * HALF, (i + 1) * HALF)
        out[i : i + 1, cols] = qkv[0:1, part] + qkv_b[0:1, part]
    for i in range(4):
        out[3 + i : 4 + i, cols] = hidden[0:1, i * HALF : (i + 1) * HALF]
    for i in range(4):
        out[7 + i : 8 + i, :] = two[i : i + 1, :]
    for i in range(2):
        out[11 + i : 12 + i, :] = one[i : i + 1, :]
        half = slice(i * (TAB // 2), (i + 1) * (TAB // 2))
        rel = lax.dot_general(
            to_offset[...],
            tab[half, :] + tab_b[half, :],
            (((1,), (0,)), ((), ())),
            preferred_element_type=F32,
            precision=lax.Precision.HIGHEST,
        )
        for k in range(4):
            out[16 + 8 * i : 24 + 8 * i, k * LANES : (k + 1) * LANES] = rel[8 * k : 8 * k + 8]


def tally_kernel(*refs):
    if len(refs) == 3:
        refs[2][...] = refs[0][...] + refs[1][...]
    else:
        refs[4][...] = (refs[0][...] + refs[1][...]) + (refs[2][...] + refs[3][...])


def tally(parts, after=()):
    return call(
        tally_kernel,
        "tally",
        [(v, None) for v in parts],
        [(array(parts[0].shape, F32), None)],
        after=after,
    )[0]


def unpack_kernel(total, *outs):
    qkv, height, width, proj, gain_two, bias_two, hidden, output, gain_one, bias_one = outs
    for i in range(3):
        qkv[i * D : (i + 1) * D] = total[i, :]
    for i in range(4):
        hidden[i * D : (i + 1) * D] = total[3 + i, :]
    rows = (gain_two, bias_two, proj, output, gain_one, bias_one)
    for i, out in enumerate(rows):
        out[...] = total[7 + i, :]
    for i, out in enumerate((height, width)):
        at = slice(16 + 8 * i, 24 + 8 * i)
        rel = jnp.concatenate([total[at, k * LANES : (k + 1) * LANES] for k in range(4)])
        out[...] = (rel + pltpu.roll(rel, HD, 1))[: 2 * WIN - 1, :HD]


def unpack(total):
    rel = (2 * WIN - 1, HD)
    shapes = [(2 * QKV,), rel, rel] + [(D,)] * 3 + [(FF,)] + [(D,)] * 3
    return call(
        unpack_kernel, "unpack", [(total, None)], [(array(shape, F32), None) for shape in shapes]
    )


def per_device(
    n_dp,
    image_tokens,
    slot_window,
    first_gain,
    first_bias,
    qkv_weight,
    qkv_bias,
    rel_height,
    rel_width,
    proj_weight,
    proj_bias,
    second_gain,
    second_bias,
    hidden_weight,
    hidden_bias,
    output_weight,
    output_bias,
    cotangent,
):
    COUNT.clear()
    images = image_tokens.shape[0]
    count = 2 * images
    c = lax.axis_index("dp") % 2
    s = lax.axis_index("seq")
    z = lax.axis_index("fsdp")
    a = jnp.where(c == 0, s ^ 1, s ^ 2)
    b = jnp.where(c == 0, s ^ 2, s ^ 1)
    where = jnp.stack([z, s, a, b, s ^ 3, c]).astype(jnp.int32)

    def plane_perm(step):
        out = []
        for i in range(n_dp):
            hop = (1, 2)[(i + step) % 2]
            out += [(i * 4 + j, i * 4 + (j ^ hop)) for j in range(4)]
        return out

    plane_one, plane_two = plane_perm(0), plane_perm(1)

    def to_core(v):
        return lax.ppermute(v, "dp", [(i, i ^ 1) for i in range(n_dp)])

    def to_seq(v, k):
        return lax.ppermute(v, "seq", [(i, i ^ k) for i in range(4)])

    def to_z(v, k):
        return lax.ppermute(v, "fsdp", [(i, (i + k) % 4) for i in range(4)])

    def swap_z(v, hop):
        return lax.ppermute(v, "fsdp", [(i, i ^ hop) for i in range(4)])

    def to_plane(v, perm):
        return lax.ppermute(v, ("dp", "seq"), perm)

    def pick(v, index, axis=0):
        return lax.dynamic_index_in_dim(v, index, axis, keepdims=False)

    row = jnp.arange(ROWS)
    token = (s ^ (row // PAD)) * TOK + row % PAD
    real = row % PAD < TOK
    t_r, t_c = token // WIN, token % WIN
    slot = pick(slot_window, s)
    ok = (
        real
        & (slot >= 0)
        & (slot // NWS * WIN + t_r < GRID)
        & (slot % NWS * WIN + t_c < GRID)
    ).astype(F32)[:, None]
    ones = jnp.ones((ROWS, 1), F32)
    near_offset = jnp.arange(WIN)[:, None] - jnp.arange(WIN)[None, :] + WIN - 1
    height = rel_height[near_offset].reshape(WIN * WIN, HD).T
    width = rel_width[near_offset].reshape(WIN * WIN, HD).T
    gap = jnp.zeros((HD, TAB // 2 - WIN * WIN), BF)
    flat = jnp.concatenate([height, gap, width, gap], axis=1)
    blank = jnp.zeros_like(flat)
    table = jnp.stack([jnp.concatenate([flat, blank]), jnp.concatenate([blank, flat])])
    col = jnp.arange(TAB)
    in_half = col % (TAB // 2)
    col_from = jnp.where(in_half < WIN * WIN, in_half // WIN, -1)
    spot = (
        jnp.where(col[None, :] < TAB // 2, t_r[:, None], t_c[:, None]) == col_from[None, :]
    ).astype(F32)
    col_to = jnp.where(in_half < WIN * WIN, in_half % WIN + WIN * (col // (TAB // 2)), -1)
    fold = (col_to[:, None] == jnp.arange(LANES)[None, :]).astype(BF)
    lanes = jnp.arange(LANES)[None, :]
    keys = (
        real[:, None] & ((lanes == t_r[:, None]) | (lanes == WIN + t_c[:, None]))
    ).astype(BF)
    key_bias = jnp.where(real, 0.0, NEG).astype(F32)[None, :]
    tables = (table, spot, fold, keys, key_bias)
    gain_one, bias_one = first_gain[None], first_bias[None]
    gain_two, bias_two = second_gain[None], second_bias[None]

    def along_z(piece):
        return [to_z(piece, k) for k in (1, 2, 3)]

    def in_plane(first):
        second = to_plane(first, plane_one)
        third = to_plane(first, plane_two)
        fourth = to_plane(second, plane_two)
        return first, second, third, fourth

    def exchange(parts, after=()):
        near, both, far = parts
        one = to_plane(both, plane_one)
        send = pair_up(far, one, after)
        return near, one, to_plane(send, plane_two), send

    ho_piece, qp_piece = pieces(where, qkv_weight, proj_weight, hidden_weight, output_weight)
    z_qp = along_z(qp_piece)
    tokens_cut = cut(where, image_tokens, cotangent, after=[qp_piece])
    ho_one = swap_z(ho_piece, 1)
    first_qp = join(z_qp, after=[tokens_cut[0]])
    got_qp = in_plane(first_qp)
    ho_pair = both_of(ho_piece, ho_one, after=[first_qp])
    ho_two = swap_z(ho_pair, 2)
    near, one, two, mid = exchange(tokens_cut, after=[got_qp[1], ho_pair])
    first_ho = join_ho(ho_one, ho_two, after=[mid])
    own = weld(where, ok, near, one, two, after=got_qp[1:] + (first_ho,))
    other = to_core(own)
    got_ho = in_plane(first_ho)
    w_qp, proj_send = call(
        place_qp_kernel,
        "place_qp",
        [(where, SMEM), (qkv_weight, HBM), (proj_weight, HBM)] + [(v, ANY) for v in got_qp],
        [
            (array((4, 4, PIECE, WIDE)), None),
            (array((2, 4, PIECE, HALF)), None),
        ],
        scratch=[pltpu.SemaphoreType.DMA((28,))],
        after=[own],
    )
    w_qp = w_qp.reshape(D, WIDE)
    proj_other = to_core(proj_send.reshape(HALF, HALF))
    normed = norm_one(ok, own, other, gain_one, bias_one, after=[w_qp])
    packed, attended, probs, low, branch_other = attn_fwd(
        where, 1, normed, w_qp, proj_other, qkv_bias[None], tables
    )
    packed, attended, probs, low, branch = attn_fwd(
        where, 0, normed, w_qp, proj_other, qkv_bias[None], tables,
        before=(packed, attended, probs, low), after=[got_ho[1]],
    )
    there = to_core(low)
    w_ho = call(
        place_ho_kernel,
        "place_ho",
        [(where, SMEM), (hidden_weight, HBM), (output_weight, HBM)] + [(v, ANY) for v in got_ho],
        [(array((4, 4, 4 * PIECE, D)), None)],
        scratch=[pltpu.SemaphoreType.DMA((32,))],
        after=[packed],
    )[0].reshape(16, 4 * PIECE, D)
    middle, second = norm_two(
        own, other, branch, branch_other, there, proj_bias[None], gain_two, bias_two, after=[w_ho]
    )
    active, slope = hidden_layer(where, second, w_ho, hidden_bias[None])

    def natural(keep_two, send_two):
        out = jnp.zeros((2, 4, 96, WIDE), BF)
        for q, part in ((s, keep_two[0]), (b, keep_two[1]), (a, send_two[0]), (s ^ 3, send_two[1])):
            out = lax.dynamic_update_index_in_dim(out, part, q, 1)
        return out.astype(F32)

    def sum_rows(full):
        return lax.psum_scatter(full, ("dp", "seq", "fsdp"), scatter_dimension=0, tiled=True)

    def spread_cols(grad, parts):
        grad = grad.reshape(D, parts, HALF)
        zero = jnp.zeros_like(grad)
        return jnp.where(
            c == 0, jnp.stack([grad, zero], axis=2), jnp.stack([zero, grad], axis=2)
        ).reshape(D, 2 * parts * HALF)

    def larger_wide(keep_two, send_two):
        return sum_rows(spread_cols(natural(keep_two, send_two).reshape(D, WIDE), 4))

    def larger_qp(keep_two, send_two):
        grad = natural(keep_two, send_two)
        qkv = sum_rows(spread_cols(grad[..., :QKV].reshape(D, QKV), 3))
        proj = jnp.concatenate(list(grad[..., QKV:].reshape(2, HALF, HALF)), axis=1)
        zero = jnp.zeros_like(proj)
        proj = jnp.where(c == 0, jnp.concatenate([proj, zero]), jnp.concatenate([zero, proj]))
        return qkv, sum_rows(proj)

    def step_one(send):
        return to_plane(send, plane_one)

    def step_two(parts, after=()):
        stay, send = add_one(parts, after)
        return stay, to_plane(send, plane_two), send

    def step_three(stay, got, after=()):
        keep, send = add_two(where, stay, got, after)
        return keep, swap_z(send, 1), send

    def step_four(keep, got, after=()):
        stay, send = add_three(keep, got, after)
        return stay, swap_z(send, 2), send

    def step_five(stay, got, after=()):
        total, send = add_four(where, stay, got, after)
        return total, to_core(send), send

    pair = n_dp == 2

    o_keep, o_send = weight_grad(where, [own, other], active)
    o_got = step_one(o_send) if pair else o_send
    grad_pre, part, part_low, hidden_sums = grad_pre_of(own, other, slope, w_ho, after=[o_send])
    part_there = to_core(part_low)
    h_keep, h_send = weight_grad(where, [second], grad_pre)
    h_got = step_one(h_send) if pair else h_send
    grad_middle, grad_branch, sums_two = norm_two_back(
        part, part_there, middle, gain_two, own, other, after=[h_send]
    )
    grad_packed, tab_grad, qkv_sums = attn_bwd(
        where, 0, packed, grad_branch, probs, w_qp, proj_other, tables
    )
    held = [grad_packed]
    if pair:
        oh_stay, oh_got, mid = step_two([(o_keep, o_got), (h_keep, h_got)], after=held)
        held = [mid]
    grad_packed, tab_grad_b, qkv_sums_b = attn_bwd(
        where, 1, packed, grad_branch, probs, w_qp, proj_other, tables,
        before=(grad_packed,), after=held,
    )
    q_keep, q_send = weight_grad_qp(where, normed, grad_packed, attended, grad_branch)
    held = [q_send]
    if pair:
        q_got = step_one(q_send)
        oh_keep, oh_got, mid = step_three(oh_stay, oh_got, after=held)
        held = [mid]
    back, back_low = product(
        "back", grad_packed, w_qp, pl.BlockSpec((D, QKV), lambda w: (0, 0)),
        lambda left, right: mm(left, right[...], ((1,), (1,))), after=held,
    )
    back_there = to_core(back_low)
    feed, feed_low = product(
        "feed", active, w_ho, None, lambda left, right: mm(left, output_part(right)),
        after=[back_low],
    )
    feed_there = to_core(feed_low)
    held = [feed_low]
    if pair:
        q_stay, q_got, mid = step_two([(q_keep, q_got)], after=held)
        held = [mid]
    *parts, sums_one = last(
        where, ok, back, back_there, own, gain_one, grad_middle, middle, feed, feed_there,
        output_bias[None], after=held,
    )
    to_offset = jnp.pad(
        (near_offset.reshape(-1)[None, :] == jnp.arange(2 * WIN - 1)[:, None]).astype(F32),
        ((0, 32 - (2 * WIN - 1)), (0, TAB // 2 - WIN * WIN)),
    )
    ins = (sums_two, sums_one, hidden_sums, qkv_sums, qkv_sums_b, tab_grad, tab_grad_b, to_offset)
    small = call(
        small_kernel,
        "small",
        [(where, SMEM)] + [(v, None) for v in ins],
        [(array((32, D), F32), None)],
    )[0]
    small_got = to_core(small)
    held = [small]
    if pair:
        oh_stay, oh_got, mid = step_four(oh_keep, oh_got, after=held)
        q_keep, q_got, mid = step_three(q_stay, q_got, after=[mid])
        held = [mid]
    small = tally([small, small_got], after=held)
    small_got = to_seq(small, 1)
    *parts, mid = exchange(parts, after=[small])
    small = tally([small, small_got], after=[mid])
    small_got = to_seq(small, 2)
    held = [small]
    if pair:
        q_stay, q_got, mid = step_four(q_keep, q_got, after=held)
        oh_total, oh_there, mid = step_five(oh_stay, oh_got, after=[mid])
        held = [mid]
    small = tally([small, small_got], after=held)
    small_got = swap_z(small, 1)
    input_grad, block_out = home(where, *parts, after=[small])
    small = tally([small, small_got], after=[input_grad])
    small_got = swap_z(small, 2)
    held = [small]
    if pair:
        q_total, q_there, mid = step_five(q_stay, q_got, after=held)
        held = [mid]
    small = tally([small, small_got], after=held)
    if pair:
        g_output, g_hidden, g_qkv, g_proj = finish(
            where, oh_total, oh_there, q_total, q_there, after=[small]
        )
        g_output = g_output.T
    else:
        g_output = larger_wide(o_keep, o_send).T
        g_hidden = larger_wide(h_keep, h_send)
        g_qkv, g_proj = larger_qp(q_keep, q_send)
    if n_dp > 2:
        groups = [list(range(core, n_dp, 2)) for core in range(2)]
        small = lax.psum(small, "dp", axis_index_groups=groups)
    (
        d_qkv_bias, d_height, d_width, d_proj_bias, d_gain_two, d_bias_two, d_hidden_bias,
        d_output_bias, d_gain_one, d_bias_one,
    ) = unpack(small)
    return (
        block_out,
        input_grad,
        d_gain_one,
        d_bias_one,
        g_qkv,
        d_qkv_bias,
        d_height,
        d_width,
        g_proj,
        d_proj_bias,
        d_gain_two,
        d_bias_two,
        g_hidden,
        d_hidden_bias,
        g_output,
        d_output_bias,
    )


def solution(mesh):
    tokens = P("dp", "fsdp", "seq", None)
    rows = P("fsdp", None)
    every = P(("dp", "seq", "fsdp"), None)
    args = (tokens, P("fsdp"), P(), P(), rows, P(), P(), P(), rows)
    args += (P(), P(), P(), rows, P(), rows, P(), tokens)
    outs = (tokens, tokens, P(), P(), every, P(), P(), P(), every)
    outs += (P(), P(), P(), every, P(), P(None, ("dp", "seq", "fsdp")), P())
    return jax.shard_map(
        functools.partial(per_device, mesh.shape["dp"]),
        mesh=mesh,
        in_specs=args,
        out_specs=outs,
        check_vma=False,
    )
```

```python
import functools

import jax
import jax.numpy as jnp
from jax import lax
from jax.experimental import pallas as pl
from jax.experimental.pallas import tpu as pltpu
from jax.sharding import PartitionSpec as P

D = 768
HD = 64
FF = 3072
WIN = 14
GRID = 48
NWS = 4
TOK = 49
PAD = 56
ROWS = 4 * PAD
SPLIT = 4 * TOK
HALF = D // 2
QKV = 3 * HALF
WIDE = 4 * HALF
PIECE = 48
PAIRS = 3
LANES = 128
TAB = 512
NEG = -1e30
EPS = 1e-06
SCALE = HD**-0.5
BF = jnp.bfloat16
F32 = jnp.float32
ANY = pl.BlockSpec(memory_space=pl.ANY)
HBM = pl.BlockSpec(memory_space=pltpu.HBM)
SMEM = pl.BlockSpec(memory_space=pltpu.SMEM)


def mm(left, right, dims=((1,), (0,))):
    return lax.dot_general(left, right, (dims, ((), ())), preferred_element_type=F32)


def array(shape, dtype=BF):
    return jax.ShapeDtypeStruct(shape, dtype)


def whole(shape):
    return pl.BlockSpec(shape, lambda *at: (0,) * len(shape))


def window(shape, index=None):
    index = index or (lambda w: w)
    return pl.BlockSpec((1,) + shape, lambda w: (index(w),) + (0,) * len(shape))


TIMES = dict(
    add_four0=1, add_four1=0.1, add_one1=8, add_two0=3, add_two1=1, attn_bwd0=1, attn_bwd1=1, attn_fwd1=1,
    back0=8, both_of0=3, cut0=3, feed0=1, grad_pre0=50, join0=0.3, join_ho0=20, last0=20, norm_one0=0.3,
    norm_two0=3, norm_two_back0=20, pair_up0=0.3, pair_up1=50, place_qp0=87, small0=0.3, tables0=3, tally0=8,
    tally3=500, tally4=8, unpack0=3, weight_grad1=50, weld0=0.3,
)


COUNT = {}


def call(kernel, name, ins, outs, grid=(), scratch=(), after=(), vmem=8, alias=()):
    count = len(ins)
    extra = len(after)
    at = COUNT.get(name, 0)
    COUNT[name] = at + 1
    cost = TIMES.get(name + str(at), 87.0)

    def held(v):
        mode = pl.Buffered(1) if grid else None
        return pl.BlockSpec(v.shape, lambda *at: (0,) * len(v.shape), pipeline_mode=mode)

    def body(*refs):
        return kernel(*refs[:count], *refs[count + extra :])

    return pl.pallas_call(
        body,
        grid=grid,
        in_specs=[spec or held(v) for v, spec in ins] + [ANY] * extra,
        out_specs=[spec or whole(v.shape) for v, spec in outs],
        out_shape=[v for v, _ in outs],
        scratch_shapes=list(scratch),
        compiler_params=pltpu.CompilerParams(vmem_limit_bytes=vmem * 1024 * 1024),
        input_output_aliases=dict(alias),
        cost_estimate=pl.CostEstimate(
            flops=int(1.15e9 * cost),
            bytes_accessed=int(1.15e6 * cost),
            transcendentals=0,
        ),
        name=name,
    )(*[v for v, _ in ins], *after)


def pieces_kernel(where, qkv, proj, hidden, output, out, qp_out, sems):
    s, c = where[1], where[5]
    rows = pl.ds(pl.multiple_of(s * PIECE, PIECE), PIECE)
    start = pl.multiple_of(c * HALF + s * 2 * PIECE, 2 * PIECE)
    copies = [(output.at[pl.ds(start, 2 * PIECE)], out.at[: 2 * PIECE])]
    for i in range(4):
        cols = pl.ds(pl.multiple_of(i * D + c * HALF, LANES), HALF)
        at = (2 + i // 2) * PIECE
        half = slice(i % 2 * HALF, (i % 2 + 1) * HALF)
        copies.append((hidden.at[rows, cols], out.at[at : at + PIECE, half]))
    for i in range(3):
        cols = pl.ds(pl.multiple_of(i * D + c * HALF, LANES), HALF)
        copies.append((qkv.at[rows, cols], qp_out.at[:, i * HALF : (i + 1) * HALF]))
    cols = pl.ds(pl.multiple_of(c * HALF, LANES), HALF)
    copies.append((proj.at[rows, cols], qp_out.at[:, QKV:]))
    run_copies(copies, sems)


def run_copies(pairs, sems):
    copies = [
        pltpu.make_async_copy(src, dst, sems.at[n]) for n, (src, dst) in enumerate(pairs)
    ]
    for copy in copies:
        copy.start()
    for copy in copies:
        copy.wait()


def pieces(where, qkv, proj, hidden, output):
    return call(
        pieces_kernel,
        "pieces",
        [(where, SMEM), (qkv, HBM), (proj, HBM), (hidden, HBM), (output, HBM)],
        [(array((4 * PIECE, D)), None), (array((PIECE, WIDE)), None)],
        scratch=[pltpu.SemaphoreType.DMA((9,))],
        vmem=60,
    )


def output_part(w, first=0, count=16):
    return w[first : first + count, : 2 * PIECE, :].reshape(count * 2 * PIECE, D)


def hidden_part(w, half):
    at = (2 + half) * PIECE
    return w[:, at : at + PIECE, :].reshape(D, D)


def join_kernel(one, two, three, out):
    out[0] = one[...]
    out[1] = two[...]
    out[2] = three[...]


def join(parts, after=()):
    return call(
        join_kernel,
        "join",
        [(part, None) for part in parts],
        [(array((3,) + parts[0].shape), None)],
        after=after,
    )[0]


def both_kernel(one, two, out):
    out[0] = one[...]
    out[1] = two[...]


def both_of(one, two, after=()):
    return call(
        both_kernel,
        "both_of",
        [(one, None), (two, None)],
        [(array((2,) + one.shape), None)],
        after=after,
    )[0]


def join_ho_kernel(one, two, out):
    out[0] = one[...]
    out[1] = two[0]
    out[2] = two[1]


def join_ho(one, two, after=()):
    return call(
        join_ho_kernel,
        "join_ho",
        [(one, None), (two, None)],
        [(array((3,) + one.shape), None)],
        after=after,
    )[0]


def place_qp_kernel(where, qkv, proj, first, second, third, fourth, out, send, sems):
    z, c = where[0], where[5]
    copies = []

    def add(src, dst):
        copies.append(pltpu.make_async_copy(src, dst, sems.at[len(copies)]))

    for i in range(3):
        for q in range(4):
            cols = pl.ds(pl.multiple_of(i * D + c * HALF, LANES), HALF)
            add(
                qkv.at[q * PIECE : (q + 1) * PIECE, cols],
                out.at[z, q, :, i * HALF : (i + 1) * HALF],
            )
    for q in range(4):
        cols = pl.ds(pl.multiple_of(c * HALF, LANES), HALF)
        add(proj.at[q * PIECE : (q + 1) * PIECE, cols], out.at[z, q, :, QKV:])
    for i in range(3):
        zz = lax.rem(z + 3 - i, 4)
        for n, src in enumerate((first, second, third, fourth)):
            add(src.at[i], out.at[zz, where[1 + n]])
    for copy in copies:
        copy.start()
    for copy in copies:
        copy.wait()
    send[...] = out[pl.ds(2 * (1 - c), 2), :, :, QKV:]


def place_ho_kernel(where, hidden, output, first, second, third, fourth, out, sems):
    z, c = where[0], where[5]
    copies = []
    for q in range(4):
        start = pl.multiple_of(c * HALF + q * 2 * PIECE, 2 * PIECE)
        copies.append((output.at[pl.ds(start, 2 * PIECE)], out.at[z, q, : 2 * PIECE]))
        for i in range(4):
            cols = pl.ds(pl.multiple_of(i * D + c * HALF, LANES), HALF)
            at = (2 + i // 2) * PIECE
            half = slice(i % 2 * HALF, (i % 2 + 1) * HALF)
            copies.append(
                (
                    hidden.at[q * PIECE : (q + 1) * PIECE, cols],
                    out.at[z, q, at : at + PIECE, half],
                )
            )
    for i in range(3):
        zz = z ^ (i + 1)
        for n, src in enumerate((first, second, third, fourth)):
            copies.append((src.at[i], out.at[zz, where[1 + n]]))
    run_copies(copies, sems)


def hand_out(c, rows, i, outs):
    near, both, far = outs

    def piece(k):
        return rows[pl.ds(pl.multiple_of(k * PAD, 8), PAD), :].astype(BF)

    near[i] = piece(0)
    both[0, i] = piece(1 + c)
    both[1, i] = piece(3)
    far[i] = piece(2 - c)


def handed(images):
    shape = (images, PAD, D)
    return [(array(shape), None), (array((2,) + shape), None), (array(shape), None)]


ROWS_F32 = pltpu.VMEM((ROWS, D), F32)


def gathered_rows(c, near, one, two, i):
    first, second = one[0, i].astype(F32), two[0, i].astype(F32)
    parts = [near[i].astype(F32)]
    parts += [jnp.where(c == 0, first, second), jnp.where(c == 0, second, first)]
    return jnp.concatenate(parts + [two[1, i].astype(F32)])


def pair_kernel(far, one, out):
    out[0] = far[...]
    out[1] = one[1]


def pair_up(far, one, after=()):
    return call(
        pair_kernel,
        "pair_up",
        [(far, None), (one, None)],
        [(array((2,) + far.shape), None)],
        after=after,
    )[0]


def cut_kernel(where, tokens, cotangent, *rest):
    s, c = where[1], where[5]
    images = tokens.shape[0]
    outs, rows = rest[:3], rest[3]
    row = lax.broadcasted_iota(jnp.int32, (ROWS, SPLIT), 0)
    col = lax.broadcasted_iota(jnp.int32, (ROWS, SPLIT), 1)
    token = row % PAD
    take = ((token < TOK) & (col == token * 4 + (s ^ (row // PAD)))).astype(F32).astype(BF)
    for i in range(2 * images):
        rows[...] = mm(take, tokens[i] if i < images else cotangent[i - images])
        hand_out(c, rows, i, outs)


def cut(where, tokens, cotangent, after=()):
    images = tokens.shape[0]
    flat = [jnp.transpose(v, (0, 2, 1, 3)).reshape(images, SPLIT, D) for v in (tokens, cotangent)]
    return call(
        cut_kernel,
        "cut",
        [(where, SMEM)] + [(v, None) for v in flat],
        handed(2 * images),
        scratch=[ROWS_F32],
        after=after,
        vmem=12,
    )


def weld_kernel(where, ok, near, one, two, out):
    count = out.shape[0]
    for i in range(count):
        rows = gathered_rows(where[5], near, one, two, i)
        out[i] = (rows if i < count // 2 else rows * ok[...]).astype(BF)


def weld(where, ok, near, one, two, after=()):
    return call(
        weld_kernel,
        "weld",
        [(where, SMEM), (ok, None)] + [(part, None) for part in (near, one, two)],
        [(array((near.shape[0], ROWS, D)), None)],
        after=after,
    )[0]


def home_kernel(where, near, one, two, *outs):
    s = where[1]
    row = lax.broadcasted_iota(jnp.int32, (SPLIT, ROWS), 0)
    col = lax.broadcasted_iota(jnp.int32, (SPLIT, ROWS), 1)
    token = col % PAD
    take = ((token < TOK) & (row == token * 4 + (s ^ (col // PAD)))).astype(F32).astype(BF)
    images = outs[0].shape[0]
    for i in range(2 * images):
        rows = gathered_rows(where[5], near, one, two, i).astype(BF)
        outs[i // images][i % images] = mm(take, rows).astype(BF)


def home(where, near, one, two, after=()):
    images = near.shape[0] // 2
    flat = call(
        home_kernel,
        "home",
        [(where, SMEM)] + [(part, None) for part in (near, one, two)],
        [(array((images, SPLIT, D)), None)] * 2,
        after=after,
        vmem=12,
    )
    return [jnp.transpose(v.reshape(images, TOK, 4, D), (0, 2, 1, 3)) for v in flat]


def unit_of(v):
    v = v - jnp.mean(v, axis=-1, keepdims=True)
    rstd = lax.rsqrt(jnp.mean(v * v, axis=-1, keepdims=True) + EPS)
    return v * rstd, rstd


def norm_back(grad, unit, rstd):
    return rstd * (
        grad
        - jnp.mean(grad, axis=-1, keepdims=True)
        - unit * jnp.mean(grad * unit, axis=-1, keepdims=True)
    )


def norm_one_kernel(ok, own, other, gain, shift, out):
    images = own.shape[0] // 2
    for w in range(2 * images):
        x = own[w] if w < images else other[w - images]
        unit, _ = unit_of(x.astype(F32))
        out[w] = ((unit * gain[...] + shift[...]) * ok[...]).astype(BF)


def norm_one(ok, own, other, gain, shift, after=()):
    return call(
        norm_one_kernel,
        "norm_one",
        [(v, None) for v in (ok, own, other, gain, shift)],
        [(array(own.shape), None)],
        after=after,
        vmem=12,
    )[0]


def norm_two_kernel(
    own, other, branch, branch_other, there, bias, gain, shift, middle, second
):
    images = own.shape[0] // 2
    for w in range(2 * images):
        x, mine = (own, branch) if w < images else (other, branch_other)
        at = w % images
        value = x[at].astype(F32) + (mine[at] + there[w].astype(F32)) + bias[...]
        middle[w] = value
        unit, _ = unit_of(value)
        second[w] = (unit * gain[...] + shift[...]).astype(BF)


def norm_two(own, other, branch, branch_other, there, bias, gain, shift, after=()):
    shape = own.shape
    ins = (own, other, branch, branch_other, there, bias, gain, shift)
    return call(
        norm_two_kernel,
        "norm_two",
        [(v, None) for v in ins],
        [(array(shape, F32), None), (array(shape), None)],
        after=after,
        vmem=14,
    )


def norm_two_back_kernel(
    images, part, there, middle, gain, feed, feed_other, grad_middle, grad_branch, sums
):
    sums[...] = jnp.zeros_like(sums)
    for w in range(2 * images):
        grad = part[w] + there[w].astype(F32)
        unit, rstd = unit_of(middle[w])
        feed_w = (feed[images + w] if w < images else feed_other[w]).astype(F32)
        total = feed_w + norm_back(grad * gain[...], unit, rstd)
        low = total.astype(BF)
        grad_branch[w] = low
        if w < images:
            grad_middle[w] = total
            sums[0:1] += jnp.sum(grad * unit, axis=0, keepdims=True)
            sums[1:2] += jnp.sum(grad, axis=0, keepdims=True)
            sums[2:3] += jnp.sum(low.astype(F32), axis=0, keepdims=True)
            sums[3:4] += jnp.sum(feed_w, axis=0, keepdims=True)


def norm_two_back(part, there, middle, gain, feed, feed_other, after=()):
    count = part.shape[0]
    return call(
        functools.partial(norm_two_back_kernel, count // 2),
        "norm_two_back",
        [(v, None) for v in (part, there, middle, gain, feed, feed_other)],
        [
            (array((count // 2, ROWS, D), F32), None),
            (array((count, ROWS, D)), None),
            (array((8, D), F32), None),
        ],
        after=after,
        vmem=16,
    )


def last_kernel(
    where, ok, back, back_there, own, gain, grad_middle, middle, feed, feed_there, bias, *rest
):
    outs, sums, rows = rest[:3], rest[3], rest[4]
    images = back.shape[0]
    sums[...] = jnp.zeros_like(sums)
    for w in range(images):
        grad = (back[w] + back_there[w].astype(F32)) * ok[...]
        unit, rstd = unit_of(own[w].astype(F32))
        sums[0:1] += jnp.sum(grad * unit, axis=0, keepdims=True)
        sums[1:2] += jnp.sum(grad, axis=0, keepdims=True)
        rows[...] = grad_middle[w] + norm_back(grad * gain[...], unit, rstd)
        hand_out(where[5], rows, w, outs)
        rows[...] = (middle[w] + feed[w] + feed_there[w].astype(F32) + bias[...]) * ok[...]
        hand_out(where[5], rows, images + w, outs)


def last(where, ok, back, back_there, own, gain, grad_middle, middle, feed, feed_there, bias, after=()):
    ins = (ok, back, back_there, own, gain, grad_middle, middle, feed, feed_there, bias)
    return call(
        last_kernel,
        "last",
        [(where, SMEM)] + [(v, None) for v in ins],
        handed(own.shape[0]) + [(array((8, D), F32), None)],
        scratch=[ROWS_F32],
        after=after,
        vmem=20,
    )


def attn_fwd_kernel(
    where, normed, w_qp, other, b_qkv, table, spot, fold, keys, bias, *rest
):
    packed, out, probs, low, branch = rest[-5:]
    c = where[5]
    lane = lax.broadcasted_iota(jnp.int32, (ROWS, LANES), 1)
    shift = [b_qkv[:, pl.ds(pl.multiple_of(i * D + c * HALF, LANES), HALF)] for i in range(3)]
    packed[0] = (mm(normed[0], w_qp[:, :QKV]) + jnp.concatenate(shift, axis=1)).astype(BF)

    def columns(part, pair):
        at = part * HALF + pair * LANES
        return packed[0, :, at : at + LANES]

    queries = jnp.concatenate([columns(0, pair) for pair in range(PAIRS)])
    mask = jnp.concatenate([spot[...]] * PAIRS)
    rels = [mm((mm(queries, table[e]) * mask).astype(BF), fold[...]).astype(BF) for e in range(2)]
    for pair in range(PAIRS):
        q, k, v = columns(0, pair), columns(1, pair), columns(2, pair)
        right = jnp.concatenate([k, keys[...]], axis=1)
        parts = []
        for e in range(2):
            mine = (lane < HD) if e == 0 else (lane >= HD)
            rel = rels[e][pair * ROWS : (pair + 1) * ROWS]
            scaled = jnp.where(mine, q.astype(F32) * SCALE, 0.0).astype(BF)
            left = jnp.concatenate([scaled, rel], axis=1)
            s = mm(left, right, ((1,), (1,))) + bias[...]
            p = jnp.exp(s - jnp.max(s, axis=1, keepdims=True))
            p = (p * (1.0 / jnp.sum(p, axis=1, keepdims=True))).astype(BF)
            probs[0, 2 * pair + e] = p
            parts.append(mm(p, v))
        out[0, :, pair * LANES : (pair + 1) * LANES] = jnp.where(
            lane < HD, parts[0], parts[1]
        ).astype(BF)
    att = out[0]
    own_cols = pl.ds(pl.multiple_of(c * HALF, LANES), HALF)
    other_cols = pl.ds(pl.multiple_of((1 - c) * HALF, LANES), HALF)
    own_rows = pl.ds(pl.multiple_of(c * HALF, HALF), HALF)
    mine = mm(att, w_qp[own_rows, QKV:])
    theirs = mm(att, other[...])
    branch[0, :, own_cols] = mine
    branch[0, :, other_cols] = theirs
    low[0, :, own_cols] = mine.astype(BF)
    low[0, :, other_cols] = theirs.astype(BF)


def attn_fwd(where, group, normed, w_qp, other, b_qkv, tables, before=(), after=()):
    table, spot, fold, keys, bias = tables
    count = normed.shape[0]
    half = count // 2
    start = group * half
    ins = [(where, SMEM), (normed, window((ROWS, D), lambda w: w + start))]
    ins += [(v, None) for v in (w_qp, other, b_qkv, table, spot, fold, keys, bias)]
    kept = ((ROWS, QKV), (ROWS, HALF), (2 * PAIRS, ROWS, ROWS))
    outs = [(array((count,) + shape), window(shape, lambda w: w + start)) for shape in kept]
    outs += [
        (array((count, ROWS, D)), window((ROWS, D), lambda w: (w + start + half) % count)),
        (array((half, ROWS, D), F32), window((ROWS, D))),
    ]
    return call(
        attn_fwd_kernel,
        "attn_fwd",
        ins + [(v, ANY) for v in before],
        outs,
        grid=(half,),
        after=after,
        alias=[(len(ins) + n, n) for n in range(len(before))],
        vmem=18,
    )


def attn_bwd_kernel(
    where, packed, grad_branch, probs, w_qp, other, table, spot, fold, keys, *rest
):
    out, tab_grad, sums, att = rest[-4:]
    c = where[5]
    lane = lax.broadcasted_iota(jnp.int32, (ROWS, LANES), 1)
    lane_t = lax.broadcasted_iota(jnp.int32, (TAB, LANES), 1)

    @pl.when(pl.program_id(0) == 0)
    def _():
        tab_grad[...] = jnp.zeros_like(tab_grad)
        sums[...] = jnp.zeros_like(sums)

    own_cols = pl.ds(pl.multiple_of(c * HALF, LANES), HALF)
    other_cols = pl.ds(pl.multiple_of((1 - c) * HALF, LANES), HALF)
    own_rows = pl.ds(pl.multiple_of(c * HALF, HALF), HALF)
    att[...] = (
        mm(grad_branch[0, :, own_cols], w_qp[own_rows, QKV:], ((1,), (1,)))
        + mm(grad_branch[0, :, other_cols], other[...], ((1,), (1,)))
    ).astype(BF)
    def columns(part, pair):
        at = part * HALF + pair * LANES
        return packed[0, :, at : at + LANES]

    queries = jnp.concatenate([columns(0, pair) for pair in range(PAIRS)])
    mask = jnp.concatenate([spot[...]] * PAIRS)
    both, dk, dv = [[], []], [[], []], [[], []]
    for pair in range(PAIRS):
        q, k, v = columns(0, pair), columns(1, pair), columns(2, pair)
        go = att[:, pair * LANES : (pair + 1) * LANES]
        right = jnp.concatenate([k, keys[...]], axis=1)
        for e in range(2):
            mine = (lane < HD) if e == 0 else (lane >= HD)
            go_e = jnp.where(mine, go.astype(F32), 0.0).astype(BF)
            p_low = probs[0, 2 * pair + e]
            p = p_low.astype(F32)
            dp = mm(go_e, v, ((1,), (1,)))
            ds = (p * (dp - jnp.sum(dp * p, axis=1, keepdims=True))).astype(BF)
            both[e].append(mm(ds, right))
            dk[e].append(SCALE * mm(ds, q, ((0,), (0,))))
            dv[e].append(mm(p_low, go, ((0,), (0,))))
    dq, dt = [], []
    for e in range(2):
        rel = jnp.concatenate([part[:, LANES:] for part in both[e]]).astype(BF)
        spread = (mm(rel, fold[...], ((1,), (1,))) * mask).astype(BF)
        flat = jnp.concatenate([part[:, :LANES] for part in both[e]])
        dq.append(SCALE * flat + mm(spread, table[e], ((1,), (1,))))
        dt.append(mm(spread, queries, ((0,), (0,))))
    tab_grad[...] += jnp.where(lane_t < HD, dt[0], dt[1])
    for pair in range(PAIRS):
        rows = slice(pair * ROWS, (pair + 1) * ROWS)
        pairs = ((dq[0][rows], dq[1][rows]), (dk[0][pair], dk[1][pair]), (dv[0][pair], dv[1][pair]))
        for part, two in enumerate(pairs):
            low = jnp.where(lane < HD, two[0], two[1]).astype(BF)
            cols = slice(part * HALF + pair * LANES, part * HALF + (pair + 1) * LANES)
            out[0, :, cols] = low
            sums[0:1, cols] += jnp.sum(low.astype(F32), axis=0, keepdims=True)


def attn_bwd(where, group, packed, grad_branch, probs, w_qp, other, tables, before=(), after=()):
    table, spot, fold, keys, _ = tables
    count = packed.shape[0]
    half = count // 2
    start = group * half
    ins = [
        (where, SMEM),
        (packed, window((ROWS, QKV), lambda w: w + start)),
        (grad_branch, window((ROWS, D), lambda w: w + start)),
        (probs, window((2 * PAIRS, ROWS, ROWS), lambda w: w + start)),
    ]
    ins += [(v, None) for v in (w_qp, other, table, spot, fold, keys)]
    return call(
        attn_bwd_kernel,
        "attn_bwd",
        ins + [(v, ANY) for v in before],
        [
            (array((count, ROWS, QKV)), window((ROWS, QKV), lambda w: w + start)),
            (array((TAB, LANES), F32), None),
            (array((8, QKV), F32), None),
        ],
        grid=(half,),
        scratch=[pltpu.VMEM((ROWS, HALF), BF)],
        after=after,
        alias=[(len(ins) + n, n) for n in range(len(before))],
        vmem=18,
    )


def hidden_kernel(where, second, w, bias, active, slope):
    c = where[5]
    for half in range(2):
        cols = slice(half * D, (half + 1) * D)
        shift = [
            bias[:, pl.ds(pl.multiple_of(i * D + c * HALF, LANES), HALF)]
            for i in (2 * half, 2 * half + 1)
        ]
        v = mm(second[0], hidden_part(w, half)) + jnp.concatenate(shift, axis=1)
        phi = 0.5 * (1.0 + lax.erf(v * (0.5**0.5)))
        active[0, :, cols] = (v * phi).astype(BF)
        slope[0, :, cols] = (phi + v * (jnp.exp(-0.5 * v * v) * 0.3989422804014327)).astype(BF)


def hidden_layer(where, second, w_hidden, bias, after=()):
    count = second.shape[0]
    return call(
        hidden_kernel,
        "hidden",
        [(where, SMEM), (second, window((ROWS, D))), (w_hidden, None), (bias, None)],
        [(array((count, ROWS, WIDE)), window((ROWS, WIDE)))] * 2,
        grid=(count,),
        after=after,
        vmem=14,
    )


def product_kernel(of, count, left, right, own, low):
    w = pl.program_id(0)
    value = of(left[0], right)

    @pl.when(w < count // 2)
    def _():
        low[w] = value.astype(BF)

    @pl.when(w >= count // 2)
    def _():
        own[w - count // 2] = value


def product(name, left, right, right_spec, of, after=()):
    count = left.shape[0]
    shape = (count // 2, ROWS, D)
    return call(
        functools.partial(product_kernel, of, count),
        name,
        [(left, window(left.shape[1:], lambda w: (w + count // 2) % count)), (right, right_spec)],
        [(array(shape, F32), None), (array(shape), None)],
        grid=(count,),
        after=after,
        vmem=14,
    )


def grad_pre_kernel(count, own, other, slope, w, out, part, low, sums):
    feed = jnp.where(pl.program_id(0) < count // 2, own[0].astype(F32), other[0].astype(F32))
    feed = feed.astype(BF)

    @pl.when(pl.program_id(0) == 0)
    def _():
        sums[...] = jnp.zeros_like(sums)

    for half in range(2):
        cols = slice(half * D, (half + 1) * D)
        value = mm(feed, output_part(w, 8 * half, 8), ((1,), (1,))) * slope[0, :, cols].astype(F32)
        value = value.astype(BF)
        out[0, :, cols] = value
        sums[0:1, cols] += jnp.sum(value.astype(F32), axis=0, keepdims=True)
    value = mm(out[0, :, :D], hidden_part(w, 0), ((1,), (1,)))
    value = value + mm(out[0, :, D:], hidden_part(w, 1), ((1,), (1,)))
    part[0] = value
    low[0] = value.astype(BF)


def grad_pre_of(own, other, slope, w, after=()):
    count = slope.shape[0]
    half = count // 2
    return call(
        functools.partial(grad_pre_kernel, count),
        "grad_pre",
        [
            (own, window((ROWS, D), lambda w: half + jnp.minimum(w, half - 1))),
            (other, window((ROWS, D), lambda w: half + jnp.maximum(w - half, 0))),
            (slope, window((ROWS, WIDE))),
            (w, None),
        ],
        [
            (array((count, ROWS, WIDE)), window((ROWS, WIDE))),
            (array((count, ROWS, D), F32), window((ROWS, D))),
            (array((count, ROWS, D)), window((ROWS, D), lambda w: (w + count // 2) % count)),
            (array((8, WIDE), F32), None),
        ],
        grid=(count,),
        after=after,
        vmem=18,
    )


def deal(where, total, keep, send, cols):
    for n, out in enumerate((keep, keep, send, send)):
        q = where[(1, 3, 2, 4)[n]]
        for h in range(2):
            rows = pl.ds(pl.multiple_of(h * HALF + q * 96, 8), 96)
            out[n % 2, h, :, cols] = total[rows, :].astype(BF)


def weight_grad_kernel(count, where, *refs):
    lefts, (right, keep, send, flip, total) = refs[:count], refs[count:]
    rows = right.shape[0] // count
    for n, left in enumerate(lefts):
        flip[:, n * rows : (n + 1) * rows] = left[left.shape[0] - rows :, :].T
    for at in range(0, WIDE, TAB):
        cols = slice(at, at + TAB)
        total[...] = mm(flip[...], right[:, cols])
        deal(where, total, keep, send, cols)


def weight_grad(where, lefts, right, after=()):
    rows = right.shape[0] * right.shape[1]
    shape = (2, 2, 96, WIDE)
    return call(
        functools.partial(weight_grad_kernel, len(lefts)),
        "weight_grad",
        [(where, SMEM)]
        + [(left.reshape(-1, D), None) for left in lefts]
        + [(right.reshape(rows, WIDE), None)],
        [(array(shape), None), (array(shape), None)],
        scratch=[pltpu.VMEM((D, rows), BF), pltpu.VMEM((D, TAB), F32)],
        after=after,
        vmem=16,
    )


def weight_grad_qp_kernel(
    where, normed, packed, att, branch, keep, send, flip, total, flip_att, total_att
):
    flip[...] = normed[...].T
    for at in range(0, QKV, HALF):
        cols = slice(at, at + HALF)
        total[...] = mm(flip[...], packed[:, cols])
        deal(where, total, keep, send, cols)
    flip_att[...] = att[...].T
    total_att[...] = mm(flip_att[...], branch[...])
    for n, out in enumerate((keep, keep, send, send)):
        q = where[(1, 3, 2, 4)[n]]
        rows = pl.ds(pl.multiple_of(q * 96, 8), 96)
        for h in range(2):
            out[n % 2, h, :, QKV:] = total_att[rows, h * HALF : (h + 1) * HALF].astype(BF)


def weight_grad_qp(where, normed, packed, att, branch, after=()):
    rows = normed.shape[0] * normed.shape[1]
    shape = (2, 2, 96, WIDE)
    return call(
        weight_grad_qp_kernel,
        "weight_grad_qp",
        [(where, SMEM)]
        + [(v.reshape(rows, v.shape[-1]), None) for v in (normed, packed, att, branch)],
        [(array(shape), None), (array(shape), None)],
        scratch=[
            pltpu.VMEM((D, rows), BF),
            pltpu.VMEM((D, HALF), F32),
            pltpu.VMEM((HALF, rows), BF),
            pltpu.VMEM((HALF, D), F32),
        ],
        after=after,
        vmem=16,
    )


def add_one_kernel(*refs):
    stay, send = refs[-2:]
    for i in range(len(refs) // 2 - 1):
        keep, got = refs[2 * i], refs[2 * i + 1]
        for h in range(2):
            for q in range(4):
                rows = slice(q * 24, (q + 1) * 24)
                stay[i, h, q] = keep[0, h, rows].astype(F32) + got[0, h, rows].astype(F32)
                total = keep[1, h, rows].astype(F32) + got[1, h, rows].astype(F32)
                send[i, h, q] = total.astype(BF)


def add_one(parts, after=()):
    shape = (len(parts), 2, 4, 24, WIDE)
    return call(
        add_one_kernel,
        "add_one",
        [(v, None) for part in parts for v in part],
        [(array(shape, F32), None), (array(shape), None)],
        after=after,
        vmem=16,
    )


def add_two_kernel(where, stay, got, keep, send):
    z = where[0]
    for i in range(stay.shape[0]):
        for n in range(2):
            mine, theirs = z ^ (2 * n), z ^ (2 * n + 1)
            for h in range(2):
                keep[n, i, h] = stay[i, h, mine] + got[i, h, mine].astype(F32)
                send[n, i, h] = (stay[i, h, theirs] + got[i, h, theirs].astype(F32)).astype(BF)


def add_two(where, stay, got, after=()):
    shape = (2, stay.shape[0], 2, 24, WIDE)
    return call(
        add_two_kernel,
        "add_two",
        [(where, SMEM), (stay, None), (got, None)],
        [(array(shape, F32), None), (array(shape), None)],
        after=after,
        vmem=14,
    )


def add_three_kernel(keep, got, stay, send):
    for i in range(stay.shape[0]):
        for h in range(2):
            stay[i, h] = keep[0, i, h] + got[0, i, h].astype(F32)
            send[i, h] = (keep[1, i, h] + got[1, i, h].astype(F32)).astype(BF)


def add_three(keep, got, after=()):
    shape = keep.shape[1:]
    return call(
        add_three_kernel,
        "add_three",
        [(keep, None), (got, None)],
        [(array(shape, F32), None), (array(shape), None)],
        after=after,
    )


def add_four_kernel(where, stay, got, total, send):
    for i in range(stay.shape[0]):
        for h in range(2):
            total[i, h] = stay[i, h] + got[i, h].astype(F32)
        send[i] = total[i, 1 - where[5]]


def add_four(where, stay, got, after=()):
    shape = (stay.shape[0],) + stay.shape[2:]
    return call(
        add_four_kernel,
        "add_four",
        [(where, SMEM), (stay, None), (got, None)],
        [(array(stay.shape, F32), None), (array(shape, F32), None)],
        after=after,
    )


def finish_kernel(where, two, two_there, total, there, output, hidden, qkv, proj):
    c = where[5]

    def lay(out, blocks, mine, theirs):
        for i in range(blocks):
            cols = slice(i * HALF, (i + 1) * HALF)
            out[:, pl.ds(pl.multiple_of(i * D + c * HALF, LANES), HALF)] = mine[:, cols]
            out[:, pl.ds(pl.multiple_of(i * D + (1 - c) * HALF, LANES), HALF)] = theirs[:, cols]

    lay(output, 4, two.at[0, c], two_there.at[0])
    lay(hidden, 4, two.at[1, c], two_there.at[1])
    lay(qkv, 3, total.at[0, c], there.at[0])
    for h in range(2):
        proj[:, h * HALF : (h + 1) * HALF] = total[0, h, :, QKV:]


def finish(where, two, two_there, total, there, after=()):
    return call(
        finish_kernel,
        "finish",
        [(where, SMEM)] + [(v, None) for v in (two, two_there, total, there)],
        [(array((24, blocks * D), F32), None) for blocks in (4, 4, 3, 1)],
        after=after,
    )


def small_kernel(where, two, one, hidden, qkv, qkv_b, tab, tab_b, to_offset, out):
    c = where[5]
    out[...] = jnp.zeros_like(out)
    cols = pl.ds(pl.multiple_of(c * HALF, LANES), HALF)
    for i in range(3):
        part = slice(i * HALF, (i + 1) * HALF)
        out[i : i + 1, cols] = qkv[0:1, part] + qkv_b[0:1, part]
    for i in range(4):
        out[3 + i : 4 + i, cols] = hidden[0:1, i * HALF : (i + 1) * HALF]
    for i in range(4):
        out[7 + i : 8 + i, :] = two[i : i + 1, :]
    for i in range(2):
        out[11 + i : 12 + i, :] = one[i : i + 1, :]
        half = slice(i * (TAB // 2), (i + 1) * (TAB // 2))
        rel = lax.dot_general(
            to_offset[...],
            tab[half, :] + tab_b[half, :],
            (((1,), (0,)), ((), ())),
            preferred_element_type=F32,
            precision=lax.Precision.HIGHEST,
        )
        for k in range(4):
            out[16 + 8 * i : 24 + 8 * i, k * LANES : (k + 1) * LANES] = rel[8 * k : 8 * k + 8]


def tally_kernel(*refs):
    if len(refs) == 3:
        refs[2][...] = refs[0][...] + refs[1][...]
    else:
        refs[4][...] = (refs[0][...] + refs[1][...]) + (refs[2][...] + refs[3][...])


def tally(parts, after=()):
    return call(
        tally_kernel,
        "tally",
        [(v, None) for v in parts],
        [(array(parts[0].shape, F32), None)],
        after=after,
    )[0]


def unpack_kernel(total, *outs):
    qkv, height, width, proj, gain_two, bias_two, hidden, output, gain_one, bias_one = outs
    for i in range(3):
        qkv[i * D : (i + 1) * D] = total[i, :]
    for i in range(4):
        hidden[i * D : (i + 1) * D] = total[3 + i, :]
    rows = (gain_two, bias_two, proj, output, gain_one, bias_one)
    for i, out in enumerate(rows):
        out[...] = total[7 + i, :]
    for i, out in enumerate((height, width)):
        at = slice(16 + 8 * i, 24 + 8 * i)
        rel = jnp.concatenate([total[at, k * LANES : (k + 1) * LANES] for k in range(4)])
        out[...] = (rel + pltpu.roll(rel, HD, 1))[: 2 * WIN - 1, :HD]


def unpack(total):
    rel = (2 * WIN - 1, HD)
    shapes = [(2 * QKV,), rel, rel] + [(D,)] * 3 + [(FF,)] + [(D,)] * 3
    return call(
        unpack_kernel, "unpack", [(total, None)], [(array(shape, F32), None) for shape in shapes]
    )


def per_device(
    n_dp,
    image_tokens,
    slot_window,
    first_gain,
    first_bias,
    qkv_weight,
    qkv_bias,
    rel_height,
    rel_width,
    proj_weight,
    proj_bias,
    second_gain,
    second_bias,
    hidden_weight,
    hidden_bias,
    output_weight,
    output_bias,
    cotangent,
):
    COUNT.clear()
    images = image_tokens.shape[0]
    count = 2 * images
    c = lax.axis_index("dp") % 2
    s = lax.axis_index("seq")
    z = lax.axis_index("fsdp")
    a = jnp.where(c == 0, s ^ 1, s ^ 2)
    b = jnp.where(c == 0, s ^ 2, s ^ 1)
    where = jnp.stack([z, s, a, b, s ^ 3, c]).astype(jnp.int32)

    def plane_perm(step):
        out = []
        for i in range(n_dp):
            hop = (1, 2)[(i + step) % 2]
            out += [(i * 4 + j, i * 4 + (j ^ hop)) for j in range(4)]
        return out

    plane_one, plane_two = plane_perm(0), plane_perm(1)

    def to_core(v):
        return lax.ppermute(v, "dp", [(i, i ^ 1) for i in range(n_dp)])

    def to_seq(v, k):
        return lax.ppermute(v, "seq", [(i, i ^ k) for i in range(4)])

    def to_z(v, k):
        return lax.ppermute(v, "fsdp", [(i, (i + k) % 4) for i in range(4)])

    def swap_z(v, hop):
        return lax.ppermute(v, "fsdp", [(i, i ^ hop) for i in range(4)])

    def to_plane(v, perm):
        return lax.ppermute(v, ("dp", "seq"), perm)

    def pick(v, index, axis=0):
        return lax.dynamic_index_in_dim(v, index, axis, keepdims=False)

    row = jnp.arange(ROWS)
    token = (s ^ (row // PAD)) * TOK + row % PAD
    real = row % PAD < TOK
    t_r, t_c = token // WIN, token % WIN
    slot = pick(slot_window, s)
    ok = (
        real
        & (slot >= 0)
        & (slot // NWS * WIN + t_r < GRID)
        & (slot % NWS * WIN + t_c < GRID)
    ).astype(F32)[:, None]
    ones = jnp.ones((ROWS, 1), F32)
    near_offset = jnp.arange(WIN)[:, None] - jnp.arange(WIN)[None, :] + WIN - 1
    height = rel_height[near_offset].reshape(WIN * WIN, HD).T
    width = rel_width[near_offset].reshape(WIN * WIN, HD).T
    gap = jnp.zeros((HD, TAB // 2 - WIN * WIN), BF)
    flat = jnp.concatenate([height, gap, width, gap], axis=1)
    blank = jnp.zeros_like(flat)
    table = jnp.stack([jnp.concatenate([flat, blank]), jnp.concatenate([blank, flat])])
    col = jnp.arange(TAB)
    in_half = col % (TAB // 2)
    col_from = jnp.where(in_half < WIN * WIN, in_half // WIN, -1)
    spot = (
        jnp.where(col[None, :] < TAB // 2, t_r[:, None], t_c[:, None]) == col_from[None, :]
    ).astype(F32)
    col_to = jnp.where(in_half < WIN * WIN, in_half % WIN + WIN * (col // (TAB // 2)), -1)
    fold = (col_to[:, None] == jnp.arange(LANES)[None, :]).astype(BF)
    lanes = jnp.arange(LANES)[None, :]
    keys = (
        real[:, None] & ((lanes == t_r[:, None]) | (lanes == WIN + t_c[:, None]))
    ).astype(BF)
    key_bias = jnp.where(real, 0.0, NEG).astype(F32)[None, :]
    tables = (table, spot, fold, keys, key_bias)
    gain_one, bias_one = first_gain[None], first_bias[None]
    gain_two, bias_two = second_gain[None], second_bias[None]

    def along_z(piece):
        return [to_z(piece, k) for k in (1, 2, 3)]

    def in_plane(first):
        second = to_plane(first, plane_one)
        third = to_plane(first, plane_two)
        fourth = to_plane(second, plane_two)
        return first, second, third, fourth

    def exchange(parts, after=()):
        near, both, far = parts
        one = to_plane(both, plane_one)
        send = pair_up(far, one, after)
        return near, one, to_plane(send, plane_two), send

    ho_piece, qp_piece = pieces(where, qkv_weight, proj_weight, hidden_weight, output_weight)
    z_qp = along_z(qp_piece)
    tokens_cut = cut(where, image_tokens, cotangent, after=[qp_piece])
    ho_one = swap_z(ho_piece, 1)
    first_qp = join(z_qp, after=[tokens_cut[0]])
    got_qp = in_plane(first_qp)
    ho_pair = both_of(ho_piece, ho_one, after=[first_qp])
    ho_two = swap_z(ho_pair, 2)
    near, one, two, mid = exchange(tokens_cut, after=[got_qp[1], ho_pair])
    first_ho = join_ho(ho_one, ho_two, after=[mid])
    own = weld(where, ok, near, one, two, after=got_qp[1:] + (first_ho,))
    other = to_core(own)
    got_ho = in_plane(first_ho)
    w_qp, proj_send = call(
        place_qp_kernel,
        "place_qp",
        [(where, SMEM), (qkv_weight, HBM), (proj_weight, HBM)] + [(v, ANY) for v in got_qp],
        [
            (array((4, 4, PIECE, WIDE)), None),
            (array((2, 4, PIECE, HALF)), None),
        ],
        scratch=[pltpu.SemaphoreType.DMA((28,))],
        after=[own],
    )
    w_qp = w_qp.reshape(D, WIDE)
    proj_other = to_core(proj_send.reshape(HALF, HALF))
    normed = norm_one(ok, own, other, gain_one, bias_one, after=[w_qp])
    packed, attended, probs, low, branch_other = attn_fwd(
        where, 1, normed, w_qp, proj_other, qkv_bias[None], tables
    )
    packed, attended, probs, low, branch = attn_fwd(
        where, 0, normed, w_qp, proj_other, qkv_bias[None], tables,
        before=(packed, attended, probs, low), after=[got_ho[1]],
    )
    there = to_core(low)
    w_ho = call(
        place_ho_kernel,
        "place_ho",
        [(where, SMEM), (hidden_weight, HBM), (output_weight, HBM)] + [(v, ANY) for v in got_ho],
        [(array((4, 4, 4 * PIECE, D)), None)],
        scratch=[pltpu.SemaphoreType.DMA((32,))],
        after=[packed],
    )[0].reshape(16, 4 * PIECE, D)
    middle, second = norm_two(
        own, other, branch, branch_other, there, proj_bias[None], gain_two, bias_two, after=[w_ho]
    )
    active, slope = hidden_layer(where, second, w_ho, hidden_bias[None])

    def natural(keep_two, send_two):
        out = jnp.zeros((2, 4, 96, WIDE), BF)
        for q, part in ((s, keep_two[0]), (b, keep_two[1]), (a, send_two[0]), (s ^ 3, send_two[1])):
            out = lax.dynamic_update_index_in_dim(out, part, q, 1)
        return out.astype(F32)

    def sum_rows(full):
        return lax.psum_scatter(full, ("dp", "seq", "fsdp"), scatter_dimension=0, tiled=True)

    def spread_cols(grad, parts):
        grad = grad.reshape(D, parts, HALF)
        zero = jnp.zeros_like(grad)
        return jnp.where(
            c == 0, jnp.stack([grad, zero], axis=2), jnp.stack([zero, grad], axis=2)
        ).reshape(D, 2 * parts * HALF)

    def larger_wide(keep_two, send_two):
        return sum_rows(spread_cols(natural(keep_two, send_two).reshape(D, WIDE), 4))

    def larger_qp(keep_two, send_two):
        grad = natural(keep_two, send_two)
        qkv = sum_rows(spread_cols(grad[..., :QKV].reshape(D, QKV), 3))
        proj = jnp.concatenate(list(grad[..., QKV:].reshape(2, HALF, HALF)), axis=1)
        zero = jnp.zeros_like(proj)
        proj = jnp.where(c == 0, jnp.concatenate([proj, zero]), jnp.concatenate([zero, proj]))
        return qkv, sum_rows(proj)

    def step_one(send):
        return to_plane(send, plane_one)

    def step_two(parts, after=()):
        stay, send = add_one(parts, after)
        return stay, to_plane(send, plane_two), send

    def step_three(stay, got, after=()):
        keep, send = add_two(where, stay, got, after)
        return keep, swap_z(send, 1), send

    def step_four(keep, got, after=()):
        stay, send = add_three(keep, got, after)
        return stay, swap_z(send, 2), send

    def step_five(stay, got, after=()):
        total, send = add_four(where, stay, got, after)
        return total, to_core(send), send

    pair = n_dp == 2

    o_keep, o_send = weight_grad(where, [own, other], active)
    o_got = step_one(o_send) if pair else o_send
    grad_pre, part, part_low, hidden_sums = grad_pre_of(own, other, slope, w_ho, after=[o_send])
    part_there = to_core(part_low)
    h_keep, h_send = weight_grad(where, [second], grad_pre)
    h_got = step_one(h_send) if pair else h_send
    grad_middle, grad_branch, sums_two = norm_two_back(
        part, part_there, middle, gain_two, own, other, after=[h_send]
    )
    grad_packed, tab_grad, qkv_sums = attn_bwd(
        where, 0, packed, grad_branch, probs, w_qp, proj_other, tables
    )
    held = [grad_packed]
    if pair:
        oh_stay, oh_got, mid = step_two([(o_keep, o_got), (h_keep, h_got)], after=held)
        held = [mid]
    grad_packed, tab_grad_b, qkv_sums_b = attn_bwd(
        where, 1, packed, grad_branch, probs, w_qp, proj_other, tables,
        before=(grad_packed,), after=held,
    )
    q_keep, q_send = weight_grad_qp(where, normed, grad_packed, attended, grad_branch)
    held = [q_send]
    if pair:
        q_got = step_one(q_send)
        oh_keep, oh_got, mid = step_three(oh_stay, oh_got, after=held)
        held = [mid]
    back, back_low = product(
        "back", grad_packed, w_qp, pl.BlockSpec((D, QKV), lambda w: (0, 0)),
        lambda left, right: mm(left, right[...], ((1,), (1,))), after=held,
    )
    back_there = to_core(back_low)
    feed, feed_low = product(
        "feed", active, w_ho, None, lambda left, right: mm(left, output_part(right)),
        after=[back_low],
    )
    feed_there = to_core(feed_low)
    held = [feed_low]
    if pair:
        q_stay, q_got, mid = step_two([(q_keep, q_got)], after=held)
        held = [mid]
    *parts, sums_one = last(
        where, ok, back, back_there, own, gain_one, grad_middle, middle, feed, feed_there,
        output_bias[None], after=held,
    )
    to_offset = jnp.pad(
        (near_offset.reshape(-1)[None, :] == jnp.arange(2 * WIN - 1)[:, None]).astype(F32),
        ((0, 32 - (2 * WIN - 1)), (0, TAB // 2 - WIN * WIN)),
    )
    ins = (sums_two, sums_one, hidden_sums, qkv_sums, qkv_sums_b, tab_grad, tab_grad_b, to_offset)
    small = call(
        small_kernel,
        "small",
        [(where, SMEM)] + [(v, None) for v in ins],
        [(array((32, D), F32), None)],
    )[0]
    small_got = to_core(small)
    held = [small]
    if pair:
        oh_stay, oh_got, mid = step_four(oh_keep, oh_got, after=held)
        q_keep, q_got, mid = step_three(q_stay, q_got, after=[mid])
        held = [mid]
    small = tally([small, small_got], after=held)
    small_got = to_seq(small, 1)
    *parts, mid = exchange(parts, after=[small])
    small = tally([small, small_got], after=[mid])
    small_got = to_seq(small, 2)
    held = [small]
    if pair:
        q_stay, q_got, mid = step_four(q_keep, q_got, after=held)
        oh_total, oh_there, mid = step_five(oh_stay, oh_got, after=[mid])
        held = [mid]
    small = tally([small, small_got], after=held)
    small_got = swap_z(small, 1)
    input_grad, block_out = home(where, *parts, after=[small])
    small = tally([small, small_got], after=[input_grad])
    small_got = swap_z(small, 2)
    held = [small]
    if pair:
        q_total, q_there, mid = step_five(q_stay, q_got, after=held)
        held = [mid]
    small = tally([small, small_got], after=held)
    if pair:
        g_output, g_hidden, g_qkv, g_proj = finish(
            where, oh_total, oh_there, q_total, q_there, after=[small]
        )
        g_output = g_output.T
    else:
        g_output = larger_wide(o_keep, o_send).T
        g_hidden = larger_wide(h_keep, h_send)
        g_qkv, g_proj = larger_qp(q_keep, q_send)
    if n_dp > 2:
        groups = [list(range(core, n_dp, 2)) for core in range(2)]
        small = lax.psum(small, "dp", axis_index_groups=groups)
    (
        d_qkv_bias, d_height, d_width, d_proj_bias, d_gain_two, d_bias_two, d_hidden_bias,
        d_output_bias, d_gain_one, d_bias_one,
    ) = unpack(small)
    return (
        block_out,
        input_grad,
        d_gain_one,
        d_bias_one,
        g_qkv,
        d_qkv_bias,
        d_height,
        d_width,
        g_proj,
        d_proj_bias,
        d_gain_two,
        d_bias_two,
        g_hidden,
        d_hidden_bias,
        g_output,
        d_output_bias,
    )


def solution(mesh):
    tokens = P("dp", "fsdp", "seq", None)
    rows = P("fsdp", None)
    every = P(("dp", "seq", "fsdp"), None)
    args = (tokens, P("fsdp"), P(), P(), rows, P(), P(), P(), rows)
    args += (P(), P(), P(), rows, P(), rows, P(), tokens)
    outs = (tokens, tokens, P(), P(), every, P(), P(), P(), every)
    outs += (P(), P(), P(), every, P(), P(None, ("dp", "seq", "fsdp")), P())
    return jax.shard_map(
        functools.partial(per_device, mesh.shape["dp"]),
        mesh=mesh,
        in_specs=args,
        out_specs=outs,
        check_vma=False,
    )
```
